32 devices in a mesh: dp: 16 (over z, x, core), seq: 2 (over y).
Axes of the slice: x: 2, y: 2, z: 4, core: 2. Of those that a mesh axis runs over, the one named last changes fastest.
Arguments:
- decoder_in: bfloat16 [16, 1024, 768], P('dp', 'seq'), may hold values from -6 to 6
- encoder_out: bfloat16 [16, 2048, 768], P('dp', 'seq'), may hold values from -6 to 6
- dec_lengths: int32 [16, 2], P('dp'), may hold values from 1 to 1022, as said below
- pair_flags: int32 [16, 2], P('dp'), may hold values from 0 to 1
- enc_segments: int32 [16, 2048], P('dp'), may hold values from 0 to 2, as said below
- self_proj: float32 [3, 768, 768], P(None, ('dp', 'seq')), may hold values from -0.21875 to 0.21875
- self_out: float32 [768, 768], P(('dp', 'seq')), may hold values from -0.875 to 0.875
- cross_proj: float32 [3, 768, 768], P(None, ('dp', 'seq')), may hold values from -0.21875 to 0.21875
- cross_out: float32 [768, 768], P(('dp', 'seq')), may hold values from -1.25 to 1.25
- ffn_in: float32 [768, 3072], P(('dp', 'seq')), may hold values from -0.21875 to 0.21875
- ffn_out: float32 [3072, 768], P(('dp', 'seq')), may hold values from -0.109375 to 0.109375
- norm_gains: float32 [3, 768], P(None, ('dp', 'seq')), may hold values from 0.25 to 1.75
- rel_table: float32 [768], P(('dp', 'seq')), may hold values from -4 to 4
- out_grad: bfloat16 [16, 1024, 768], P('dp', 'seq'), may hold values from -6 to 6
Outputs:
- layer_out: bfloat16 [16, 1024, 768], P('dp', 'seq')
- grad_input: float32 [16, 1024, 768], P('dp', 'seq')
- grad_encoder: float32 [16, 2048, 768], P('dp', 'seq')
- grad_self_proj: float32 [3, 768, 768], P(None, ('dp', 'seq'))
- grad_self_out: float32 [768, 768], P(('dp', 'seq'))
- grad_cross_proj: float32 [3, 768, 768], P(None, ('dp', 'seq'))
- grad_cross_out: float32 [768, 768], P(('dp', 'seq'))
- grad_ffn_in: float32 [768, 3072], P(('dp', 'seq'))
- grad_ffn_out: float32 [3072, 768], P(('dp', 'seq'))
- grad_gains: float32 [3, 768], P(None, ('dp', 'seq'))
- grad_table: float32 [768], P(('dp', 'seq'))
The draws below stay inside these ranges and needn't reach their ends.
Inputs may be any that keep to these rules, and one draw needn't show every extreme that they name: `dec_lengths`: each row holds the decoder lengths of the stream's two pairs; after them come 1 to 128 padding positions. Some stream has a pair of length 1 and one of length 1022. `enc_segments`: along a stream the pair numbers never fall: 0 for the first pair, 1 for the second, 2 for padding; each of the three appears, padding at most 1024 // 4 times.
All inputs are finite; a program needn't handle non-finite values.
Results may differ from the reference program's by a relative error of at most 0.03.
Values may be sent and summed in bfloat16 or wider, within the bound.
A program may use at most 1 GiB of HBM per device.

```python
import jax
import jax.numpy as jnp
from jax import lax

D = 768
HEADS = 12
HDIM = 64
FF = 3072
BUCKETS = 32
DEC_LEN = 1024
ENC_LEN = 2048
BATCH = 16
DEC_SHARD = 512
ENC_SHARD = 1024


def pair_lengths(key, shard_len, total_len):
    key_short, key_pad, key_order = jax.random.split(key, 3)
    stream_ids = jnp.arange(BATCH, dtype=jnp.int32)
    short_len = jax.random.randint(key_short, (BATCH,), 1, shard_len // 4 + 1)
    pad_len = jax.random.randint(key_pad, (BATCH,), 1, shard_len // 4 + 1)
    short_len = jnp.where(stream_ids == 0, 1, short_len)
    pad_len = jnp.where(stream_ids == 0, 1, pad_len)
    long_len = total_len - short_len - pad_len
    order_bit = jax.random.randint(key_order, (BATCH,), 0, 2)
    first_len = jnp.where(order_bit == 1, long_len, short_len)
    second_len = jnp.where(order_bit == 1, short_len, long_len)
    return (first_len, second_len)


def draw_dec_lengths(key, part):
    key = jax.random.fold_in(key, 3)
    first_len, second_len = pair_lengths(key, DEC_SHARD, DEC_LEN)
    return jnp.stack((first_len, second_len), axis=1).astype(jnp.int32)


def draw_enc_segments(key, part):
    key = jax.random.fold_in(key, 7)
    first_len, second_len = pair_lengths(key, ENC_SHARD, ENC_LEN)
    positions = jnp.arange(ENC_LEN, dtype=jnp.int32)
    first_part = (positions[None, :] >= first_len[:, None]).astype(jnp.int32)
    second_part = (positions[None, :] >= (first_len + second_len)[:, None]).astype(jnp.int32)
    return (first_part + second_part).astype(jnp.int32)


def touch_ends(result, own_key, smallest, high):
    longest = result.shape.index(max(result.shape))
    spots = []
    for shift in (0, 1):
        where = [jax.random.randint(jax.random.fold_in(own_key, axis), (), 0, length) for axis, length in enumerate(result.shape)]
        where[longest] = (where[longest] + shift) % result.shape[longest]
        spots.append(tuple(where))
    return result.at[spots[0]].set(smallest).at[spots[1]].set(high)


def steps_of(rng, dims, cuts, least, top_value):
    loudness, own = 1.0, jax.random.fold_in(rng, 6)
    for position, blocks in cuts:
        steps = jnp.exp(jax.random.uniform(jax.random.fold_in(own, position), (blocks,), jnp.float32, least / len(cuts), top_value / len(cuts)))
        loudness = loudness * jnp.repeat(steps, dims[position] // blocks).reshape([-1 if axis == position else 1 for axis in range(len(dims))])
    return loudness


def bell_draw(stream_key, extent, deviation, bound, cuts=(), kind=jnp.bfloat16):
    loudness = steps_of(stream_key, extent, cuts, -0.22, 0.18) if cuts else 1.0
    array = jax.random.normal(stream_key, extent, jnp.float32) * deviation * loudness
    return jnp.minimum(jnp.maximum(array, -bound), bound).astype(kind)


def setup_inputs(seed: int = 0) -> dict:
    keys = jax.random.split(jax.random.key(seed), 15)
    return {
        "decoder_in": bell_draw(keys[0], (BATCH, DEC_LEN, D), 1.0, 6.0, ((0, 16), (1, 2))),
        "encoder_out": bell_draw(keys[1], (BATCH, ENC_LEN, D), 1.0, 6.0, ((0, 16), (1, 2))),
        "dec_lengths": draw_dec_lengths(jax.random.fold_in(keys[14], 71), 0),
        "pair_flags": touch_ends(jax.random.randint(keys[3], (BATCH, 2), 0, 2), jax.random.fold_in(keys[3], 1), 0, 1).astype(jnp.int32),
        "enc_segments": draw_enc_segments(jax.random.fold_in(keys[14], 71), 0),
        "self_proj": bell_draw(keys[5], (3, D, D), D ** -0.5, 0.21875, ((1, 32),), jnp.float32),
        "self_out": bell_draw(keys[6], (D, D), (D // 16) ** -0.5, 0.875, ((0, 32),), jnp.float32),
        "cross_proj": bell_draw(keys[7], (3, D, D), D ** -0.5, 0.21875, ((1, 32),), jnp.float32),
        "cross_out": bell_draw(keys[8], (D, D), (D // 32) ** -0.5, 1.25, ((0, 32),), jnp.float32),
        "ffn_in": bell_draw(keys[9], (D, FF), D ** -0.5, 0.21875, ((0, 32),), jnp.float32),
        "ffn_out": bell_draw(keys[10], (FF, D), FF ** -0.5, 0.109375, ((0, 32),), jnp.float32),
        "norm_gains": jnp.clip(1.0 + 0.15 * jax.random.normal(keys[11], (3, D), jnp.float32), 0.25, 1.75),
        "rel_table": bell_draw(keys[12], (2 * BUCKETS * HEADS,), 1.0, 4.0, ((0, 32),), jnp.float32),
        "out_grad": bell_draw(keys[13], (BATCH, DEC_LEN, D), 1.0, 6.0, ((0, 16), (1, 2))),
    }


@jax.custom_vjp
def low(v):
    return lax.optimization_barrier(v.astype(jnp.bfloat16)).astype(jnp.float32)

@jax.custom_vjp
def low_back(v):
    return v

def low_keep(v):
    return (low(v), None)

def low_pass(kept, grad):
    return (grad,)

def back_keep(v):
    return (v, None)

def back_low(kept, grad):
    return (low(grad),)
low.defvjp(low_keep, low_pass)
low_back.defvjp(back_keep, back_low)
epsilon = 1e-06
neg_large = -1e+30
highest = lax.Precision.HIGHEST
bucket_edges = (19, 21, 24, 27, 31, 35, 40, 46, 52, 59, 67, 77, 87, 99, 113)

def round_both(values):
    return low(low_back(values))

def bucket_of(distance):
    above_count = sum(((distance >= border).astype(jnp.int32) for border in bucket_edges))
    return jnp.where(distance < 16, distance, 16 + above_count)

def rms_norm(values, gain_vec):
    return values * lax.rsqrt(lax.optimization_barrier(jnp.mean(values * values, axis=-1, keepdims=True)) + epsilon) * gain_vec

def attend(queries, key_rows, value_rows, allowed, bias_term):
    row_count = queries.shape[0]
    query_heads = queries.reshape(row_count, HEADS, HDIM)
    key_heads = key_rows.reshape(key_rows.shape[0], HEADS, HDIM)
    value_heads = value_rows.reshape(value_rows.shape[0], HEADS, HDIM)
    scores = jnp.einsum('qhe,khe->hqk', query_heads, key_heads, precision=highest) * 0.125 + bias_term
    scores = low_back(scores)
    scores = jnp.where(allowed[None], scores, neg_large)
    row_peak = lax.optimization_barrier(jnp.max(scores, axis=-1, keepdims=True))
    weighted = jnp.exp(scores - row_peak)
    soft_probs = weighted / lax.optimization_barrier(jnp.sum(weighted, axis=-1, keepdims=True))
    mixed_out = jnp.einsum('hqk,khe->qhe', low(soft_probs), value_heads, precision=highest)
    return round_both(mixed_out.reshape(row_count, HEADS * HDIM))

def one_stream(rounded, stream):
    proj_self, out_self, proj_cross, out_cross, mat_in, mat_out, gain_vals, table_vals = rounded
    decoder_rows, encoder_rows, lengths, flags_row, enc_pairs = stream
    dec_len = decoder_rows.shape[0]
    positions = jnp.arange(dec_len, dtype=jnp.int32)
    pair_ids = (positions >= lengths[0]).astype(jnp.int32) + (positions >= lengths[0] + lengths[1]).astype(jnp.int32)
    flag_ids = jnp.where(pair_ids == 0, flags_row[0], jnp.where(pair_ids == 1, flags_row[1], 0))
    distance = jnp.maximum(positions[:, None] - positions[None, :], 0)
    self_allowed = (pair_ids[:, None] == pair_ids[None, :]) & (positions[None, :] <= positions[:, None])
    code_ids = (flag_ids[:, None] * BUCKETS + bucket_of(distance)).astype(jnp.int32)
    bias_self = jnp.transpose(table_vals.reshape(2 * BUCKETS, HEADS)[code_ids], (2, 0, 1))
    normed_one = low(rms_norm(decoder_rows, gain_vals[0]))
    qkv_rows = round_both(jnp.einsum('td,cde->tce', normed_one, proj_self, precision=highest))
    attn_one = attend(qkv_rows[:, 0], qkv_rows[:, 1], qkv_rows[:, 2], self_allowed, bias_self)
    resid_one = decoder_rows + low_back(jnp.dot(attn_one, out_self, precision=highest))
    normed_two = low(rms_norm(resid_one, gain_vals[1]))
    query_two = round_both(jnp.dot(normed_two, proj_cross[0], precision=highest))
    kv_two = round_both(jnp.einsum('td,cde->tce', encoder_rows, proj_cross[1:], precision=highest))
    cross_allowed = pair_ids[:, None] == enc_pairs[None, :]
    attn_two = attend(query_two, kv_two[:, 0], kv_two[:, 1], cross_allowed, 0.0)
    resid_two = resid_one + low_back(jnp.dot(attn_two, out_cross, precision=highest))
    normed_three = low(rms_norm(resid_two, gain_vals[2]))
    hidden_pre = low_back(jnp.dot(normed_three, mat_in, precision=highest))
    hidden_act = low(jax.nn.gelu(hidden_pre, approximate=False))
    return resid_two + low_back(jnp.dot(hidden_act, mat_out, precision=highest))

def reference(decoder_in, encoder_out, dec_lengths, pair_flags, enc_segments, self_proj, self_out, cross_proj, cross_out, ffn_in, ffn_out, norm_gains, rel_table, out_grad):
    masters = (self_proj, self_out, cross_proj, cross_out, ffn_in, ffn_out, norm_gains, rel_table)
    stream_step = jax.checkpoint(one_stream)

    def forward(decoder_rows, encoder_rows, weights):
        rounded = tuple((low(weight) for weight in weights))

        def per_stream(stream):
            return stream_step(rounded, stream)
        return lax.map(per_stream, (decoder_rows, encoder_rows, dec_lengths, pair_flags, enc_segments))
    layer_f32, pull_back = jax.vjp(forward, decoder_in.astype(jnp.float32), encoder_out.astype(jnp.float32), masters)
    grad_input, grad_encoder, grad_weights = pull_back(out_grad.astype(jnp.float32))
    return (layer_f32.astype(jnp.bfloat16), grad_input, grad_encoder, grad_weights[0], grad_weights[1], grad_weights[2], grad_weights[3], grad_weights[4], grad_weights[5], grad_weights[6], grad_weights[7])
```

```python
import functools
import math

import jax
import jax.numpy as jnp
from jax import lax
from jax.experimental import pallas as pl
from jax.experimental.pallas import tpu as pltpu
from jax.sharding import PartitionSpec as P

D = 768
HEADS = 12
HDIM = 64
FF = 3072
BUCKETS = 32
PAIRS = HEADS // 2
LOG2E = math.log2(math.e)
LN2 = math.log(2.0)
epsilon = 1e-06
neg_large = -1e30
bucket_edges = (19, 21, 24, 27, 31, 35, 40, 46, 52, 59, 67, 77, 87, 99, 113)
f32 = jnp.float32
bf16 = jnp.bfloat16
NT = (((1,), (1,)), ((), ()))
NN = (((1,), (0,)), ((), ()))
TN = (((0,), (0,)), ((), ()))
BOTH = ("dp", "seq")


def bucket_of(distance):
    above_count = sum(((distance >= border).astype(jnp.int32) for border in bucket_edges))
    return jnp.where(distance < 16, distance, 16 + above_count)


def mm(a, b, dims=NN):
    return lax.dot_general(a, b, dims, preferred_element_type=f32)


def head_lanes(which):
    low = lax.broadcasted_iota(jnp.int32, (1, 128), 1) < HDIM
    return low if which == 0 else jnp.logical_not(low)


def row_chunks(rows, keys, causal, step):
    return [
        (slice(i, i + step), (keys - rows + i + step) if causal else keys)
        for i in range(0, rows, step)
    ]


def near_bias(near_ref, which):
    row = lax.broadcasted_iota(jnp.int32, (128, 256), 0)
    column = lax.broadcasted_iota(jnp.int32, (128, 256), 1)
    tiles = []
    for flag in (0, 1):
        line = near_ref[0, 2 * which + flag : 2 * which + flag + 1, :]
        tile = pltpu.roll(jnp.broadcast_to(line, (128, 256)), 0, 1, stride=1, stride_axis=0)
        tiles.append(jnp.where(column - row > 128, neg_large, tile))
    return tiles


def diagonal_sums(tile):
    for step in (64, 32, 16, 8):
        tile = tile[:step] + pltpu.roll(tile[step:], 256 - step, 1)
    row = lax.broadcasted_iota(jnp.int32, (8, 256), 0)
    for step in (4, 2, 1):
        tile = jnp.where((row & step) != 0, pltpu.roll(tile, 256 - step, 1), tile)
    return jnp.sum(tile, axis=0, keepdims=True)


def attend_body(rows, keys, causal, step, *refs):
    if causal:
        q_ref, k_ref, v_ref, qx_ref, kx_ref, far_ref, near_ref, flag_ref = refs[:8]
    else:
        q_ref, k_ref, v_ref, qx_ref, kx_ref = refs[:5]
    o_ref, e_ref, inv_ref = refs[-3:]
    extra = kx_ref[...]
    if causal:
        extra = extra + far_ref[0]
    key_pair = k_ref[...]
    value_pair = v_ref[...]
    chunks = row_chunks(rows, keys, causal, step)
    found = []
    for which in (0, 1):
        mine = head_lanes(which)
        key_head = jnp.where(mine, key_pair, extra)
        value_head = jnp.where(mine, value_pair, jnp.ones_like(value_pair))
        if causal:
            tile_zero, tile_one = near_bias(near_ref, which)
        parts = []
        for here, width in chunks:
            query = jnp.where(mine, q_ref[here], qx_ref[here])
            scores = mm(query, key_head[:width], NT)
            if causal:
                cut = width - 256
                near = scores[:, cut:] + jnp.where(flag_ref[here, :1] > 0, tile_one, tile_zero)
                far = scores[:, :cut]
                peak = jnp.maximum(
                    jnp.max(far, axis=1, keepdims=True), jnp.max(near, axis=1, keepdims=True)
                )
                near = jnp.exp2(near - peak).astype(bf16)
                far = jnp.exp2(far - peak).astype(bf16)
                e_ref[which, here, :cut] = far
                e_ref[which, here, cut:width] = near
                mixed = mm(far, value_head[:cut]) + mm(near, value_head[cut:width])
            else:
                peak = jnp.max(scores, axis=1, keepdims=True)
                weights = jnp.exp2(scores - peak).astype(bf16)
                e_ref[which, here, :] = weights
                mixed = mm(weights, value_head)
            total = mixed[:, HDIM : HDIM + 1] if which == 0 else mixed[:, 0:1]
            inverse = 1.0 / total
            parts.append((mixed * inverse, jnp.broadcast_to(inverse, mixed.shape)))
        found.append(parts)
    low = head_lanes(0)
    for index, (here, _) in enumerate(chunks):
        o_ref[here] = jnp.where(low, found[0][index][0], found[1][index][0]).astype(bf16)
        inv_ref[here] = jnp.where(low, found[0][index][1], found[1][index][1])


def pair_columns(rows):
    return pl.BlockSpec((rows, 128), lambda p: (0, p))


def same_block(rows):
    return pl.BlockSpec((rows, 128), lambda p: (0, 0))


def per_pair(height, width):
    return pl.BlockSpec((1, height, width), lambda p: (p, 0, 0))


def attend(query, key, value, query_extra, key_extra, far=None, near=None, flags=None):
    rows, keys = query.shape[0], key.shape[0]
    causal = far is not None
    step = 128 if causal else min(256, rows)
    operands = [query, key, value, query_extra, key_extra]
    specs = [
        pair_columns(rows),
        pair_columns(keys),
        pair_columns(keys),
        same_block(rows),
        same_block(keys),
    ]
    if causal:
        operands += [far, near, flags]
        specs += [per_pair(1, 128), per_pair(4, 256), same_block(rows)]
    work = HEADS * rows * keys
    return pl.pallas_call(
        functools.partial(attend_body, rows, keys, causal, step),
        grid=(PAIRS,),
        in_specs=specs,
        out_specs=(
            pair_columns(rows),
            pl.BlockSpec((2, rows, keys), lambda p: (p, 0, 0)),
            pair_columns(rows),
        ),
        out_shape=(
            jax.ShapeDtypeStruct((rows, D), bf16),
            jax.ShapeDtypeStruct((HEADS, rows, keys), bf16),
            jax.ShapeDtypeStruct((rows, D), f32),
        ),
        compiler_params=pltpu.CompilerParams(vmem_limit_bytes=56 << 20),
        cost_estimate=pl.CostEstimate(
            flops=4 * work * 256, bytes_accessed=2 * work, transcendentals=work
        ),
        name="attend_causal" if causal else "attend_cross",
    )(*operands)


def attend_back_body(rows, keys, causal, step, *refs):
    q_ref, k_ref, v_ref, e_ref, o_ref, inv_ref, d_ref = refs[:7]
    if causal:
        flag_ref, dq_ref, dk_ref, dv_ref, near_ref, sum_ref, ds_ref = refs[7:]
    else:
        dq_ref, dk_ref, dv_ref, ds_ref = refs[7:]
    lane = lax.broadcasted_iota(jnp.int32, (1, 128), 1)
    key_pair = k_ref[...]
    value_pair = v_ref[...]
    scaled = (d_ref[...].astype(f32) * inv_ref[...]).astype(bf16)
    product = scaled.astype(f32) * o_ref[...].astype(f32)
    scaled_t = scaled.T
    query_t = q_ref[...].T
    chunks = row_chunks(rows, keys, causal, step)
    query_parts = []
    for which in (0, 1):
        mine = head_lanes(which)
        base = HDIM if which == 0 else 0
        value_head = jnp.where(mine, value_pair, jnp.ones_like(value_pair))
        key_head = jnp.where(mine, key_pair, jnp.ones_like(key_pair))
        delta = jnp.sum(jnp.where(mine, product, 0.0), axis=1, keepdims=True)
        high = delta.astype(bf16)
        rest = (delta - high.astype(f32)).astype(bf16)
        extra = jnp.where(
            lane == base, -high, jnp.where(lane == base + 1, -rest, jnp.zeros_like(rest))
        )
        grad_head = jnp.where(mine, scaled, extra)
        parts = []
        if causal:
            near_all = jnp.zeros((128, 256), f32)
            near_one = jnp.zeros((128, 256), f32)
        for here, width in chunks:
            centred = mm(grad_head[here], value_head[:width], NT)
            grad_scores = e_ref[which, here, :width].astype(f32) * centred
            if causal:
                near = grad_scores[:, width - 256 :]
                near_all = near_all + near
                near_one = near_one + jnp.where(flag_ref[here, :1] > 0, near, 0.0)
            grad_scores = grad_scores.astype(bf16)
            ds_ref[here, :width] = grad_scores
            parts.append(mm(grad_scores, key_head[:width]))
        query_parts.append(parts)
        half = slice(HDIM * which, HDIM * which + HDIM)
        if causal:
            spans = [(slice(0, keys - rows), 0)] if keys > rows else []
            spans += [
                (slice(keys - rows + i, keys - rows + i + step), i) for i in range(0, rows, step)
            ]
        else:
            spans = [(slice(0, keys), 0)]
        for span, first in spans:
            grad_key = mm(query_t[half, first:], ds_ref[first:, span])
            dk_ref[half, span] = (grad_key * LN2).astype(dk_ref.dtype)
            grad_value = mm(scaled_t[half, first:], e_ref[which, first:, span])
            dv_ref[half, span] = grad_value.astype(dv_ref.dtype)
        if causal:
            for flag, tile in ((0, near_all - near_one), (1, near_one)):
                near_ref[0, 2 * which + flag : 2 * which + flag + 1, :] = diagonal_sums(tile)
    low = head_lanes(0)
    for index, (here, _) in enumerate(chunks):
        both = jnp.where(low, query_parts[0][index], query_parts[1][index])
        dq_ref[here] = (both * 0.125).astype(dq_ref.dtype)
    if causal:
        flagged = flag_ref[:, :1] > 0
        for which in (0, 1):
            whole = jnp.concatenate(query_parts[which], axis=0)
            one = jnp.sum(jnp.where(flagged, whole, 0.0), axis=0, keepdims=True)
            every = jnp.sum(whole, axis=0, keepdims=True)
            sum_ref[0, 2 * which : 2 * which + 1, :] = every - one
            sum_ref[0, 2 * which + 1 : 2 * which + 2, :] = one


def attend_back(query, key, value, weights, mixed, inverse, grad_mixed, flags=None):
    rows, keys = query.shape[0], key.shape[0]
    causal = flags is not None
    step = 128 if causal else min(256, rows)
    operands = [query, key, value, weights, mixed, inverse, grad_mixed]
    specs = [
        pair_columns(rows),
        pair_columns(keys),
        pair_columns(keys),
        pl.BlockSpec((2, rows, keys), lambda p: (p, 0, 0)),
        pair_columns(rows),
        pair_columns(rows),
        pair_columns(rows),
    ]
    turned = jax.ShapeDtypeStruct((D, keys), bf16)
    turned_spec = pl.BlockSpec((128, keys), lambda p: (p, 0))
    shapes = [jax.ShapeDtypeStruct((rows, D), bf16), turned, turned]
    out_specs = [pair_columns(rows), turned_spec, turned_spec]
    if causal:
        operands.append(flags)
        specs.append(same_block(rows))
        shapes += [
            jax.ShapeDtypeStruct((PAIRS, 4, 256), f32),
            jax.ShapeDtypeStruct((PAIRS, 4, 128), f32),
        ]
        out_specs += [per_pair(4, 256), per_pair(4, 128)]
    work = HEADS * rows * keys
    return pl.pallas_call(
        functools.partial(attend_back_body, rows, keys, causal, step),
        grid=(PAIRS,),
        in_specs=specs,
        out_specs=tuple(out_specs),
        out_shape=tuple(shapes),
        scratch_shapes=[pltpu.VMEM((rows, keys), bf16)],
        compiler_params=pltpu.CompilerParams(vmem_limit_bytes=56 << 20),
        cost_estimate=pl.CostEstimate(
            flops=6 * work * 256, bytes_accessed=2 * work, transcendentals=0
        ),
        name="attend_causal_back" if causal else "attend_cross_back",
    )(*operands)


def pair_of(positions, lengths):
    return (positions >= lengths[0]).astype(jnp.int32) + (
        positions >= lengths[0] + lengths[1]
    ).astype(jnp.int32)


def on_both_halves(columns):
    half = jnp.pad(columns, ((0, 0), (0, HDIM - columns.shape[1])))
    return jnp.concatenate((half, half), axis=1).astype(bf16)


def pair_mask(key_pairs):
    wrong = key_pairs[:, None] != jnp.arange(3, dtype=jnp.int32)[None, :]
    return on_both_halves(jnp.where(wrong, neg_large, 0.0))


def bias_parts(table):
    scaled = table.astype(f32) * LOG2E
    far = jnp.stack((scaled[BUCKETS - 1], scaled[2 * BUCKETS - 1]), axis=0)
    high = far.astype(bf16)
    rest = (far - high.astype(f32)).astype(bf16)
    columns = jnp.stack((high[0], rest[0], high[1], rest[1]), axis=1)
    columns = jnp.pad(columns, ((0, 0), (3, HDIM - 7))).reshape(PAIRS, 2, HDIM)
    far_lanes = jnp.concatenate((columns[:, 1], columns[:, 0]), axis=1).reshape(PAIRS, 1, 128)
    place = jnp.arange(256, dtype=jnp.int32)
    buckets = bucket_of(jnp.where(place <= 128, 128 - place, 384 - place))
    chosen = (buckets[:, None] == jnp.arange(BUCKETS, dtype=jnp.int32)[None, :]).astype(f32)
    steps = scaled.reshape(2, BUCKETS, HEADS) - far[:, None, :]
    lines = jnp.einsum("jb,fbh->hfj", chosen, steps, precision=lax.Precision.HIGHEST)
    return far_lanes, lines.reshape(PAIRS, 4, 256), chosen


def table_gradient(near_lines, row_sums, chosen):
    lines = near_lines.reshape(HEADS, 2, 256)
    near = jnp.einsum("hfj,jb->fbh", lines, chosen, precision=lax.Precision.HIGHEST)
    sums = row_sums.reshape(PAIRS, 2, 2, 128)
    every = jnp.stack((sums[:, 0, :, HDIM], sums[:, 1, :, 0]), axis=1).reshape(HEADS, 2).T
    rest = every - jnp.sum(near[:, : BUCKETS - 1], axis=1)
    return jnp.concatenate((near[:, : BUCKETS - 1], rest[:, None]), axis=1).reshape(-1)


def inverse_rms(values):
    return lax.rsqrt(jnp.mean(values * values, axis=-1, keepdims=True) + epsilon)


def norm_back(values, inverse, gain, grad):
    unit = values * inverse
    grad_gain = jnp.sum(grad * unit, axis=0)
    grad = grad * gain
    return inverse * (grad - unit * jnp.mean(grad * unit, axis=-1, keepdims=True)), grad_gain


def gelu_and_slope(value):
    upper = 0.5 * (1.0 + lax.erf(value * math.sqrt(0.5)))
    density = jnp.exp(-0.5 * value * value) * (1.0 / math.sqrt(2.0 * math.pi))
    return value * upper, upper + value * density


def seq_shift(array, count):
    length = array.shape[0]
    return lax.dynamic_slice_in_dim(jnp.concatenate((array, array), axis=0), count, length, axis=0)


def others_rows(rows, own_last):
    parts = lax.axis_size("seq")
    if parts == 2:
        return lax.ppermute(rows, "seq", [(0, 1)] if own_last else [(0, 1), (1, 0)])
    whole = lax.all_gather(rows, "seq", axis=0, tiled=True)
    step = rows.shape[0]
    start = lax.rem(lax.axis_index("seq") + 1, parts) * step
    return seq_shift(whole, start)[: (parts - 1) * step]


def to_owners(grads, own_last):
    parts = lax.axis_size("seq")
    if parts == 2:
        return lax.ppermute(grads, "seq", [(1, 0)] if own_last else [(0, 1), (1, 0)])
    step = grads.shape[0] // (parts - 1)
    whole = jnp.concatenate((grads, jnp.zeros((step, grads.shape[1]), grads.dtype)), axis=0)
    start = lax.rem(parts - 1 - lax.axis_index("seq"), parts) * step
    return lax.psum_scatter(seq_shift(whole, start), "seq", scatter_dimension=0, tiled=True)


def on_device(
    decoder_in,
    encoder_out,
    dec_lengths,
    pair_flags,
    enc_segments,
    self_proj,
    self_out,
    cross_proj,
    cross_out,
    ffn_in,
    ffn_out,
    norm_gains,
    rel_table,
    out_grad,
):
    shard = self_out.shape[0]
    small = jnp.concatenate((norm_gains, rel_table[None]), axis=0).T
    block_self = jnp.concatenate(
        (self_proj[0], self_proj[1], self_proj[2], self_out, jnp.pad(small, ((0, 0), (0, 124)))),
        axis=1,
    ).astype(bf16)
    block_cross = jnp.concatenate(
        (cross_proj[0], cross_proj[1], cross_proj[2], cross_out), axis=1
    ).astype(bf16)
    all_self = lax.all_gather(block_self, BOTH, axis=0, tiled=True)
    all_cross = lax.all_gather(block_cross, BOTH, axis=0, tiled=True)
    mat_in = lax.all_gather(ffn_in.astype(bf16), BOTH, axis=0, tiled=True)
    mat_out = lax.all_gather(ffn_out.astype(bf16), BOTH, axis=0, tiled=True)
    self_q, self_k, self_v, out_self = (all_self[:, i * D : (i + 1) * D] for i in range(4))
    cross_q, cross_k, cross_v, out_cross = (all_cross[:, i * D : (i + 1) * D] for i in range(4))
    small_all = all_self[:, 4 * D : 4 * D + 4].T
    gains = small_all[:3].astype(f32)
    table = small_all[3].reshape(2 * BUCKETS, HEADS)

    tokens = decoder_in[0]
    memory = encoder_out[0]
    grad_out = out_grad[0]
    rows, enc_rows = tokens.shape[0], memory.shape[0]
    seq_count = lax.axis_size("seq")
    seq_index = lax.axis_index("seq")
    keys, enc_keys = rows * seq_count, enc_rows * seq_count

    lengths = dec_lengths[0]
    place_here = seq_index * rows + jnp.arange(rows, dtype=jnp.int32)
    place_keys = (seq_index + 1) * rows - keys + jnp.arange(keys, dtype=jnp.int32)
    pair_here = pair_of(place_here, lengths)
    pair_keys = jnp.where(place_keys < 0, 3, pair_of(place_keys, lengths))
    segments = seq_shift(enc_segments[0], seq_index * enc_rows)
    flag_here = jnp.where(
        pair_here == 0, pair_flags[0, 0], jnp.where(pair_here == 1, pair_flags[0, 1], 0)
    )
    one_pair = (pair_here[:, None] == jnp.arange(3, dtype=jnp.int32)[None, :]).astype(f32)
    one_flag = (flag_here[:, None] == jnp.array((0, 0, 1, 1), jnp.int32)[None, :]).astype(f32)
    query_extra = on_both_halves(jnp.concatenate((one_pair, one_flag), axis=1))
    key_extra = pair_mask(pair_keys)
    memory_extra = pair_mask(segments)
    flag_rows = jnp.broadcast_to(flag_here.astype(f32)[:, None], (rows, 128))
    far_lanes, near_lines, chosen = bias_parts(table)

    before = others_rows(tokens, True)
    others = others_rows(memory, False)
    memory_all = jnp.concatenate((memory, others), axis=0)

    tokens = tokens.astype(f32)
    inverse_one = inverse_rms(tokens)
    normed_one = (tokens * inverse_one * gains[0]).astype(bf16)
    before = before.astype(f32)
    normed_before = (before * inverse_rms(before) * gains[0]).astype(bf16)
    normed_all = jnp.concatenate((normed_before, normed_one), axis=0)
    scale = 0.125 * LOG2E
    query_one = (mm(normed_one, self_q) * scale).astype(bf16)
    key_one = mm(normed_all, self_k).astype(bf16)
    value_one = mm(normed_all, self_v).astype(bf16)
    mixed_one, weights_one, total_one = attend(
        query_one, key_one, value_one, query_extra, key_extra, far_lanes, near_lines, flag_rows
    )
    resid_one = tokens + mm(mixed_one, out_self)
    inverse_two = inverse_rms(resid_one)
    normed_two = (resid_one * inverse_two * gains[1]).astype(bf16)
    query_two = (mm(normed_two, cross_q) * scale).astype(bf16)
    key_two = mm(memory_all, cross_k).astype(bf16)
    value_two = mm(memory_all, cross_v).astype(bf16)
    mixed_two, weights_two, total_two = attend(
        query_two, key_two, value_two, query_extra, memory_extra
    )
    resid_two = resid_one + mm(mixed_two, out_cross)
    inverse_three = inverse_rms(resid_two)
    normed_three = (resid_two * inverse_three * gains[2]).astype(bf16)
    hidden_act, hidden_slope = gelu_and_slope(mm(normed_three, mat_in))
    hidden_act = hidden_act.astype(bf16)
    layer_out = (resid_two + mm(hidden_act, mat_out)).astype(bf16)

    grad_pre = (hidden_slope * mm(grad_out, mat_out, NT)).astype(bf16)
    grad_ffn_out = mm(hidden_act, grad_out, TN).astype(bf16)
    grad_ffn_in = mm(normed_three, grad_pre, TN).astype(bf16)
    part, gain_three = norm_back(resid_two, inverse_three, gains[2], mm(grad_pre, mat_in, NT))
    grad_resid = grad_out.astype(f32) + part
    grad_low = grad_resid.astype(bf16)
    grad_cross_out = mm(mixed_two, grad_low, TN)
    grad_mixed = mm(grad_low, out_cross, NT).astype(bf16)
    grad_query, grad_key, grad_value = attend_back(
        query_two, key_two, value_two, weights_two, mixed_two, total_two, grad_mixed
    )
    turned = (((0,), (1,)), ((), ()))
    grad_memory = mm(grad_key, cross_k, turned) + mm(grad_value, cross_v, turned)
    grad_others = to_owners(grad_memory[enc_rows:].astype(bf16), False)
    grad_encoder = grad_memory[:enc_rows] + grad_others.astype(f32)
    grad_cross = jnp.concatenate(
        (
            mm(normed_two, grad_query, TN),
            mm(memory_all, grad_key, turned),
            mm(memory_all, grad_value, turned),
            grad_cross_out,
        ),
        axis=1,
    ).astype(bf16)
    part, gain_two = norm_back(resid_one, inverse_two, gains[1], mm(grad_query, cross_q, NT))
    grad_resid = grad_resid + part
    grad_low = grad_resid.astype(bf16)
    grad_self_out = mm(mixed_one, grad_low, TN)
    grad_mixed = mm(grad_low, out_self, NT).astype(bf16)
    grad_query, grad_key, grad_value, near_sums, row_sums = attend_back(
        query_one, key_one, value_one, weights_one, mixed_one, total_one, grad_mixed, flag_rows
    )
    grad_normed = mm(grad_key, self_k, turned) + mm(grad_value, self_v, turned)
    grad_before = to_owners(grad_normed[: keys - rows].astype(bf16), True)
    grad_normed = grad_normed[keys - rows :] + mm(grad_query, self_q, NT)
    grad_normed = grad_normed + grad_before.astype(f32)
    part, gain_one = norm_back(tokens, inverse_one, gains[0], grad_normed)
    grad_input = grad_resid + part
    table_grad = table_gradient(near_sums, row_sums, chosen)
    small = jnp.stack((gain_one, gain_two, gain_three, table_grad), axis=1)
    grad_self = jnp.concatenate(
        (
            mm(normed_one, grad_query, TN),
            mm(normed_all, grad_key, turned),
            mm(normed_all, grad_value, turned),
            grad_self_out,
            jnp.pad(small, ((0, 0), (0, 124))),
        ),
        axis=1,
    ).astype(bf16)

    def owned(array):
        return lax.psum_scatter(array, BOTH, scatter_dimension=0, tiled=True).astype(f32)

    own_ffn_out = owned(grad_ffn_out)
    own_ffn_in = owned(grad_ffn_in)
    own_cross = owned(grad_cross)
    own_self = owned(grad_self)
    own_small = own_self[:, 4 * D : 4 * D + 4].T

    def projections(block):
        return jnp.stack([block[:, i * D : (i + 1) * D] for i in range(3)], axis=0)

    return (
        layer_out[None],
        grad_input[None],
        grad_encoder[None],
        projections(own_self),
        own_self[:, 3 * D : 4 * D],
        projections(own_cross),
        own_cross[:, 3 * D : 4 * D],
        own_ffn_in,
        own_ffn_out,
        own_small[:3],
        own_small[3],
    )


def solution(mesh):
    hidden = P("dp", "seq", None)
    rows_split = P(BOTH, None)
    stacked = P(None, BOTH, None)
    stream = P("dp", None)
    return jax.shard_map(
        on_device,
        mesh=mesh,
        in_specs=(
            hidden,
            hidden,
            stream,
            stream,
            stream,
            stacked,
            rows_split,
            stacked,
            rows_split,
            rows_split,
            rows_split,
            P(None, BOTH),
            P(BOTH),
            hidden,
        ),
        out_specs=(
            hidden,
            hidden,
            hidden,
            stacked,
            rows_split,
            stacked,
            rows_split,
            rows_split,
            rows_split,
            P(None, BOTH),
            P(BOTH),
        ),
        check_vma=False,
    )
```

```python
import functools
import math

import jax
import jax.numpy as jnp
from jax import lax
from jax.experimental import pallas as pl
from jax.experimental.pallas import tpu as pltpu
from jax.sharding import PartitionSpec as P

D = 768
HEADS = 12
HDIM = 64
FF = 3072
BUCKETS = 32
PAIRS = HEADS // 2
LOG2E = math.log2(math.e)
LN2 = math.log(2.0)
epsilon = 1e-06
neg_large = -1e30
bucket_edges = (19, 21, 24, 27, 31, 35, 40, 46, 52, 59, 67, 77, 87, 99, 113)
f32 = jnp.float32
bf16 = jnp.bfloat16
NT = (((1,), (1,)), ((), ()))
NN = (((1,), (0,)), ((), ()))
TN = (((0,), (0,)), ((), ()))
BOTH = ("dp", "seq")
MESH = pl.DeviceIdType.MESH


def bucket_of(distance):
    above_count = sum(((distance >= border).astype(jnp.int32) for border in bucket_edges))
    return jnp.where(distance < 16, distance, 16 + above_count)


def mm(a, b, dims=NN):
    return lax.dot_general(a, b, dims, preferred_element_type=f32)


def head_lanes(which):
    low = lax.broadcasted_iota(jnp.int32, (1, 128), 1) < HDIM
    return low if which == 0 else jnp.logical_not(low)


def row_chunks(rows, keys, causal, step):
    return [
        (slice(i, i + step), (keys - rows + i + step) if causal else keys)
        for i in range(0, rows, step)
    ]


def near_bias(near_ref, which):
    row = lax.broadcasted_iota(jnp.int32, (128, 256), 0)
    column = lax.broadcasted_iota(jnp.int32, (128, 256), 1)
    tiles = []
    for flag in (0, 1):
        line = near_ref[0, 2 * which + flag : 2 * which + flag + 1, :]
        tile = pltpu.roll(jnp.broadcast_to(line, (128, 256)), 0, 1, stride=1, stride_axis=0)
        tiles.append(jnp.where(column - row > 128, neg_large, tile))
    return tiles


def diagonal_sums(tile):
    for step in (64, 32, 16, 8):
        tile = tile[:step] + pltpu.roll(tile[step:], 256 - step, 1)
    row = lax.broadcasted_iota(jnp.int32, (8, 256), 0)
    for step in (4, 2, 1):
        tile = jnp.where((row & step) != 0, pltpu.roll(tile, 256 - step, 1), tile)
    return jnp.sum(tile, axis=0, keepdims=True)


def attend_body(rows, keys, causal, step, *refs):
    if causal:
        q_ref, k_ref, v_ref, qx_ref, kx_ref, far_ref, near_ref, flag_ref = refs[:8]
    else:
        q_ref, k_ref, v_ref, qx_ref, kx_ref = refs[:5]
    o_ref, e_ref, inv_ref = refs[-3:]
    extra = kx_ref[...]
    if causal:
        extra = extra + far_ref[0]
    key_pair = k_ref[...]
    value_pair = v_ref[...]
    chunks = row_chunks(rows, keys, causal, step)
    found = []
    for which in (0, 1):
        mine = head_lanes(which)
        key_head = jnp.where(mine, key_pair, extra)
        value_head = jnp.where(mine, value_pair, jnp.ones_like(value_pair))
        if causal:
            tile_zero, tile_one = near_bias(near_ref, which)
        parts = []
        for here, width in chunks:
            query = jnp.where(mine, q_ref[here], qx_ref[here])
            scores = mm(query, key_head[:width], NT)
            if causal:
                cut = width - 256
                near = scores[:, cut:] + jnp.where(flag_ref[here, :1] > 0, tile_one, tile_zero)
                far = scores[:, :cut]
                peak = jnp.maximum(
                    jnp.max(far, axis=1, keepdims=True), jnp.max(near, axis=1, keepdims=True)
                )
                near = jnp.exp2(near - peak).astype(bf16)
                far = jnp.exp2(far - peak).astype(bf16)
                e_ref[which, here, :cut] = far
                e_ref[which, here, cut:width] = near
                mixed = mm(far, value_head[:cut]) + mm(near, value_head[cut:width])
            else:
                peak = jnp.max(scores, axis=1, keepdims=True)
                weights = jnp.exp2(scores - peak).astype(bf16)
                e_ref[which, here, :] = weights
                mixed = mm(weights, value_head)
            total = mixed[:, HDIM : HDIM + 1] if which == 0 else mixed[:, 0:1]
            inverse = 1.0 / total
            parts.append((mixed * inverse, jnp.broadcast_to(inverse, mixed.shape)))
        found.append(parts)
    low = head_lanes(0)
    for index, (here, _) in enumerate(chunks):
        o_ref[here] = jnp.where(low, found[0][index][0], found[1][index][0]).astype(bf16)
        inv_ref[here] = jnp.where(low, found[0][index][1], found[1][index][1])


def pair_columns(rows):
    return pl.BlockSpec((rows, 128), lambda p: (0, p))


def same_block(rows):
    return pl.BlockSpec((rows, 128), lambda p: (0, 0))


def per_pair(height, width):
    return pl.BlockSpec((1, height, width), lambda p: (p, 0, 0))


def attend(query, key, value, query_extra, key_extra, far=None, near=None, flags=None):
    rows, keys = query.shape[0], key.shape[0]
    causal = far is not None
    step = 128 if causal else min(256, rows)
    operands = [query, key, value, query_extra, key_extra]
    specs = [
        pair_columns(rows),
        pair_columns(keys),
        pair_columns(keys),
        same_block(rows),
        same_block(keys),
    ]
    if causal:
        operands += [far, near, flags]
        specs += [per_pair(1, 128), per_pair(4, 256), same_block(rows)]
    work = HEADS * rows * keys
    return pl.pallas_call(
        functools.partial(attend_body, rows, keys, causal, step),
        grid=(PAIRS,),
        in_specs=specs,
        out_specs=(
            pair_columns(rows),
            pl.BlockSpec((2, rows, keys), lambda p: (p, 0, 0)),
            pair_columns(rows),
        ),
        out_shape=(
            jax.ShapeDtypeStruct((rows, D), bf16),
            jax.ShapeDtypeStruct((HEADS, rows, keys), bf16),
            jax.ShapeDtypeStruct((rows, D), f32),
        ),
        compiler_params=pltpu.CompilerParams(vmem_limit_bytes=56 << 20),
        cost_estimate=pl.CostEstimate(
            flops=4 * work * 256, bytes_accessed=2 * work, transcendentals=work
        ),
        name="attend_causal" if causal else "attend_cross",
    )(*operands)


def attend_back_body(rows, keys, causal, step, *refs):
    q_ref, k_ref, v_ref, e_ref, o_ref, inv_ref, d_ref = refs[:7]
    if causal:
        flag_ref, dq_ref, dk_ref, dv_ref, near_ref, sum_ref, ds_ref = refs[7:]
    else:
        dq_ref, dk_ref, dv_ref, ds_ref = refs[7:]
    lane = lax.broadcasted_iota(jnp.int32, (1, 128), 1)
    key_pair = k_ref[...]
    value_pair = v_ref[...]
    scaled = (d_ref[...].astype(f32) * inv_ref[...]).astype(bf16)
    product = scaled.astype(f32) * o_ref[...].astype(f32)
    scaled_t = scaled.T
    query_t = q_ref[...].T
    chunks = row_chunks(rows, keys, causal, step)
    query_parts = []
    for which in (0, 1):
        mine = head_lanes(which)
        base = HDIM if which == 0 else 0
        value_head = jnp.where(mine, value_pair, jnp.ones_like(value_pair))
        key_head = jnp.where(mine, key_pair, jnp.ones_like(key_pair))
        delta = jnp.sum(jnp.where(mine, product, 0.0), axis=1, keepdims=True)
        high = delta.astype(bf16)
        rest = (delta - high.astype(f32)).astype(bf16)
        extra = jnp.where(
            lane == base, -high, jnp.where(lane == base + 1, -rest, jnp.zeros_like(rest))
        )
        grad_head = jnp.where(mine, scaled, extra)
        parts = []
        if causal:
            near_all = jnp.zeros((128, 256), f32)
            near_one = jnp.zeros((128, 256), f32)
        for here, width in chunks:
            centred = mm(grad_head[here], value_head[:width], NT)
            grad_scores = e_ref[which, here, :width].astype(f32) * centred
            if causal:
                near = grad_scores[:, width - 256 :]
                near_all = near_all + near
                near_one = near_one + jnp.where(flag_ref[here, :1] > 0, near, 0.0)
            grad_scores = grad_scores.astype(bf16)
            ds_ref[here, :width] = grad_scores
            parts.append(mm(grad_scores, key_head[:width]))
        query_parts.append(parts)
        half = slice(HDIM * which, HDIM * which + HDIM)
        if causal:
            spans = [(slice(0, keys - rows), 0)] if keys > rows else []
            spans += [
                (slice(keys - rows + i, keys - rows + i + step), i) for i in range(0, rows, step)
            ]
        else:
            spans = [(slice(0, keys), 0)]
        for span, first in spans:
            grad_key = mm(query_t[half, first:], ds_ref[first:, span])
            dk_ref[half, span] = (grad_key * LN2).astype(dk_ref.dtype)
            grad_value = mm(scaled_t[half, first:], e_ref[which, first:, span])
            dv_ref[half, span] = grad_value.astype(dv_ref.dtype)
        if causal:
            for flag, tile in ((0, near_all - near_one), (1, near_one)):
                near_ref[0, 2 * which + flag : 2 * which + flag + 1, :] = diagonal_sums(tile)
    low = head_lanes(0)
    for index, (here, _) in enumerate(chunks):
        both = jnp.where(low, query_parts[0][index], query_parts[1][index])
        dq_ref[here] = (both * 0.125).astype(dq_ref.dtype)
    if causal:
        flagged = flag_ref[:, :1] > 0
        for which in (0, 1):
            whole = jnp.concatenate(query_parts[which], axis=0)
            one = jnp.sum(jnp.where(flagged, whole, 0.0), axis=0, keepdims=True)
            every = jnp.sum(whole, axis=0, keepdims=True)
            sum_ref[0, 2 * which : 2 * which + 1, :] = every - one
            sum_ref[0, 2 * which + 1 : 2 * which + 2, :] = one


def attend_back(query, key, value, weights, mixed, inverse, grad_mixed, flags=None):
    rows, keys = query.shape[0], key.shape[0]
    causal = flags is not None
    step = 128 if causal else min(256, rows)
    operands = [query, key, value, weights, mixed, inverse, grad_mixed]
    specs = [
        pair_columns(rows),
        pair_columns(keys),
        pair_columns(keys),
        pl.BlockSpec((2, rows, keys), lambda p: (p, 0, 0)),
        pair_columns(rows),
        pair_columns(rows),
        pair_columns(rows),
    ]
    turned = jax.ShapeDtypeStruct((D, keys), bf16)
    turned_spec = pl.BlockSpec((128, keys), lambda p: (p, 0))
    shapes = [jax.ShapeDtypeStruct((rows, D), bf16), turned, turned]
    out_specs = [pair_columns(rows), turned_spec, turned_spec]
    if causal:
        operands.append(flags)
        specs.append(same_block(rows))
        shapes += [
            jax.ShapeDtypeStruct((PAIRS, 4, 256), f32),
            jax.ShapeDtypeStruct((PAIRS, 4, 128), f32),
        ]
        out_specs += [per_pair(4, 256), per_pair(4, 128)]
    work = HEADS * rows * keys
    return pl.pallas_call(
        functools.partial(attend_back_body, rows, keys, causal, step),
        grid=(PAIRS,),
        in_specs=specs,
        out_specs=tuple(out_specs),
        out_shape=tuple(shapes),
        scratch_shapes=[pltpu.VMEM((rows, keys), bf16)],
        compiler_params=pltpu.CompilerParams(vmem_limit_bytes=56 << 20),
        cost_estimate=pl.CostEstimate(
            flops=6 * work * 256, bytes_accessed=2 * work, transcendentals=0
        ),
        name="attend_causal_back" if causal else "attend_cross_back",
    )(*operands)


def place_here():
    index = lax.axis_index("dp")
    return index // 4, (index // 2) % 2, index % 2, lax.axis_index("seq")


def block_of(z, x, core, y):
    return ((z * 2 + x) * 2 + core) * 2 + y


def device_of(z, x, core, y):
    return ((z * 2 + x) * 2 + core, y)


def greet_neighbours(z, x, core, y):
    barrier = pltpu.get_barrier_semaphore()

    def greet(device):
        pl.semaphore_signal(barrier, inc=1, device_id=device, device_id_type=MESH)

    greet(device_of(z, x, 1 - core, y))
    greet(device_of(z, 1 - x, core, y))
    greet(device_of(z, x, core, 1 - y))

    @pl.when(z > 0)
    def _():
        greet(device_of(z - 1, x, core, y))

    @pl.when(z < 3)
    def _():
        greet(device_of(z + 1, x, core, y))

    pl.semaphore_wait(barrier, 4 + ((z + 1) // 2) % 2)


def gather_body(count, *refs):
    sources, wholes = refs[:count], refs[count : 2 * count]
    own_sems, up_sems, down_sems, side_sems, turn_sems, mate_sems, recv_sems = refs[2 * count :]
    z, x, core, y = place_here()
    mate = device_of(z, x, 1 - core, y)
    me = block_of(z, x, core, y)
    greet_neighbours(z, x, core, y)

    def near(which, side, turn):
        return ((x + side) % 2, (y + turn) % 2) if which == 0 else ((x + turn) % 2, (y + side) % 2)

    def send(which, source, block, send_sem, device):
        return pltpu.make_async_remote_copy(
            src_ref=source,
            dst_ref=wholes[which].at[block],
            send_sem=send_sem,
            recv_sem=recv_sems.at[which, block],
            device_id=device,
            device_id_type=MESH,
        )

    def copies(which, far, up, side, turn, source=None):
        at_z = z + far if up else z - far
        bx, by = near(which, side, turn)
        block = block_of(at_z, bx, core, by)
        source = wholes[which].at[block] if source is None else source
        slot = (2 * far + (1 if up else 0)) if far else 0
        slot = max(slot - 1, 0)
        out = [(None, send(which, source, block, mate_sems.at[which, (side * 2 + turn) * 7 + slot], mate))]
        if turn == 0:
            tx, ty = near(which, 0, 1)
            out.append(
                (None, send(which, source, block, turn_sems.at[which, side * 7 + slot], device_of(z, tx, core, ty)))
            )
            if side == 0:
                sx, sy = near(which, 1, 0)
                out.append((None, send(which, source, block, side_sems.at[which, slot], device_of(z, sx, core, sy))))
                if far == 0 or not up:
                    out.append(
                        (z < 3, send(which, source, block, up_sems.at[which, far], device_of(z + 1, x, core, y)))
                    )
                if far == 0 or up:
                    out.append(
                        (z > 0, send(which, source, block, down_sems.at[which, far], device_of(z - 1, x, core, y)))
                    )
        return block, out

    def when(condition, action):
        if condition is None:
            action()
        else:
            pl.when(condition)(action)

    def exists(far, up):
        if far == 0:
            return None
        return z + far < 4 if up else z - far >= 0

    def onwards(which, far, up, side, turn, source=None):
        def run():
            block, out = copies(which, far, up, side, turn, source)
            if source is None:
                pltpu.make_async_copy(wholes[which].at[block], wholes[which].at[block], recv_sems.at[which, block]).wait()
            for condition, copy in reversed(out):
                when(condition, copy.start)

        when(exists(far, up), run)

    own = [
        pltpu.make_async_copy(sources[i], wholes[i].at[me], own_sems.at[i]) for i in range(count)
    ]
    for which in range(count):
        onwards(which, 0, True, 0, 0, sources[which])
    for copy in own:
        copy.start()
    waves = [[] for _ in range(6)]
    for side in (0, 1):
        for turn in (0, 1):
            for far in range(4):
                for up in (False, True):
                    if far == 0 and (up or (side == 0 and turn == 0)):
                        continue
                    waves[far + side + turn].append((far, up, side, turn))
    for wave in waves:
        for far, up, side, turn in wave:
            for which in range(count):
                onwards(which, far, up, side, turn)
    for side in (0, 1):
        for turn in (0, 1):
            for far in range(4):
                for up in (False, True):
                    if far == 0 and up:
                        continue
                    for which in range(count):

                        def finish(which=which, far=far, up=up, side=side, turn=turn):
                            at_z = z + far if up else z - far
                            bx, by = near(which, side, turn)
                            block = block_of(at_z, bx, 1 - core, by)
                            whole = wholes[which].at[block]
                            pltpu.make_async_copy(whole, whole, recv_sems.at[which, block]).wait()
                            source = sources[which] if (far, side, turn) == (0, 0, 0) else None
                            _, out = copies(which, far, up, side, turn, source)
                            for condition, copy in out:
                                when(condition, copy.wait_send)

                        when(exists(far, up), finish)
    for copy in own:
        copy.wait()


def gather_blocks(*blocks):
    count = len(blocks)
    any_space = pl.BlockSpec(memory_space=pl.ANY)
    dma = pltpu.SemaphoreType.DMA
    return pl.pallas_call(
        functools.partial(gather_body, count),
        in_specs=[any_space] * count,
        out_specs=[any_space] * count,
        out_shape=[jax.ShapeDtypeStruct((32, *block.shape), block.dtype) for block in blocks],
        scratch_shapes=[
            dma((count,)),
            dma((count, 4)),
            dma((count, 4)),
            dma((count, 7)),
            dma((count, 14)),
            dma((count, 28)),
            dma((count, 32)),
        ],
        compiler_params=pltpu.CompilerParams(collective_id=0, has_side_effects=True),
        name="gather_blocks",
    )(*blocks)


def scatter_body(count, *refs):
    parts, outs = refs[:count], refs[count : 2 * count]
    refs = refs[2 * count :]
    sums, mate_in, first_in, second_in, line_in = (
        refs[i * count : (i + 1) * count] for i in range(5)
    )
    local_sems, mate_sems, first_sems, second_sems, line_sems = refs[5 * count : 5 * count + 5]
    mate_recv, first_recv, second_recv, line_recv = refs[5 * count + 5 :]
    z, x, core, y = place_here()
    greet_neighbours(z, x, core, y)
    half = z // 2
    order = (3 - 3 * half, 2 - half, 1 - z + 4 * half, z)

    def near(which, first, second):
        return ((x + second) % 2, (y + first) % 2) if which == 0 else ((x + first) % 2, (y + second) % 2)

    def cell(which, i, first, second):
        bx, by = near(which, first, second)
        return (order[i] * 2 + bx) * 2 + by

    def local(which, i, first, second):
        bx, by = near(which, first, second)
        here = cell(which, i, first, second)
        return pltpu.make_async_copy(
            parts[which].at[block_of(order[i], bx, core, by)],
            sums[which].at[here],
            local_sems.at[which, here],
        )

    def to_mate(which, i, first, second):
        bx, by = near(which, first, second)
        here = cell(which, i, first, second)
        return pltpu.make_async_remote_copy(
            src_ref=parts[which].at[block_of(order[i], bx, 1 - core, by)],
            dst_ref=mate_in[which].at[here],
            send_sem=mate_sems.at[which, here],
            recv_sem=mate_recv.at[which, here],
            device_id=device_of(z, x, 1 - core, y),
            device_id_type=MESH,
        )

    def to_first(which, i, second):
        bx, by = near(which, 1, 0)
        return pltpu.make_async_remote_copy(
            src_ref=sums[which].at[cell(which, i, 1, second)],
            dst_ref=first_in[which].at[2 * i + second],
            send_sem=first_sems.at[which, 2 * i + second],
            recv_sem=first_recv.at[which, 2 * i + second],
            device_id=device_of(z, bx, core, by),
            device_id_type=MESH,
        )

    def to_second(which, i):
        bx, by = near(which, 0, 1)
        return pltpu.make_async_remote_copy(
            src_ref=sums[which].at[cell(which, i, 0, 1)],
            dst_ref=second_in[which].at[i],
            send_sem=second_sems.at[which, i],
            recv_sem=second_recv.at[which, i],
            device_id=device_of(z, bx, core, by),
            device_id_type=MESH,
        )

    def along_line(which, i):
        step = 1 - 2 * half if i < 2 else 1 - 2 * (z % 2)
        came = (1 - step) // 2
        return came, pltpu.make_async_remote_copy(
            src_ref=sums[which].at[cell(which, i, 0, 0)],
            dst_ref=line_in[which].at[came * 4 + order[i]],
            send_sem=line_sems.at[which, i],
            recv_sem=line_recv.at[which, came * 4 + order[i]],
            device_id=device_of(z + step, x, core, y),
            device_id_type=MESH,
        )

    def arrived(buffer, sem):
        pltpu.make_async_copy(buffer, buffer, sem).wait()

    def wide(ref, index):
        return ref[index].astype(f32)

    every = [(1, 1), (1, 0), (0, 1), (0, 0)]
    for first, second in every:
        for i in range(4):
            for which in range(count):
                to_mate(which, i, first, second).start()
                local(which, i, first, second).start()

    def chip_sum(which, i, first, second):
        here = cell(which, i, first, second)
        local(which, i, first, second).wait()
        arrived(mate_in[which].at[here], mate_recv.at[which, here])
        return here, wide(sums[which], here) + wide(mate_in[which], here)

    for second in (1, 0):
        for i in range(4):
            for which in range(count):
                here, total = chip_sum(which, i, 1, second)
                sums[which][here] = total.astype(bf16)
                to_first(which, i, second).start()
    for i in range(4):
        for which in range(count):
            here, total = chip_sum(which, i, 0, 1)
            arrived(first_in[which].at[2 * i + 1], first_recv.at[which, 2 * i + 1])
            sums[which][here] = (total + wide(first_in[which], 2 * i + 1)).astype(bf16)
            to_second(which, i).start()
    middle = (z + 1) // 2 == 1
    for i in range(4):
        for which in range(count):
            here, total = chip_sum(which, i, 0, 0)
            arrived(first_in[which].at[2 * i], first_recv.at[which, 2 * i])
            arrived(second_in[which].at[i], second_recv.at[which, i])
            total = total + wide(first_in[which], 2 * i) + wide(second_in[which], i)
            if i < 3:
                sums[which][here] = total.astype(bf16)
                came, copy = along_line(which, i)
                slot = came * 4 + order[i]

                @pl.when(middle)
                def _():
                    arrived(line_in[which].at[slot], line_recv.at[which, slot])
                    sums[which][here] = (wide(sums[which], here) + wide(line_in[which], slot)).astype(bf16)

                copy.start()
            else:
                outs[which][...] = total
    for which in range(count):
        for came, there in ((0, z > 0), (1, z < 3)):
            slot = came * 4 + z

            @pl.when(there)
            def _():
                arrived(line_in[which].at[slot], line_recv.at[which, slot])
                outs[which][...] += wide(line_in[which], slot)

    for which in range(count):
        for i in range(4):
            for first, second in every:
                to_mate(which, i, first, second).wait_send()
            for second in (0, 1):
                to_first(which, i, second).wait_send()
            to_second(which, i).wait_send()
            if i < 3:
                along_line(which, i)[1].wait_send()


def scatter_blocks(*parts):
    count = len(parts)
    dma = pltpu.SemaphoreType.DMA

    def buffers(slots):
        return [pltpu.VMEM((slots, *part.shape[1:]), part.dtype) for part in parts]

    return pl.pallas_call(
        functools.partial(scatter_body, count),
        in_specs=[pl.BlockSpec(memory_space=pl.ANY)] * count,
        out_specs=[pl.BlockSpec(memory_space=pltpu.VMEM)] * count,
        out_shape=[jax.ShapeDtypeStruct(part.shape[1:], f32) for part in parts],
        scratch_shapes=buffers(16)
        + buffers(16)
        + buffers(8)
        + buffers(4)
        + buffers(8)
        + [
            dma((count, 16)),
            dma((count, 16)),
            dma((count, 8)),
            dma((count, 4)),
            dma((count, 3)),
            dma((count, 16)),
            dma((count, 8)),
            dma((count, 4)),
            dma((count, 8)),
        ],
        compiler_params=pltpu.CompilerParams(
            collective_id=1, has_side_effects=True, vmem_limit_bytes=48 << 20
        ),
        name="scatter_blocks",
    )(*parts)


def pair_of(positions, lengths):
    return (positions >= lengths[0]).astype(jnp.int32) + (
        positions >= lengths[0] + lengths[1]
    ).astype(jnp.int32)


def on_both_halves(columns):
    half = jnp.pad(columns, ((0, 0), (0, HDIM - columns.shape[1])))
    return jnp.concatenate((half, half), axis=1).astype(bf16)


def pair_mask(key_pairs):
    wrong = key_pairs[:, None] != jnp.arange(3, dtype=jnp.int32)[None, :]
    return on_both_halves(jnp.where(wrong, neg_large, 0.0))


def bias_parts(table):
    scaled = table.astype(f32) * LOG2E
    far = jnp.stack((scaled[BUCKETS - 1], scaled[2 * BUCKETS - 1]), axis=0)
    high = far.astype(bf16)
    rest = (far - high.astype(f32)).astype(bf16)
    columns = jnp.stack((high[0], rest[0], high[1], rest[1]), axis=1)
    columns = jnp.pad(columns, ((0, 0), (3, HDIM - 7))).reshape(PAIRS, 2, HDIM)
    far_lanes = jnp.concatenate((columns[:, 1], columns[:, 0]), axis=1).reshape(PAIRS, 1, 128)
    place = jnp.arange(256, dtype=jnp.int32)
    buckets = bucket_of(jnp.where(place <= 128, 128 - place, 384 - place))
    chosen = (buckets[:, None] == jnp.arange(BUCKETS, dtype=jnp.int32)[None, :]).astype(f32)
    steps = scaled.reshape(2, BUCKETS, HEADS) - far[:, None, :]
    lines = jnp.einsum("jb,fbh->hfj", chosen, steps, precision=lax.Precision.HIGHEST)
    return far_lanes, lines.reshape(PAIRS, 4, 256), chosen


def table_gradient(near_lines, row_sums, chosen):
    lines = near_lines.reshape(HEADS, 2, 256)
    near = jnp.einsum("hfj,jb->fbh", lines, chosen, precision=lax.Precision.HIGHEST)
    sums = row_sums.reshape(PAIRS, 2, 2, 128)
    every = jnp.stack((sums[:, 0, :, HDIM], sums[:, 1, :, 0]), axis=1).reshape(HEADS, 2).T
    rest = every - jnp.sum(near[:, : BUCKETS - 1], axis=1)
    return jnp.concatenate((near[:, : BUCKETS - 1], rest[:, None]), axis=1).reshape(-1)


def inverse_rms(values):
    return lax.rsqrt(jnp.mean(values * values, axis=-1, keepdims=True) + epsilon)


def norm_back(values, inverse, gain, grad):
    unit = values * inverse
    grad_gain = jnp.sum(grad * unit, axis=0)
    grad = grad * gain
    return inverse * (grad - unit * jnp.mean(grad * unit, axis=-1, keepdims=True)), grad_gain


def gelu_and_slope(value):
    upper = 0.5 * (1.0 + lax.erf(value * math.sqrt(0.5)))
    density = jnp.exp(-0.5 * value * value) * (1.0 / math.sqrt(2.0 * math.pi))
    return value * upper, upper + value * density


def seq_shift(array, count):
    length = array.shape[0]
    return lax.dynamic_slice_in_dim(jnp.concatenate((array, array), axis=0), count, length, axis=0)


def others_rows(rows, own_last):
    parts = lax.axis_size("seq")
    if parts == 2:
        return lax.ppermute(rows, "seq", [(0, 1)] if own_last else [(0, 1), (1, 0)])
    whole = lax.all_gather(rows, "seq", axis=0, tiled=True)
    step = rows.shape[0]
    start = lax.rem(lax.axis_index("seq") + 1, parts) * step
    return seq_shift(whole, start)[: (parts - 1) * step]


def to_owners(grads, own_last):
    parts = lax.axis_size("seq")
    if parts == 2:
        return lax.ppermute(grads, "seq", [(1, 0)] if own_last else [(0, 1), (1, 0)])
    step = grads.shape[0] // (parts - 1)
    whole = jnp.concatenate((grads, jnp.zeros((step, grads.shape[1]), grads.dtype)), axis=0)
    start = lax.rem(parts - 1 - lax.axis_index("seq"), parts) * step
    return lax.psum_scatter(seq_shift(whole, start), "seq", scatter_dimension=0, tiled=True)


def on_device(
    decoder_in,
    encoder_out,
    dec_lengths,
    pair_flags,
    enc_segments,
    self_proj,
    self_out,
    cross_proj,
    cross_out,
    ffn_in,
    ffn_out,
    norm_gains,
    rel_table,
    out_grad,
):
    shard = self_out.shape[0]
    small = jnp.concatenate((norm_gains, rel_table[None]), axis=0).T
    block_self = jnp.concatenate(
        (self_proj[0], self_proj[1], self_proj[2], self_out, jnp.pad(small, ((0, 0), (0, 124)))),
        axis=1,
    ).astype(bf16)
    block_cross = jnp.concatenate(
        (cross_proj[0], cross_proj[1], cross_proj[2], cross_out), axis=1
    ).astype(bf16)
    own_kernels = (lax.axis_size("dp"), lax.axis_size("seq")) == (16, 2)
    if own_kernels:
        all_self, all_cross = gather_blocks(block_self, block_cross)
        all_self = all_self.reshape(-1, all_self.shape[2])
        all_cross = all_cross.reshape(-1, all_cross.shape[2])
    else:
        all_self = lax.all_gather(block_self, BOTH, axis=0, tiled=True)
        all_cross = lax.all_gather(block_cross, BOTH, axis=0, tiled=True)
    mat_in = lax.all_gather(ffn_in.astype(bf16), BOTH, axis=0, tiled=True)
    mat_out = lax.all_gather(ffn_out.astype(bf16), BOTH, axis=0, tiled=True)
    self_q, self_k, self_v, out_self = (all_self[:, i * D : (i + 1) * D] for i in range(4))
    cross_q, cross_k, cross_v, out_cross = (all_cross[:, i * D : (i + 1) * D] for i in range(4))
    small_all = all_self[:, 4 * D : 4 * D + 4].T
    gains = small_all[:3].astype(f32)
    table = small_all[3].reshape(2 * BUCKETS, HEADS)

    tokens = decoder_in[0]
    memory = encoder_out[0]
    grad_out = out_grad[0]
    rows, enc_rows = tokens.shape[0], memory.shape[0]
    seq_count = lax.axis_size("seq")
    seq_index = lax.axis_index("seq")
    keys, enc_keys = rows * seq_count, enc_rows * seq_count

    lengths = dec_lengths[0]
    place_here = seq_index * rows + jnp.arange(rows, dtype=jnp.int32)
    place_keys = (seq_index + 1) * rows - keys + jnp.arange(keys, dtype=jnp.int32)
    pair_here = pair_of(place_here, lengths)
    pair_keys = jnp.where(place_keys < 0, 3, pair_of(place_keys, lengths))
    segments = seq_shift(enc_segments[0], seq_index * enc_rows)
    flag_here = jnp.where(
        pair_here == 0, pair_flags[0, 0], jnp.where(pair_here == 1, pair_flags[0, 1], 0)
    )
    one_pair = (pair_here[:, None] == jnp.arange(3, dtype=jnp.int32)[None, :]).astype(f32)
    one_flag = (flag_here[:, None] == jnp.array((0, 0, 1, 1), jnp.int32)[None, :]).astype(f32)
    query_extra = on_both_halves(jnp.concatenate((one_pair, one_flag), axis=1))
    key_extra = pair_mask(pair_keys)
    memory_extra = pair_mask(segments)
    flag_rows = jnp.broadcast_to(flag_here.astype(f32)[:, None], (rows, 128))
    far_lanes, near_lines, chosen = bias_parts(table)

    before = others_rows(tokens, True)
    others = others_rows(memory, False)
    memory_all = jnp.concatenate((memory, others), axis=0)

    tokens = tokens.astype(f32)
    inverse_one = inverse_rms(tokens)
    normed_one = (tokens * inverse_one * gains[0]).astype(bf16)
    before = before.astype(f32)
    normed_before = (before * inverse_rms(before) * gains[0]).astype(bf16)
    normed_all = jnp.concatenate((normed_before, normed_one), axis=0)
    scale = 0.125 * LOG2E
    query_one = (mm(normed_one, self_q) * scale).astype(bf16)
    key_one = mm(normed_all, self_k).astype(bf16)
    value_one = mm(normed_all, self_v).astype(bf16)
    mixed_one, weights_one, total_one = attend(
        query_one, key_one, value_one, query_extra, key_extra, far_lanes, near_lines, flag_rows
    )
    resid_one = tokens + mm(mixed_one, out_self)
    inverse_two = inverse_rms(resid_one)
    normed_two = (resid_one * inverse_two * gains[1]).astype(bf16)
    query_two = (mm(normed_two, cross_q) * scale).astype(bf16)
    key_two = mm(memory_all, cross_k).astype(bf16)
    value_two = mm(memory_all, cross_v).astype(bf16)
    mixed_two, weights_two, total_two = attend(
        query_two, key_two, value_two, query_extra, memory_extra
    )
    resid_two = resid_one + mm(mixed_two, out_cross)
    inverse_three = inverse_rms(resid_two)
    normed_three = (resid_two * inverse_three * gains[2]).astype(bf16)
    hidden_act, hidden_slope = gelu_and_slope(mm(normed_three, mat_in))
    hidden_act = hidden_act.astype(bf16)
    layer_out = (resid_two + mm(hidden_act, mat_out)).astype(bf16)

    grad_pre = (hidden_slope * mm(grad_out, mat_out, NT)).astype(bf16)
    grad_ffn_out = mm(hidden_act, grad_out, TN).astype(bf16)
    grad_ffn_in = mm(normed_three, grad_pre, TN).astype(bf16)
    part, gain_three = norm_back(resid_two, inverse_three, gains[2], mm(grad_pre, mat_in, NT))
    grad_resid = grad_out.astype(f32) + part
    grad_low = grad_resid.astype(bf16)
    grad_cross_out = mm(mixed_two, grad_low, TN)
    grad_mixed = mm(grad_low, out_cross, NT).astype(bf16)
    grad_query, grad_key, grad_value = attend_back(
        query_two, key_two, value_two, weights_two, mixed_two, total_two, grad_mixed
    )
    turned = (((0,), (1,)), ((), ()))
    grad_memory = mm(grad_key, cross_k, turned) + mm(grad_value, cross_v, turned)
    grad_others = to_owners(grad_memory[enc_rows:].astype(bf16), False)
    grad_encoder = grad_memory[:enc_rows] + grad_others.astype(f32)
    grad_cross = jnp.concatenate(
        (
            mm(normed_two, grad_query, TN),
            mm(memory_all, grad_key, turned),
            mm(memory_all, grad_value, turned),
            grad_cross_out,
        ),
        axis=1,
    ).astype(bf16)
    part, gain_two = norm_back(resid_one, inverse_two, gains[1], mm(grad_query, cross_q, NT))
    grad_resid = grad_resid + part
    grad_low = grad_resid.astype(bf16)
    grad_self_out = mm(mixed_one, grad_low, TN)
    grad_mixed = mm(grad_low, out_self, NT).astype(bf16)
    grad_query, grad_key, grad_value, near_sums, row_sums = attend_back(
        query_one, key_one, value_one, weights_one, mixed_one, total_one, grad_mixed, flag_rows
    )
    grad_normed = mm(grad_key, self_k, turned) + mm(grad_value, self_v, turned)
    grad_before = to_owners(grad_normed[: keys - rows].astype(bf16), True)
    grad_normed = grad_normed[keys - rows :] + mm(grad_query, self_q, NT)
    grad_normed = grad_normed + grad_before.astype(f32)
    part, gain_one = norm_back(tokens, inverse_one, gains[0], grad_normed)
    grad_input = grad_resid + part
    table_grad = table_gradient(near_sums, row_sums, chosen)
    small = jnp.stack((gain_one, gain_two, gain_three, table_grad), axis=1)
    grad_self = jnp.concatenate(
        (
            mm(normed_one, grad_query, TN),
            mm(normed_all, grad_key, turned),
            mm(normed_all, grad_value, turned),
            grad_self_out,
            jnp.pad(small, ((0, 0), (0, 124))),
        ),
        axis=1,
    ).astype(bf16)

    def owned(array):
        return lax.psum_scatter(array, BOTH, scatter_dimension=0, tiled=True).astype(f32)

    own_ffn_out = owned(grad_ffn_out)
    own_ffn_in = owned(grad_ffn_in)
    if own_kernels:
        own_self, own_cross = scatter_blocks(
            grad_self.reshape(-1, shard, grad_self.shape[1]),
            grad_cross.reshape(-1, shard, grad_cross.shape[1]),
        )
    else:
        own_cross = owned(grad_cross)
        own_self = owned(grad_self)
    own_small = own_self[:, 4 * D : 4 * D + 4].T

    def projections(block):
        return jnp.stack([block[:, i * D : (i + 1) * D] for i in range(3)], axis=0)

    return (
        layer_out[None],
        grad_input[None],
        grad_encoder[None],
        projections(own_self),
        own_self[:, 3 * D : 4 * D],
        projections(own_cross),
        own_cross[:, 3 * D : 4 * D],
        own_ffn_in,
        own_ffn_out,
        own_small[:3],
        own_small[3],
    )


def solution(mesh):
    hidden = P("dp", "seq", None)
    rows_split = P(BOTH, None)
    stacked = P(None, BOTH, None)
    stream = P("dp", None)
    return jax.shard_map(
        on_device,
        mesh=mesh,
        in_specs=(
            hidden,
            hidden,
            stream,
            stream,
            stream,
            stacked,
            rows_split,
            stacked,
            rows_split,
            rows_split,
            rows_split,
            P(None, BOTH),
            P(BOTH),
            hidden,
        ),
        out_specs=(
            hidden,
            hidden,
            hidden,
            stacked,
            rows_split,
            stacked,
            rows_split,
            rows_split,
            rows_split,
            P(None, BOTH),
            P(BOTH),
        ),
        check_vma=False,
    )
```

```python
import functools
import math

import jax
import jax.numpy as jnp
import numpy as np
from jax import lax
from jax.experimental import pallas as pl
from jax.experimental.pallas import tpu as pltpu
from jax.sharding import PartitionSpec as P

D = 768
HEADS = 12
HDIM = 64
FF = 3072
BUCKETS = 32
PAIRS = HEADS // 2
LOG2E = math.log2(math.e)
LN2 = math.log(2.0)
epsilon = 1e-06
neg_large = -1e30
bucket_edges = (19, 21, 24, 27, 31, 35, 40, 46, 52, 59, 67, 77, 87, 99, 113)
f32 = jnp.float32
bf16 = jnp.bfloat16
NT = (((1,), (1,)), ((), ()))
NN = (((1,), (0,)), ((), ()))
TN = (((0,), (0,)), ((), ()))
BOTH = ("dp", "seq")
MESH = pl.DeviceIdType.MESH


def mm(a, b, dims=NN):
    return lax.dot_general(a, b, dims, preferred_element_type=f32)


def head_lanes(which):
    low = lax.broadcasted_iota(jnp.int32, (1, 128), 1) < HDIM
    return low if which == 0 else jnp.logical_not(low)


def row_chunks(rows, keys, causal, step):
    return [
        (slice(i, i + step), (keys - rows + i + step) if causal else keys)
        for i in range(0, rows, step)
    ]


def near_bias(near_ref, which):
    row = lax.broadcasted_iota(jnp.int32, (128, 256), 0)
    column = lax.broadcasted_iota(jnp.int32, (128, 256), 1)
    tiles = []
    for flag in (0, 1):
        line = near_ref[0, 2 * which + flag : 2 * which + flag + 1, :]
        tile = pltpu.roll(jnp.broadcast_to(line, (128, 256)), 0, 1, stride=1, stride_axis=0)
        tiles.append(jnp.where(column - row > 128, neg_large, tile))
    return tiles


def diagonal_sums(tile):
    for step in (64, 32, 16, 8):
        tile = tile[:step] + pltpu.roll(tile[step:], 256 - step, 1)
    row = lax.broadcasted_iota(jnp.int32, (8, 256), 0)
    for step in (4, 2, 1):
        tile = jnp.where((row & step) != 0, pltpu.roll(tile, 256 - step, 1), tile)
    return jnp.sum(tile, axis=0, keepdims=True)


ROW, MEMORY_ROW, END_ONE, END_TWO, MEMORY_ONE, MEMORY_TWO, FLAG_ONE, FLAG_TWO = range(8)


def pairs_between(place, end_one, end_two):
    return (place >= end_one).astype(jnp.int32) + (place >= end_two).astype(jnp.int32)


def flagged(info, first, count, width):
    place = lax.broadcasted_iota(jnp.int32, (count, width), 0) + (info[ROW] + first)
    pair = pairs_between(place, info[END_ONE], info[END_TWO])
    return jnp.where(pair == 0, info[FLAG_ONE], jnp.where(pair == 1, info[FLAG_TWO], 0)) > 0


def extra_columns(info, rows, keys, causal, query_extra, key_extra):
    lane = lax.broadcasted_iota(jnp.int32, (rows, 128), 1) & (HDIM - 1)
    place = lax.broadcasted_iota(jnp.int32, (rows, 128), 0) + info[ROW]
    pair = pairs_between(place, info[END_ONE], info[END_TWO])
    flag = flagged(info, 0, rows, 128).astype(jnp.int32)
    wanted = jnp.where(lane < 3, pair, (flag << 1) + 3)
    chosen = jnp.where(lane < 3, lane, ((lane - 3) & ~1) + 3)
    here = jnp.logical_and(wanted == chosen, lane < 7)
    query_extra[...] = jnp.where(here, 1.0, 0.0).astype(bf16)
    lane = lax.broadcasted_iota(jnp.int32, (keys, 128), 1) & (HDIM - 1)
    place = lax.broadcasted_iota(jnp.int32, (keys, 128), 0)
    if causal:
        place = place + (info[ROW] + rows - keys)
        pair = pairs_between(place, info[END_ONE], info[END_TWO])
        pair = jnp.where(place < 0, 3, pair)
    else:
        place = place + info[MEMORY_ROW]
        place = jnp.where(place >= keys, place - keys, place)
        pair = pairs_between(place, info[MEMORY_ONE], info[MEMORY_TWO])
    wrong = jnp.logical_and(pair != lane, lane < 3)
    key_extra[...] = jnp.where(wrong, neg_large, 0.0).astype(bf16)


def attend_body(rows, keys, causal, step, parts, *refs):
    info, q_ref = refs[:2]
    key_refs, value_refs = refs[2 : 2 + parts], refs[2 + parts : 2 + 2 * parts]
    o_ref, e_ref, inv_ref, query_extra, key_extra = refs[-5:]

    @pl.when(pl.program_id(0) == 0)
    def _():
        extra_columns(info, rows, keys, causal, query_extra, key_extra)

    extra = key_extra[...]
    if causal:
        far_ref, near_ref = refs[2 + 2 * parts : 4 + 2 * parts]
        extra = extra + far_ref[0]
    key_pair = jnp.concatenate([ref[...] for ref in key_refs], axis=0)
    value_pair = jnp.concatenate([ref[...] for ref in value_refs], axis=0)
    chunks = row_chunks(rows, keys, causal, step)
    found = []
    for which in (0, 1):
        mine = head_lanes(which)
        key_head = jnp.where(mine, key_pair, extra)
        value_head = jnp.where(mine, value_pair, jnp.ones_like(value_pair))
        if causal:
            tile_zero, tile_one = near_bias(near_ref, which)
        done = []
        for here, width in chunks:
            query = jnp.where(mine, q_ref[here], query_extra[here])
            scores = mm(query, key_head[:width], NT)
            if causal:
                cut = width - 256
                flag = flagged(info, here.start, step, 1)
                near = scores[:, cut:] + jnp.where(flag, tile_one, tile_zero)
                far = scores[:, :cut]
                peak = jnp.maximum(
                    jnp.max(far, axis=1, keepdims=True), jnp.max(near, axis=1, keepdims=True)
                )
                near = jnp.exp2(near - peak).astype(bf16)
                far = jnp.exp2(far - peak).astype(bf16)
                e_ref[which, here, :cut] = far
                e_ref[which, here, cut:width] = near
                mixed = mm(far, value_head[:cut]) + mm(near, value_head[cut:width])
            else:
                peak = jnp.max(scores, axis=1, keepdims=True)
                weights = jnp.exp2(scores - peak).astype(bf16)
                e_ref[which, here, :] = weights
                mixed = mm(weights, value_head)
            total = mixed[:, HDIM : HDIM + 1] if which == 0 else mixed[:, 0:1]
            inverse = 1.0 / total
            done.append((mixed * inverse, jnp.broadcast_to(inverse, mixed.shape)))
        found.append(done)
    low = head_lanes(0)
    for index, (here, _) in enumerate(chunks):
        o_ref[here] = jnp.where(low, found[0][index][0], found[1][index][0]).astype(bf16)
        inv_ref[here] = jnp.where(low, found[0][index][1], found[1][index][1])


def pair_columns(rows, first=0):
    return pl.BlockSpec((rows, 128), lambda p: (0, first + p))


def operands_of(info, query, parts):
    arrays = [info, query] + [part[0] for part in parts] * 2
    specs = [pl.BlockSpec(memory_space=pltpu.SMEM), pair_columns(query.shape[0])]
    for place in (1, 2):
        specs += [pair_columns(part[0].shape[0], part[place]) for part in parts]
    return arrays, specs


def per_pair(height, width):
    return pl.BlockSpec((1, height, width), lambda p: (p, 0, 0))


def attend(info, rows, query, parts, far=None, near=None):
    keys = sum(part[0].shape[0] for part in parts)
    causal = far is not None
    step = 128 if causal else min(256, rows)
    operands, specs = operands_of(info, query, parts)
    if causal:
        operands += [far, near]
        specs += [per_pair(1, 128), per_pair(4, 256)]
    return pl.pallas_call(
        functools.partial(attend_body, rows, keys, causal, step, len(parts)),
        grid=(PAIRS,),
        in_specs=specs,
        out_specs=(
            pair_columns(rows),
            pl.BlockSpec((2, rows, keys), lambda p: (p, 0, 0)),
            pair_columns(rows),
        ),
        out_shape=(
            jax.ShapeDtypeStruct((rows, D), bf16),
            jax.ShapeDtypeStruct((HEADS, rows, keys), bf16),
            jax.ShapeDtypeStruct((rows, D), f32),
        ),
        scratch_shapes=[pltpu.VMEM((rows, 128), bf16), pltpu.VMEM((keys, 128), bf16)],
        compiler_params=pltpu.CompilerParams(vmem_limit_bytes=56 << 20),
        name="attend_causal" if causal else "attend_cross",
    )(*operands)


def attend_back_body(rows, keys, causal, step, parts, *refs):
    info, q_ref = refs[:2]
    key_refs, value_refs = refs[2 : 2 + parts], refs[2 + parts : 2 + 2 * parts]
    e_ref, o_ref, inv_ref, d_ref = refs[2 + 2 * parts : 6 + 2 * parts]
    if causal:
        dq_ref, dk_ref, dv_ref, near_ref, sum_ref, ds_ref = refs[6 + 2 * parts :]
    else:
        dq_ref, dk_ref, dv_ref, ds_ref = refs[6 + 2 * parts :]
    lane = lax.broadcasted_iota(jnp.int32, (1, 128), 1)
    key_pair = jnp.concatenate([ref[...] for ref in key_refs], axis=0)
    value_pair = jnp.concatenate([ref[...] for ref in value_refs], axis=0)
    scaled = (d_ref[...].astype(f32) * inv_ref[...]).astype(bf16)
    product = scaled.astype(f32) * o_ref[...].astype(f32)
    scaled_t = scaled.T
    query_t = q_ref[...].T
    chunks = row_chunks(rows, keys, causal, step)
    query_parts = []
    for which in (0, 1):
        mine = head_lanes(which)
        base = HDIM if which == 0 else 0
        value_head = jnp.where(mine, value_pair, jnp.ones_like(value_pair))
        key_head = jnp.where(mine, key_pair, jnp.ones_like(key_pair))
        delta = jnp.sum(jnp.where(mine, product, 0.0), axis=1, keepdims=True)
        high = delta.astype(bf16)
        rest = (delta - high.astype(f32)).astype(bf16)
        extra = jnp.where(
            lane == base, -high, jnp.where(lane == base + 1, -rest, jnp.zeros_like(rest))
        )
        grad_head = jnp.where(mine, scaled, extra)
        done = []
        if causal:
            near_all = jnp.zeros((128, 256), f32)
            near_one = jnp.zeros((128, 256), f32)
        for here, width in chunks:
            centred = mm(grad_head[here], value_head[:width], NT)
            grad_scores = e_ref[which, here, :width].astype(f32) * centred
            if causal:
                near = grad_scores[:, width - 256 :]
                near_all = near_all + near
                flag = flagged(info, here.start, step, 1)
                near_one = near_one + jnp.where(flag, near, 0.0)
            grad_scores = grad_scores.astype(bf16)
            ds_ref[here, :width] = grad_scores
            done.append(mm(grad_scores, key_head[:width]))
        query_parts.append(done)
        half = slice(HDIM * which, HDIM * which + HDIM)
        if causal:
            spans = [(slice(0, keys - rows), 0)] if keys > rows else []
            spans += [
                (slice(keys - rows + i, keys - rows + i + step), i) for i in range(0, rows, step)
            ]
        else:
            spans = [(slice(0, keys), 0)]
        for span, first in spans:
            grad_key = mm(query_t[half, first:], ds_ref[first:, span])
            dk_ref[half, span] = (grad_key * LN2).astype(dk_ref.dtype)
            grad_value = mm(scaled_t[half, first:], e_ref[which, first:, span])
            dv_ref[half, span] = grad_value.astype(dv_ref.dtype)
        if causal:
            for flag, tile in ((0, near_all - near_one), (1, near_one)):
                near_ref[0, 2 * which + flag : 2 * which + flag + 1, :] = diagonal_sums(tile)
    low = head_lanes(0)
    for index, (here, _) in enumerate(chunks):
        both = jnp.where(low, query_parts[0][index], query_parts[1][index])
        dq_ref[here] = (both * 0.125).astype(dq_ref.dtype)
    if causal:
        flags = flagged(info, 0, rows, 1)
        for which in (0, 1):
            whole = jnp.concatenate(query_parts[which], axis=0)
            one = jnp.sum(jnp.where(flags, whole, 0.0), axis=0, keepdims=True)
            every = jnp.sum(whole, axis=0, keepdims=True)
            sum_ref[0, 2 * which : 2 * which + 1, :] = every - one
            sum_ref[0, 2 * which + 1 : 2 * which + 2, :] = one


def attend_back(info, query, parts, weights, mixed, inverse, grad_mixed, causal):
    rows, keys = weights.shape[1:]
    step = 128 if causal else min(256, rows)
    operands, specs = operands_of(info, query, parts)
    operands += [weights, mixed, inverse, grad_mixed]
    specs += [pl.BlockSpec((2, rows, keys), lambda p: (p, 0, 0))] + [pair_columns(rows)] * 3
    turned = jax.ShapeDtypeStruct((D, keys), bf16)
    turned_spec = pl.BlockSpec((128, keys), lambda p: (p, 0))
    shapes = [jax.ShapeDtypeStruct((rows, D), bf16), turned, turned]
    out_specs = [pair_columns(rows), turned_spec, turned_spec]
    if causal:
        shapes += [
            jax.ShapeDtypeStruct((PAIRS, 4, 256), f32),
            jax.ShapeDtypeStruct((PAIRS, 4, 128), f32),
        ]
        out_specs += [per_pair(4, 256), per_pair(4, 128)]
    return pl.pallas_call(
        functools.partial(attend_back_body, rows, keys, causal, step, len(parts)),
        grid=(PAIRS,),
        in_specs=specs,
        out_specs=tuple(out_specs),
        out_shape=tuple(shapes),
        scratch_shapes=[pltpu.VMEM((rows, keys), bf16)],
        compiler_params=pltpu.CompilerParams(vmem_limit_bytes=56 << 20),
        name="attend_causal_back" if causal else "attend_cross_back",
    )(*operands)


def place_here():
    index = lax.axis_index("dp")
    return index // 4, (index // 2) % 2, index % 2, lax.axis_index("seq")


def block_of(z, x, core, y):
    return ((z * 2 + x) * 2 + core) * 2 + y


def device_of(z, x, core, y):
    return ((z * 2 + x) * 2 + core, y)


def greet_neighbours(z, x, core, y):
    barrier = pltpu.get_barrier_semaphore()

    def greet(device):
        pl.semaphore_signal(barrier, inc=1, device_id=device, device_id_type=MESH)

    greet(device_of(z, x, 1 - core, y))
    greet(device_of(z, 1 - x, core, y))
    greet(device_of(z, x, core, 1 - y))

    @pl.when(z > 0)
    def _():
        greet(device_of(z - 1, x, core, y))

    @pl.when(z < 3)
    def _():
        greet(device_of(z + 1, x, core, y))

    pl.semaphore_wait(barrier, 4 + ((z + 1) // 2) % 2)


def gather_body(count, *refs):
    sources, wholes = refs[:count], refs[count : 2 * count]
    own_sems, up_sems, down_sems, side_sems, turn_sems, mate_sems, recv_sems = refs[2 * count :]
    z, x, core, y = place_here()
    mate = device_of(z, x, 1 - core, y)
    me = block_of(z, x, core, y)
    greet_neighbours(z, x, core, y)

    def near(which, side, turn):
        return ((x + side) % 2, (y + turn) % 2) if which == 0 else ((x + turn) % 2, (y + side) % 2)

    def send(which, source, block, send_sem, device):
        return pltpu.make_async_remote_copy(
            src_ref=source,
            dst_ref=wholes[which].at[block],
            send_sem=send_sem,
            recv_sem=recv_sems.at[which, block],
            device_id=device,
            device_id_type=MESH,
        )

    def copies(which, far, up, side, turn, source=None):
        at_z = z + far if up else z - far
        bx, by = near(which, side, turn)
        block = block_of(at_z, bx, core, by)
        source = wholes[which].at[block] if source is None else source
        slot = (2 * far + (1 if up else 0)) if far else 0
        slot = max(slot - 1, 0)
        out = [(None, send(which, source, block, mate_sems.at[which, (side * 2 + turn) * 7 + slot], mate))]
        if turn == 0:
            tx, ty = near(which, 0, 1)
            out.append(
                (None, send(which, source, block, turn_sems.at[which, side * 7 + slot], device_of(z, tx, core, ty)))
            )
            if side == 0:
                sx, sy = near(which, 1, 0)
                out.append((None, send(which, source, block, side_sems.at[which, slot], device_of(z, sx, core, sy))))
                if far == 0 or not up:
                    out.append(
                        (z < 3, send(which, source, block, up_sems.at[which, far], device_of(z + 1, x, core, y)))
                    )
                if far == 0 or up:
                    out.append(
                        (z > 0, send(which, source, block, down_sems.at[which, far], device_of(z - 1, x, core, y)))
                    )
        return block, out

    def when(condition, action):
        if condition is None:
            action()
        else:
            pl.when(condition)(action)

    def exists(far, up):
        if far == 0:
            return None
        return z + far < 4 if up else z - far >= 0

    def onwards(which, far, up, side, turn, source=None):
        def run():
            block, out = copies(which, far, up, side, turn, source)
            if source is None:
                pltpu.make_async_copy(wholes[which].at[block], wholes[which].at[block], recv_sems.at[which, block]).wait()
            for condition, copy in reversed(out):
                when(condition, copy.start)

        when(exists(far, up), run)

    own = [
        pltpu.make_async_copy(sources[i], wholes[i].at[me], own_sems.at[i]) for i in range(count)
    ]
    for which in range(count):
        onwards(which, 0, True, 0, 0, sources[which])
    for copy in own:
        copy.start()
    waves = [[] for _ in range(6)]
    for side in (0, 1):
        for turn in (0, 1):
            for far in range(4):
                for up in (False, True):
                    if far == 0 and (up or (side == 0 and turn == 0)):
                        continue
                    waves[far + side + turn].append((far, up, side, turn))
    for wave in waves:
        for far, up, side, turn in wave:
            for which in range(count):
                onwards(which, far, up, side, turn)
    for side in (0, 1):
        for turn in (0, 1):
            for far in range(4):
                for up in (False, True):
                    if far == 0 and up:
                        continue
                    for which in range(count):

                        def finish(which=which, far=far, up=up, side=side, turn=turn):
                            at_z = z + far if up else z - far
                            bx, by = near(which, side, turn)
                            block = block_of(at_z, bx, 1 - core, by)
                            whole = wholes[which].at[block]
                            pltpu.make_async_copy(whole, whole, recv_sems.at[which, block]).wait()
                            source = sources[which] if (far, side, turn) == (0, 0, 0) else None
                            _, out = copies(which, far, up, side, turn, source)
                            for condition, copy in out:
                                when(condition, copy.wait_send)

                        when(exists(far, up), finish)
    for copy in own:
        copy.wait()


def gather_blocks(*blocks):
    count = len(blocks)
    any_space = pl.BlockSpec(memory_space=pl.ANY)
    dma = pltpu.SemaphoreType.DMA
    return pl.pallas_call(
        functools.partial(gather_body, count),
        in_specs=[any_space] * count,
        out_specs=[any_space] * count,
        out_shape=[jax.ShapeDtypeStruct((32, *block.shape), block.dtype) for block in blocks],
        scratch_shapes=[
            dma((count,)),
            dma((count, 4)),
            dma((count, 4)),
            dma((count, 7)),
            dma((count, 14)),
            dma((count, 28)),
            dma((count, 32)),
        ],
        compiler_params=pltpu.CompilerParams(collective_id=0, has_side_effects=True),
        name="gather_blocks",
    )(*blocks)


SELF_PRODUCTS = (((1,), 2, False), ((0, 1), 3, True), ((0, 1), 4, True), ((5,), 6, False))
CROSS_PRODUCTS = (((0,), 1, False), ((2, 3), 4, True), ((2, 3), 5, True), ((6,), 7, False))


def scatter_body(counts, *refs):
    total_in = sum(counts)
    arrays, small, outs = refs[:total_in], refs[total_in], refs[total_in + 1 : total_in + 6]
    refs = refs[total_in + 6 :]
    held, small_held = refs[:total_in], refs[total_in]
    refs = refs[total_in + 1 :]
    parts, mate_in, first_in, second_in, line_in = (refs[2 * i : 2 * i + 2] for i in range(5))
    load_sems, mate_sems, first_sems, second_sems, line_sems = refs[10:15]
    mate_recv, first_recv, second_recv, line_recv = refs[15:]
    z, x, core, y = place_here()
    loads = [
        pltpu.make_async_copy(source, target, load_sems.at[i])
        for i, (source, target) in enumerate(zip((*arrays, small), (*held, small_held)))
    ]
    for load in loads:
        load.start()
    greet_neighbours(z, x, core, y)
    half = z // 2
    order = (3 - 3 * half, 2 - half, 1 - z + 4 * half, z)

    def near(first, second):
        return (x + first) % 2, (y + second) % 2

    def block(i, first, second, other_core=0):
        bx, by = near(first, second)
        return block_of(order[i], bx, (core + other_core) % 2, by)

    def slot_of(i, first, second):
        bx, by = near(first, second)
        return (order[i] * 2 + bx) * 2 + by

    def remote(source, target, send_sem, recv_sem, device):
        return pltpu.make_async_remote_copy(
            src_ref=source,
            dst_ref=target,
            send_sem=send_sem,
            recv_sem=recv_sem,
            device_id=device,
            device_id_type=MESH,
        )

    def to_mate(which, i, first, second):
        slot = slot_of(i, first, second)
        return remote(
            parts[which].at[block(i, first, second, 1)],
            mate_in[which].at[slot],
            mate_sems.at[which, slot],
            mate_recv.at[which, slot],
            device_of(z, x, 1 - core, y),
        )

    def to_first(which, i, second):
        bx, by = near(1, 0)
        return remote(
            parts[which].at[block(i, 1, second)],
            first_in[which].at[2 * i + second],
            first_sems.at[which, 2 * i + second],
            first_recv.at[which, 2 * i + second],
            device_of(z, bx, core, by),
        )

    def to_second(which, i):
        bx, by = near(0, 1)
        return remote(
            parts[which].at[block(i, 0, 1)],
            second_in[which].at[i],
            second_sems.at[which, i],
            second_recv.at[which, i],
            device_of(z, bx, core, by),
        )

    def along_line(which, i, second=0):
        step = 1 - 2 * half if i < 2 else 1 - 2 * (z % 2)
        came = (1 - step) // 2
        slot = (came * 4 + order[i]) * 2 + second
        return slot, remote(
            parts[which].at[block(i, 0, second)],
            line_in[which].at[slot],
            line_sems.at[which, 2 * i + second],
            line_recv.at[which, slot],
            device_of(z + step, x, core, y),
        )

    def arrived(buffer, sem):
        pltpu.make_async_copy(buffer, buffer, sem).wait()

    def wide(ref, index):
        return ref[index].astype(f32)

    every = [(1, 1), (1, 0), (0, 1), (0, 0)]

    def products(which, i):
        first = 0 if which == 0 else counts[0]
        height = 8 * parts[which].shape[1]
        odd = order[i] % 2
        window = pl.ds(pl.multiple_of(order[i] * height - odd * 64, 128), height + 64)
        blocks = pl.ds(order[i] * 8, 8)
        taken = {}
        for column, (lefts, right, turned) in enumerate(SELF_PRODUCTS if which == 0 else CROSS_PRODUCTS):
            if i == 0:
                for needed in (*lefts, right):
                    if needed in waiting[which]:
                        waiting[which].remove(needed)
                        loads[first + needed].wait()
            for left in lefts:
                if left not in taken:
                    rows = held[first + left][:, window].T
                    taken[left] = jnp.where(odd > 0, rows[64:], rows[:height])
            other = held[first + right][...]
            value = mm(jnp.concatenate([taken[left] for left in lefts], axis=1), other, NT if turned else NN)
            value = value.reshape(8, height // 8, value.shape[1]).astype(bf16)
            parts[which][blocks, :, column * D : (column + 1) * D] = value
        if which == 0:
            if i == 0:
                loads[-1].wait()
            parts[0][blocks, :, 4 * D :] = small_held[blocks]

    waiting = [set(range(counts[0])), set(range(counts[1]))]

    def make(i):
        for which in (1, 0):
            products(which, i)
            for first, second in every:
                to_mate(which, i, first, second).start()

    def chip_sum(which, i, first, second):
        here = block(i, first, second)
        slot = slot_of(i, first, second)
        arrived(mate_in[which].at[slot], mate_recv.at[which, slot])
        return here, wide(parts[which], here) + wide(mate_in[which], slot)

    def send_first(i):
        for second in (1, 0):
            for which in (1, 0):
                here, total = chip_sum(which, i, 1, second)
                parts[which][here] = total.astype(bf16)
                to_first(which, i, second).start()

    middle = (z + 1) // 2 == 1

    def after_first(which, i, second):
        here, total = chip_sum(which, i, 0, second)
        arrived(first_in[which].at[2 * i + second], first_recv.at[which, 2 * i + second])
        return here, total + wide(first_in[which], 2 * i + second)

    def send_second(i):
        here, total = after_first(1, i, 1)
        parts[1][here] = total.astype(bf16)
        to_second(1, i).start()

    def send_line(which, i, second, here, total):
        parts[which][here] = total.astype(bf16)
        slot, copy = along_line(which, i, second)

        @pl.when(middle)
        def _():
            arrived(line_in[which].at[slot], line_recv.at[which, slot])
            total = wide(parts[which], here) + wide(line_in[which], slot)
            parts[which][here] = total.astype(bf16)

        copy.start()

    def line_self(i):
        for second in (1, 0):
            send_line(0, i, second, *after_first(0, i, second))

    def line_cross(i):
        here, total = after_first(1, i, 0)
        arrived(second_in[1].at[i], second_recv.at[1, i])
        total = total + wide(second_in[1], i)
        if i < 3:
            send_line(1, i, 0, here, total)
        else:
            put(1, total, False)

    def from_line(which, second, add):
        for came, there in ((0, z > 0), (1, z < 3)):
            slot = (came * 4 + z) * 2 + second

            @pl.when(there)
            def _():
                arrived(line_in[which].at[slot], line_recv.at[which, slot])
                add(wide(line_in[which], slot))

    def last_self():
        here, total = after_first(0, 3, 1)
        parts[0][here] = total.astype(bf16)

        def add(value):
            parts[0][here] = (wide(parts[0], here) + value).astype(bf16)

        from_line(0, 1, add)
        to_second(0, 3).start()
        put(0, after_first(0, 3, 0)[1], False)
        from_line(0, 0, lambda value: put(0, value, True))

    def put(which, value, add):
        stacked, single = outs[2 * which : 2 * which + 2]
        targets = [(stacked.at[j], j) for j in range(3)] + [(single, 3)]
        for target, j in targets:
            piece = value[:, j * D : (j + 1) * D]
            target[...] = target[...] + piece if add else piece
        if which == 0:
            piece = value[:, 4 * D :]
            outs[4][...] = outs[4][...] + piece if add else piece


    make(0)
    make(1)
    send_first(0)
    make(2)
    send_first(1)
    send_second(0)
    line_self(0)
    make(3)
    send_first(2)
    send_second(1)
    line_self(1)
    line_cross(0)
    send_first(3)
    send_second(2)
    line_self(2)
    line_cross(1)
    send_second(3)
    line_cross(2)
    last_self()
    line_cross(3)
    from_line(1, 0, lambda value: put(1, value, True))
    arrived(second_in[0].at[3], second_recv.at[0, 3])
    put(0, wide(second_in[0], 3), True)

    for which in (0, 1):
        for i in range(4):
            for first, second in every:
                to_mate(which, i, first, second).wait_send()
            for second in (0, 1):
                to_first(which, i, second).wait_send()
            if which == 1 or i == 3:
                to_second(which, i).wait_send()
            if i < 3:
                for second in (0, 1)[: 2 - which]:
                    along_line(which, i, second)[1].wait_send()


def scatter_products(self_arrays, cross_arrays, small):
    counts = (len(self_arrays), len(cross_arrays))
    arrays = (*self_arrays, *cross_arrays)
    shard = small.shape[1]
    shapes = [(shard, 4 * D + small.shape[2]), (shard, 4 * D)]
    dma = pltpu.SemaphoreType.DMA

    def buffers(slots):
        return [pltpu.VMEM((slots, *shape), bf16) for shape in shapes]

    return pl.pallas_call(
        functools.partial(scatter_body, counts),
        in_specs=[pl.BlockSpec(memory_space=pl.ANY)] * (len(arrays) + 1),
        out_specs=[pl.BlockSpec(memory_space=pltpu.VMEM)] * 5,
        out_shape=[
            jax.ShapeDtypeStruct(shape, f32)
            for shape in ((3, shard, D), (shard, D), (3, shard, D), (shard, D), (shard, small.shape[2]))
        ],
        scratch_shapes=[pltpu.VMEM(array.shape, array.dtype) for array in (*arrays, small)]
        + buffers(32)
        + buffers(16)
        + buffers(8)
        + buffers(4)
        + buffers(16)
        + [
            dma((len(arrays) + 1,)),
            dma((2, 16)),
            dma((2, 8)),
            dma((2, 4)),
            dma((2, 6)),
            dma((2, 16)),
            dma((2, 8)),
            dma((2, 4)),
            dma((2, 16)),
        ],
        compiler_params=pltpu.CompilerParams(
            collective_id=1, has_side_effects=True, vmem_limit_bytes=60 << 20
        ),
        name="scatter_products",
    )(*arrays, small)


def inverse_rms(values):
    return lax.rsqrt(jnp.mean(values * values, axis=-1, keepdims=True) + epsilon)


def norm_back(values, inverse, gain, grad):
    unit = values * inverse
    grad = grad * gain
    return inverse * (grad - unit * jnp.mean(grad * unit, axis=-1, keepdims=True))


def gelu_and_slope(value):
    upper = 0.5 * (1.0 + lax.erf(value * math.sqrt(0.5)))
    density = jnp.exp(-0.5 * value * value) * (1.0 / math.sqrt(2.0 * math.pi))
    return value * upper, upper + value * density


def feed_forward_body(rows, *refs):
    x1_ref, mixed_ref, out_ref, gain_ref, grad_ref, in_ref, back_ref = refs[:7]
    layer_ref, dx_ref, low_ref, mixed_back_ref, weight_ref = refs[7:12]
    x2, h3, h3_t, total, back, act = refs[12:]
    step, part = pl.program_id(0), pl.program_id(1)
    first = jnp.logical_and(step == 0, part == 0)
    last = jnp.logical_and(step == pl.num_programs(0) - 1, part == 1)

    @pl.when(first)
    def _():
        value = x1_ref[...] + mm(mixed_ref[...], out_ref[...])
        x2[...] = value
        normed = (value * inverse_rms(value) * gain_ref[...]).astype(bf16)
        h3[...] = normed
        h3_t[...] = normed.T
        total[...] = value
        back[...] = jnp.zeros_like(back)

    @pl.when(part == 0)
    def _():
        hidden, slope = gelu_and_slope(mm(h3[...], in_ref[...]))
        hidden = hidden.astype(bf16)
        act[...] = hidden
        total[...] += mm(hidden, back_ref[...])
        grad_pre = (slope * mm(grad_ref[...], back_ref[...], NT)).astype(bf16)
        back[...] += mm(grad_pre, in_ref[...], NT)
        weight_ref[...] = mm(h3_t[...], grad_pre).astype(bf16)

    @pl.when(part == 1)
    def _():
        weight_ref[...] = mm(act[...].T, grad_ref[...]).astype(bf16)

    @pl.when(last)
    def _():
        layer_ref[...] = total[...].astype(bf16)
        value = x2[...]
        grad = grad_ref[...].astype(f32)
        grad = grad + norm_back(value, inverse_rms(value), gain_ref[...], back[...])
        dx_ref[...] = grad
        low = grad.astype(bf16)
        low_ref[...] = low
        mixed_back_ref[...] = mm(low, out_ref[...], NT).astype(bf16)


def feed_forward(resid, mixed, all_cross, gain, grad_out, all_ffn):
    rows = resid.shape[0]
    units = FF // D

    def whole(height):
        return pl.BlockSpec((height, D), lambda j, s: (0, 0))

    rows_f32 = jax.ShapeDtypeStruct((rows, D), f32)
    rows_bf16 = jax.ShapeDtypeStruct((rows, D), bf16)
    return pl.pallas_call(
        functools.partial(feed_forward_body, rows),
        grid=(units, 2),
        in_specs=[
            whole(rows),
            whole(rows),
            pl.BlockSpec((D, D), lambda j, s: (0, 3)),
            whole(1),
            whole(rows),
            pl.BlockSpec((D, D), lambda j, s: (0, j)),
            pl.BlockSpec((D, D), lambda j, s: (0, units + j)),
        ],
        out_specs=[
            whole(rows),
            whole(rows),
            whole(rows),
            whole(rows),
            pl.BlockSpec((D, D), lambda j, s: (0, s * units + j)),
        ],
        out_shape=[
            rows_bf16,
            rows_f32,
            rows_bf16,
            rows_bf16,
            jax.ShapeDtypeStruct((D, 2 * FF), bf16),
        ],
        scratch_shapes=[
            pltpu.VMEM((rows, D), f32),
            pltpu.VMEM((rows, D), bf16),
            pltpu.VMEM((D, rows), bf16),
            pltpu.VMEM((rows, D), f32),
            pltpu.VMEM((rows, D), f32),
            pltpu.VMEM((rows, D), bf16),
        ],
        compiler_params=pltpu.CompilerParams(vmem_limit_bytes=48 << 20),
        name="feed_forward",
    )(resid, mixed, all_cross, gain[None], grad_out, all_ffn, all_ffn)


def bias_matrices():
    place = np.arange(256)
    distance = np.where(place <= 128, 128 - place, 384 - place)
    edges = np.array(bucket_edges)
    buckets = np.where(distance < 16, distance, 16 + (distance[:, None] >= edges).sum(axis=1))
    spread = np.zeros((2, 2, BUCKETS, 2, 2, 256), np.float32)
    columns = np.zeros((2, 2, BUCKETS, 128), np.float32)
    sums = np.zeros((2, 2, 128, 2, 2, BUCKETS), np.float32)
    for which in (0, 1):
        for flag in (0, 1):
            spread[which, flag, buckets, which, flag, place] += 1.0
            spread[which, flag, BUCKETS - 1, which, flag, :] -= 1.0
            base = (HDIM if which == 0 else 0) + 3 + 2 * flag
            columns[which, flag, BUCKETS - 1, base : base + 2] = 1.0
            sums[which, flag, HDIM if which == 0 else 0, which, flag, BUCKETS - 1] = 1.0
    spread = spread.reshape(128, 1024)
    forward = np.concatenate((spread, columns.reshape(128, 128)), axis=1)
    backward = np.concatenate((spread.T, sums.reshape(512, 128)), axis=0)
    return forward, backward


def bias_parts(table_low):
    by_pair = table_low.T.reshape(PAIRS, 4 * BUCKETS)
    both = mm(by_pair, jnp.asarray(bias_matrices()[0], bf16)) * LOG2E
    far = both[:, 1024:]
    high = far.astype(bf16)
    rest = (far - high.astype(f32)).astype(bf16)
    odd = lax.broadcasted_iota(jnp.int32, (1, 128), 1) % 2 == 1
    return jnp.where(odd, high, rest).reshape(PAIRS, 1, 128), both[:, :1024].reshape(PAIRS, 4, 256)


def table_gradient(near_sums, row_sums):
    both = jnp.concatenate((near_sums.reshape(PAIRS, -1), row_sums.reshape(PAIRS, -1)), axis=1)
    matrix = jnp.asarray(bias_matrices()[1], f32)
    by_pair = jnp.dot(both, matrix, precision=lax.Precision.HIGHEST, preferred_element_type=f32)
    return by_pair.reshape(HEADS, 2 * BUCKETS).T.reshape(-1)


def seq_shift(array, count):
    length = array.shape[0]
    return lax.dynamic_slice_in_dim(jnp.concatenate((array, array), axis=0), count, length, axis=0)


def others_rows(rows, own_last):
    parts = lax.axis_size("seq")
    if parts == 2:
        return lax.ppermute(rows, "seq", [(0, 1)] if own_last else [(0, 1), (1, 0)])
    whole = lax.all_gather(rows, "seq", axis=0, tiled=True)
    step = rows.shape[0]
    start = lax.rem(lax.axis_index("seq") + 1, parts) * step
    return seq_shift(whole, start)[: (parts - 1) * step]


def to_owners(grads, own_last):
    parts = lax.axis_size("seq")
    if parts == 2:
        return lax.ppermute(grads, "seq", [(1, 0)] if own_last else [(0, 1), (1, 0)])
    step = grads.shape[0] // (parts - 1)
    whole = jnp.concatenate((grads, jnp.zeros((step, grads.shape[1]), grads.dtype)), axis=0)
    start = lax.rem(parts - 1 - lax.axis_index("seq"), parts) * step
    return lax.psum_scatter(seq_shift(whole, start), "seq", scatter_dimension=0, tiled=True)


def on_device(
    decoder_in,
    encoder_out,
    dec_lengths,
    pair_flags,
    enc_segments,
    self_proj,
    self_out,
    cross_proj,
    cross_out,
    ffn_in,
    ffn_out,
    norm_gains,
    rel_table,
    out_grad,
):
    shard = self_out.shape[0]
    small = jnp.concatenate((norm_gains, rel_table[None]), axis=0).T
    block_self = jnp.concatenate(
        (self_proj[0], self_proj[1], self_proj[2], self_out, jnp.pad(small, ((0, 0), (0, 124)))),
        axis=1,
    ).astype(bf16)
    block_cross = jnp.concatenate(
        (cross_proj[0], cross_proj[1], cross_proj[2], cross_out), axis=1
    ).astype(bf16)
    own_kernels = (lax.axis_size("dp"), lax.axis_size("seq")) == (16, 2)
    if own_kernels:
        all_self, all_cross = gather_blocks(block_self, block_cross)
        all_self = all_self.reshape(-1, all_self.shape[2])
        all_cross = all_cross.reshape(-1, all_cross.shape[2])
    else:
        all_self = lax.all_gather(block_self, BOTH, axis=0, tiled=True)
        all_cross = lax.all_gather(block_cross, BOTH, axis=0, tiled=True)
    units = FF // D
    ffn_in_here = jnp.swapaxes(ffn_in.reshape(shard, D, units), 1, 2).reshape(shard, FF)
    block_ffn = jnp.concatenate((ffn_in_here, ffn_out.reshape(shard, FF)), axis=1).astype(bf16)
    block_ffn, encoder_out = lax.optimization_barrier((block_ffn, encoder_out, all_cross))[:2]
    all_ffn = lax.all_gather(block_ffn, BOTH, axis=0, tiled=True)
    self_q, self_k, self_v, out_self = (all_self[:, i * D : (i + 1) * D] for i in range(4))
    cross_q, cross_k, cross_v = (all_cross[:, i * D : (i + 1) * D] for i in range(3))
    small_all = all_self[:, 4 * D : 4 * D + 4].T
    gains = small_all[:3].astype(f32)
    far_lanes, near_lines = bias_parts(small_all[3].reshape(2 * BUCKETS, HEADS))

    tokens = decoder_in[0]
    memory = encoder_out[0]
    grad_out = out_grad[0]
    rows, enc_rows = tokens.shape[0], memory.shape[0]
    seq_count = lax.axis_size("seq")
    seq_index = lax.axis_index("seq")
    keys, enc_keys = rows * seq_count, enc_rows * seq_count

    lengths = dec_lengths[0]
    memory_one = jnp.sum((enc_segments[0] < 1).astype(jnp.int32))
    memory_two = jnp.sum((enc_segments[0] < 2).astype(jnp.int32))
    info = jnp.stack(
        (
            seq_index * rows,
            seq_index * enc_rows,
            lengths[0],
            lengths[0] + lengths[1],
            memory_one,
            memory_two,
            pair_flags[0, 0],
            pair_flags[0, 1],
        )
    ).astype(jnp.int32)
    before = others_rows(tokens, True)
    others = others_rows(memory, False)

    scale = 0.125 * LOG2E
    tokens = tokens.astype(f32)
    inverse_one = inverse_rms(tokens)
    normed_one = (tokens * inverse_one * gains[0]).astype(bf16)
    before = before.astype(f32)
    normed_before = (before * inverse_rms(before) * gains[0]).astype(bf16)
    query_one = (mm(normed_one, self_q) * scale).astype(bf16)
    kv_one = mm(normed_one, all_self[:, D : 3 * D]).astype(bf16)
    kv_before = mm(normed_before, all_self[:, D : 3 * D]).astype(bf16)
    parts_one = ((kv_before, 0, PAIRS), (kv_one, 0, PAIRS))
    mixed_one, weights_one, total_one = attend(info, rows, query_one, parts_one, far_lanes, near_lines)
    resid_one = tokens + mm(mixed_one, out_self)
    inverse_two = inverse_rms(resid_one)
    normed_two = (resid_one * inverse_two * gains[1]).astype(bf16)
    query_two = (mm(normed_two, cross_q) * scale).astype(bf16)
    kv_memory = mm(memory, all_cross[:, D : 3 * D]).astype(bf16)
    kv_others = mm(others, all_cross[:, D : 3 * D]).astype(bf16)
    parts_two = ((kv_memory, 0, PAIRS), (kv_others, 0, PAIRS))
    mixed_two, weights_two, total_two = attend(info, rows, query_two, parts_two)
    layer_out, grad_resid, grad_low_two, grad_mixed, grad_ffn = feed_forward(
        resid_one, mixed_two, all_cross, gains[2], grad_out, all_ffn
    )

    grad_query, grad_key, grad_value = attend_back(
        info, query_two, parts_two, weights_two, mixed_two, total_two, grad_mixed, False
    )
    turned = (((0,), (1,)), ((), ()))
    kv_other = mm(grad_key[:, enc_rows:], cross_k, turned)
    kv_other = (kv_other + mm(grad_value[:, enc_rows:], cross_v, turned)).astype(bf16)
    grad_memory = mm(grad_key[:, :enc_rows], cross_k, turned)
    grad_memory = grad_memory + mm(grad_value[:, :enc_rows], cross_v, turned)
    grad_two = (grad_query, grad_key, grad_value)
    grad_normed = mm(grad_query, cross_q, NT)
    grad_resid = grad_resid + norm_back(resid_one, inverse_two, gains[1], grad_normed)
    grad_low = grad_resid.astype(bf16)
    grad_mixed = mm(grad_low, out_self, NT).astype(bf16)
    grad_mixed, kv_other = lax.optimization_barrier((grad_mixed, kv_other))
    grad_query, grad_key, grad_value, near_sums, row_sums = attend_back(
        info, query_one, parts_one, weights_one, mixed_one, total_one, grad_mixed, True
    )
    grad_others = to_owners(kv_other, False)
    split = keys - rows
    grad_before = mm(grad_key[:, :split], self_k, turned) + mm(grad_value[:, :split], self_v, turned)
    grad_before = to_owners(grad_before.astype(bf16), True)
    table_grad = table_gradient(near_sums, row_sums)
    small = jnp.broadcast_to(table_grad[:, None], (D, 128)).astype(bf16)

    def owned(array):
        return lax.psum_scatter(array, BOTH, scatter_dimension=0, tiled=True).astype(f32)

    def projections(block):
        return jnp.stack([block[:, i * D : (i + 1) * D] for i in range(3)], axis=0)

    if own_kernels:
        own_self, own_self_out, own_cross, own_cross_out, own_small = scatter_products(
            (normed_before, normed_one, grad_query, grad_key, grad_value, mixed_one, grad_low),
            (normed_two, grad_two[0], memory, others, grad_two[1], grad_two[2], mixed_two, grad_low_two),
            small.reshape(-1, shard, small.shape[1]),
        )
    else:
        normed_all = jnp.concatenate((normed_before, normed_one), axis=0)
        memory_all = jnp.concatenate((memory, others), axis=0)
        self_grads = (
            mm(normed_one, grad_query, TN),
            mm(normed_all, grad_key, turned),
            mm(normed_all, grad_value, turned),
            mm(mixed_one, grad_low, TN),
        )
        cross_grads = (
            mm(normed_two, grad_two[0], TN),
            mm(memory_all, grad_two[1], turned),
            mm(memory_all, grad_two[2], turned),
            mm(mixed_two, grad_low_two, TN),
        )
        self_grads = jnp.concatenate(self_grads, axis=1).astype(bf16)
        block = owned(jnp.concatenate((self_grads, small), axis=1))
        own_self, own_self_out = projections(block), block[:, 3 * D : 4 * D]
        own_small = block[:, 4 * D :]
        block = owned(jnp.concatenate(cross_grads, axis=1).astype(bf16))
        own_cross, own_cross_out = projections(block), block[:, 3 * D :]

    arrived = lax.optimization_barrier((grad_before, grad_others, own_small))
    grad_before, grad_others, own_small = arrived
    grad_encoder = grad_memory + grad_others.astype(f32)
    grad_normed = mm(grad_key[:, split:], self_k, turned) + mm(grad_value[:, split:], self_v, turned)
    grad_normed = grad_normed + mm(grad_query, self_q, NT) + grad_before.astype(f32)
    grad_input = grad_resid + norm_back(tokens, inverse_one, gains[0], grad_normed)
    own_ffn = owned(grad_ffn)
    own_ffn_in = jnp.swapaxes(own_ffn[:, :FF].reshape(shard, units, D), 1, 2).reshape(shard, FF)
    own_ffn_out = own_ffn[:, FF:].reshape(ffn_out.shape)

    def products(weight, grad):
        return jnp.sum(weight.astype(bf16).astype(f32) * grad, axis=-1)

    gain_grads = jnp.stack(
        (
            jnp.sum(products(self_proj, own_self), axis=0),
            products(cross_proj[0], own_cross[0]),
            products(ffn_in, own_ffn_in),
        ),
        axis=0,
    )
    gain_grads = gain_grads / norm_gains.astype(bf16).astype(f32)

    return (
        layer_out[None],
        grad_input[None],
        grad_encoder[None],
        own_self,
        own_self_out,
        own_cross,
        own_cross_out,
        own_ffn_in,
        own_ffn_out,
        gain_grads,
        own_small[:, 0],
    )


def solution(mesh):
    hidden = P("dp", "seq", None)
    rows_split = P(BOTH, None)
    stacked = P(None, BOTH, None)
    stream = P("dp", None)
    return jax.shard_map(
        on_device,
        mesh=mesh,
        in_specs=(
            hidden,
            hidden,
            stream,
            stream,
            stream,
            stacked,
            rows_split,
            stacked,
            rows_split,
            rows_split,
            rows_split,
            P(None, BOTH),
            P(BOTH),
            hidden,
        ),
        out_specs=(
            hidden,
            hidden,
            hidden,
            stacked,
            rows_split,
            stacked,
            rows_split,
            rows_split,
            rows_split,
            P(None, BOTH),
            P(BOTH),
        ),
        check_vma=False,
    )
```

```python
import functools
import math

import jax
import jax.numpy as jnp
import numpy as np
from jax import lax
from jax.experimental import pallas as pl
from jax.experimental.pallas import tpu as pltpu
from jax.sharding import PartitionSpec as P

D = 768
HEADS = 12
HDIM = 64
FF = 3072
BUCKETS = 32
PAIRS = HEADS // 2
LOG2E = math.log2(math.e)
LN2 = math.log(2.0)
epsilon = 1e-06
neg_large = -1e30
bucket_edges = (19, 21, 24, 27, 31, 35, 40, 46, 52, 59, 67, 77, 87, 99, 113)
f32 = jnp.float32
bf16 = jnp.bfloat16
NT = (((1,), (1,)), ((), ()))
NN = (((1,), (0,)), ((), ()))
TN = (((0,), (0,)), ((), ()))
BOTH = ("dp", "seq")
MESH = pl.DeviceIdType.MESH


def mm(a, b, dims=NN):
    return lax.dot_general(a, b, dims, preferred_element_type=f32)


def inverse_rms(values):
    return lax.rsqrt(jnp.mean(values * values, axis=-1, keepdims=True) + epsilon)


def norm_back(values, inverse, gain, grad):
    unit = values * inverse
    grad = grad * gain
    return inverse * (grad - unit * jnp.mean(grad * unit, axis=-1, keepdims=True))


def head_lanes(which):
    low = lax.broadcasted_iota(jnp.int32, (1, 128), 1) < HDIM
    return low if which == 0 else jnp.logical_not(low)


def row_chunks(rows, keys, causal, step):
    return [
        (slice(i, i + step), (keys - rows + i + step) if causal else keys)
        for i in range(0, rows, step)
    ]


def near_bias(near_ref, which):
    row = lax.broadcasted_iota(jnp.int32, (128, 256), 0)
    column = lax.broadcasted_iota(jnp.int32, (128, 256), 1)
    tiles = []
    for flag in (0, 1):
        line = near_ref[0, 2 * which + flag : 2 * which + flag + 1, :]
        tile = pltpu.roll(jnp.broadcast_to(line, (128, 256)), 0, 1, stride=1, stride_axis=0)
        tiles.append(jnp.where(column - row > 128, neg_large, tile))
    return tiles


def diagonal_sums(tile):
    for step in (64, 32, 16, 8):
        tile = tile[:step] + pltpu.roll(tile[step:], 256 - step, 1)
    row = lax.broadcasted_iota(jnp.int32, (8, 256), 0)
    for step in (4, 2, 1):
        tile = jnp.where((row & step) != 0, pltpu.roll(tile, 256 - step, 1), tile)
    return jnp.sum(tile, axis=0, keepdims=True)


def pairs_between(place, end_one, end_two):
    return (place >= end_one).astype(jnp.int32) + (place >= end_two).astype(jnp.int32)


def decoder_pairs(lengths, place):
    return pairs_between(place, lengths[0, 0], lengths[0, 0] + lengths[0, 1])


def flagged(numbers, rows, first, count, width):
    lengths, flags = numbers
    place = lax.broadcasted_iota(jnp.int32, (count, width), 0)
    pair = decoder_pairs(lengths, place + (lax.axis_index("seq") * rows + first))
    return jnp.where(pair == 0, flags[0, 0], jnp.where(pair == 1, flags[0, 1], 0)) > 0


def extra_columns(numbers, rows, keys, segments, query_extra, key_extra):
    lengths = numbers[0]
    here = lax.axis_index("seq") * rows
    lane = lax.broadcasted_iota(jnp.int32, (rows, 128), 1) & (HDIM - 1)
    pair = decoder_pairs(lengths, lax.broadcasted_iota(jnp.int32, (rows, 128), 0) + here)
    flag = flagged(numbers, rows, 0, rows, 128).astype(jnp.int32)
    wanted = jnp.where(lane < 3, pair, (flag << 1) + 3)
    chosen = jnp.where(lane < 3, lane, ((lane - 3) & ~1) + 3)
    fits = jnp.logical_and(wanted == chosen, lane < 7)
    query_extra[...] = jnp.where(fits, 1.0, 0.0).astype(bf16)
    lane = lax.broadcasted_iota(jnp.int32, (keys, 128), 1) & (HDIM - 1)
    place = lax.broadcasted_iota(jnp.int32, (keys, 128), 0)
    if segments is None:
        place = place + (here + rows - keys)
        pair = jnp.where(place < 0, 3, decoder_pairs(lengths, place))
    else:
        place = place + lax.axis_index("seq") * (keys // lax.axis_size("seq"))
        place = jnp.where(place >= keys, place - keys, place)

        def below(pair):
            count = jnp.sum((segments[...] < pair).astype(f32), axis=0, keepdims=True)
            return jnp.sum(count, axis=1, keepdims=True).astype(jnp.int32)

        pair = pairs_between(place, below(1), below(2))
    wrong = jnp.logical_and(pair != lane, lane < 3)
    key_extra[...] = jnp.where(wrong, neg_large, 0.0).astype(bf16)


def attend_body(rows, keys, causal, step, parts, *refs):
    numbers, q_ref = refs[:2], refs[2]
    key_refs, value_refs = refs[3 : 3 + parts], refs[3 + parts : 3 + 2 * parts]
    o_ref, e_ref, inv_ref, query_extra, key_extra = refs[-5:]

    @pl.when(pl.program_id(0) == 0)
    def _():
        segments = None if causal else refs[3 + 2 * parts]
        extra_columns(numbers, rows, keys, segments, query_extra, key_extra)

    extra = key_extra[...]
    if causal:
        far_ref, near_ref = refs[3 + 2 * parts : 5 + 2 * parts]
        extra = extra + far_ref[0]
    key_pair = jnp.concatenate([ref[...] for ref in key_refs], axis=0)
    value_pair = jnp.concatenate([ref[...] for ref in value_refs], axis=0)
    chunks = row_chunks(rows, keys, causal, step)
    found = []
    for which in (0, 1):
        mine = head_lanes(which)
        key_head = jnp.where(mine, key_pair, extra)
        value_head = jnp.where(mine, value_pair, jnp.ones_like(value_pair))
        if causal:
            tile_zero, tile_one = near_bias(near_ref, which)
        done = []
        for here, width in chunks:
            query = jnp.where(mine, q_ref[here], query_extra[here])
            scores = mm(query, key_head[:width], NT)
            if causal:
                cut = width - 256
                flag = flagged(numbers, rows, here.start, step, 1)
                near = scores[:, cut:] + jnp.where(flag, tile_one, tile_zero)
                far = scores[:, :cut]
                peak = jnp.maximum(
                    jnp.max(far, axis=1, keepdims=True), jnp.max(near, axis=1, keepdims=True)
                )
                near = jnp.exp2(near - peak).astype(bf16)
                far = jnp.exp2(far - peak).astype(bf16)
                e_ref[which, here, :cut] = far
                e_ref[which, here, cut:width] = near
                mixed = mm(far, value_head[:cut]) + mm(near, value_head[cut:width])
            else:
                peak = jnp.max(scores, axis=1, keepdims=True)
                weights = jnp.exp2(scores - peak).astype(bf16)
                e_ref[which, here, :] = weights
                mixed = mm(weights, value_head)
            total = mixed[:, HDIM : HDIM + 1] if which == 0 else mixed[:, 0:1]
            inverse = 1.0 / total
            done.append((mixed * inverse, jnp.broadcast_to(inverse, mixed.shape)))
        found.append(done)
    low = head_lanes(0)
    for index, (here, _) in enumerate(chunks):
        o_ref[here] = jnp.where(low, found[0][index][0], found[1][index][0]).astype(bf16)
        inv_ref[here] = jnp.where(low, found[0][index][1], found[1][index][1])


def pair_columns(rows, first=0):
    return pl.BlockSpec((rows, 128), lambda p: (0, first + p))


def operands_of(numbers, query, parts):
    arrays = [*numbers, query] + [part[0] for part in parts] * 2
    specs = [pl.BlockSpec(memory_space=pltpu.SMEM)] * 2 + [pair_columns(query.shape[0])]
    for place in (1, 2):
        specs += [pair_columns(part[0].shape[0], part[place]) for part in parts]
    return arrays, specs


def per_pair(height, width):
    return pl.BlockSpec((1, height, width), lambda p: (p, 0, 0))


def attend(numbers, rows, query, parts, segments=None, far=None, near=None):
    keys = sum(part[0].shape[0] for part in parts)
    causal = far is not None
    step = 128 if causal else min(256, rows)
    operands, specs = operands_of(numbers, query, parts)
    if causal:
        operands += [far, near]
        specs += [per_pair(1, 128), per_pair(4, 256)]
    else:
        operands.append(segments)
        specs.append(pl.BlockSpec(segments.shape, lambda p: (0, 0)))
    return pl.pallas_call(
        functools.partial(attend_body, rows, keys, causal, step, len(parts)),
        grid=(PAIRS,),
        in_specs=specs,
        out_specs=(
            pair_columns(rows),
            pl.BlockSpec((2, rows, keys), lambda p: (p, 0, 0)),
            pair_columns(rows),
        ),
        out_shape=(
            jax.ShapeDtypeStruct((rows, D), bf16),
            jax.ShapeDtypeStruct((HEADS, rows, keys), bf16),
            jax.ShapeDtypeStruct((rows, D), f32),
        ),
        scratch_shapes=[pltpu.VMEM((rows, 128), bf16), pltpu.VMEM((keys, 128), bf16)],
        compiler_params=pltpu.CompilerParams(vmem_limit_bytes=56 << 20),
        name="attend_causal" if causal else "attend_cross",
    )(*operands)


def attend_back_body(rows, keys, causal, step, parts, *refs):
    numbers, q_ref = refs[:2], refs[2]
    refs = refs[3:]
    key_refs, value_refs = refs[:parts], refs[parts : 2 * parts]
    e_ref, o_ref, inv_ref, d_ref = refs[2 * parts : 4 + 2 * parts]
    if causal:
        dq_ref, dk_ref, dv_ref, near_ref, sum_ref, ds_ref = refs[4 + 2 * parts :]
    else:
        dq_ref, dk_ref, dv_ref, ds_ref = refs[4 + 2 * parts :]
    lane = lax.broadcasted_iota(jnp.int32, (1, 128), 1)
    key_pair = jnp.concatenate([ref[...] for ref in key_refs], axis=0)
    value_pair = jnp.concatenate([ref[...] for ref in value_refs], axis=0)
    scaled = (d_ref[...].astype(f32) * inv_ref[...]).astype(bf16)
    product = scaled.astype(f32) * o_ref[...].astype(f32)
    scaled_t = scaled.T
    query_t = q_ref[...].T
    chunks = row_chunks(rows, keys, causal, step)
    query_parts = []
    for which in (0, 1):
        mine = head_lanes(which)
        base = HDIM if which == 0 else 0
        value_head = jnp.where(mine, value_pair, jnp.ones_like(value_pair))
        key_head = jnp.where(mine, key_pair, jnp.ones_like(key_pair))
        delta = jnp.sum(jnp.where(mine, product, 0.0), axis=1, keepdims=True)
        high = delta.astype(bf16)
        rest = (delta - high.astype(f32)).astype(bf16)
        extra = jnp.where(
            lane == base, -high, jnp.where(lane == base + 1, -rest, jnp.zeros_like(rest))
        )
        grad_head = jnp.where(mine, scaled, extra)
        done = []
        if causal:
            near_all = jnp.zeros((128, 256), f32)
            near_one = jnp.zeros((128, 256), f32)
        for here, width in chunks:
            centred = mm(grad_head[here], value_head[:width], NT)
            grad_scores = e_ref[which, here, :width].astype(f32) * centred
            if causal:
                near = grad_scores[:, width - 256 :]
                near_all = near_all + near
                flag = flagged(numbers, rows, here.start, step, 1)
                near_one = near_one + jnp.where(flag, near, 0.0)
            grad_scores = grad_scores.astype(bf16)
            ds_ref[here, :width] = grad_scores
            done.append(mm(grad_scores, key_head[:width]))
        query_parts.append(done)
        half = slice(HDIM * which, HDIM * which + HDIM)
        if causal:
            spans = [(slice(0, keys - rows), 0)] if keys > rows else []
            spans += [
                (slice(keys - rows + i, keys - rows + i + step), i) for i in range(0, rows, step)
            ]
        else:
            spans = [(slice(0, keys), 0)]
        for span, first in spans:
            grad_key = mm(query_t[half, first:], ds_ref[first:, span])
            dk_ref[half, span] = (grad_key * LN2).astype(dk_ref.dtype)
            grad_value = mm(scaled_t[half, first:], e_ref[which, first:, span])
            dv_ref[half, span] = grad_value.astype(dv_ref.dtype)
        if causal:
            for flag, tile in ((0, near_all - near_one), (1, near_one)):
                near_ref[0, 2 * which + flag : 2 * which + flag + 1, :] = diagonal_sums(tile)
    low = head_lanes(0)
    for index, (here, _) in enumerate(chunks):
        both = jnp.where(low, query_parts[0][index], query_parts[1][index])
        dq_ref[here] = (both * 0.125).astype(dq_ref.dtype)
    if causal:
        flags = flagged(numbers, rows, 0, rows, 1)
        for which in (0, 1):
            whole = jnp.concatenate(query_parts[which], axis=0)
            one = jnp.sum(jnp.where(flags, whole, 0.0), axis=0, keepdims=True)
            every = jnp.sum(whole, axis=0, keepdims=True)
            sum_ref[0, 2 * which : 2 * which + 1, :] = every - one
            sum_ref[0, 2 * which + 1 : 2 * which + 2, :] = one


def attend_back(numbers, query, parts, weights, mixed, inverse, grad_mixed, causal):
    rows, keys = weights.shape[1:]
    step = 128 if causal else min(256, rows)
    operands, specs = operands_of(numbers, query, parts)
    operands += [weights, mixed, inverse, grad_mixed]
    specs += [pl.BlockSpec((2, rows, keys), lambda p: (p, 0, 0))] + [pair_columns(rows)] * 3
    turned = jax.ShapeDtypeStruct((D, keys), bf16)
    turned_spec = pl.BlockSpec((128, keys), lambda p: (p, 0))
    shapes = [jax.ShapeDtypeStruct((rows, D), bf16), turned, turned]
    out_specs = [pair_columns(rows), turned_spec, turned_spec]
    if causal:
        shapes += [
            jax.ShapeDtypeStruct((PAIRS, 4, 256), f32),
            jax.ShapeDtypeStruct((PAIRS, 4, 128), f32),
        ]
        out_specs += [per_pair(4, 256), per_pair(4, 128)]
    return pl.pallas_call(
        functools.partial(attend_back_body, rows, keys, causal, step, len(parts)),
        grid=(PAIRS,),
        in_specs=specs,
        out_specs=tuple(out_specs),
        out_shape=tuple(shapes),
        scratch_shapes=[pltpu.VMEM((rows, keys), bf16)],
        compiler_params=pltpu.CompilerParams(vmem_limit_bytes=56 << 20),
        name="attend_causal_back" if causal else "attend_cross_back",
    )(*operands)


def place_here():
    index = lax.axis_index("dp")
    return index // 4, (index // 2) % 2, index % 2, lax.axis_index("seq")


def block_of(z, x, core, y):
    return ((z * 2 + x) * 2 + core) * 2 + y


def device_of(z, x, core, y):
    return ((z * 2 + x) * 2 + core, y)


def greet_neighbours(z, x, core, y):
    barrier = pltpu.get_barrier_semaphore()

    def greet(device):
        pl.semaphore_signal(barrier, inc=1, device_id=device, device_id_type=MESH)

    greet(device_of(z, x, 1 - core, y))
    greet(device_of(z, 1 - x, core, y))
    greet(device_of(z, x, core, 1 - y))

    @pl.when(z > 0)
    def _():
        greet(device_of(z - 1, x, core, y))

    @pl.when(z < 3)
    def _():
        greet(device_of(z + 1, x, core, y))

    pl.semaphore_wait(barrier, 4 + ((z + 1) // 2) % 2)


def unit_order():
    place = np.arange(512)
    return (place[:, None] == (place % 128) * 4 + place // 128).astype(np.float32)


def gather_body(*refs):
    masters, refs = refs[:9], refs[9:]
    wholes, pair_whole = refs[:2], refs[2]
    sources, pair_source = refs[3:5], refs[5]
    own_sems, up_sems, down_sems, side_sems, turn_sems, mate_sems, recv_sems, pair_sems = refs[6:]
    self_proj, self_out, cross_proj, cross_out, ffn_in, ffn_out, norm_gains, table, order = masters
    count = 2
    shard = self_out.shape[0]
    for stacked, single, source in ((self_proj, self_out, sources[0]), (cross_proj, cross_out, sources[1])):
        for j in range(3):
            source[:, j * D : (j + 1) * D] = stacked[j].astype(bf16)
        source[:, 3 * D : 4 * D] = single[...].astype(bf16)
    lane = lax.broadcasted_iota(jnp.int32, (shard, 128), 1)
    row = lax.broadcasted_iota(jnp.int32, (shard, shard), 0)
    same = row == lax.broadcasted_iota(jnp.int32, (shard, shard), 1)
    small = jnp.zeros((shard, 128), f32)
    for j in range(4):
        line = norm_gains[j : j + 1] if j < 3 else table[...]
        column = jnp.sum(jnp.where(same, jnp.broadcast_to(line, same.shape), 0.0), axis=1, keepdims=True)
        small = jnp.where(lane == j, column, small)
    sources[0][:, 4 * D :] = small.astype(bf16)
    z, x, core, y = place_here()
    mate = device_of(z, x, 1 - core, y)
    me = block_of(z, x, core, y)
    greet_neighbours(z, x, core, y)

    def near(which, side, turn):
        return ((x + side) % 2, (y + turn) % 2) if which == 0 else ((x + turn) % 2, (y + side) % 2)

    def send(which, source, block, send_sem, device):
        return pltpu.make_async_remote_copy(
            src_ref=source,
            dst_ref=wholes[which].at[block],
            send_sem=send_sem,
            recv_sem=recv_sems.at[which, block],
            device_id=device,
            device_id_type=MESH,
        )

    def copies(which, far, up, side, turn, source=None):
        at_z = z + far if up else z - far
        bx, by = near(which, side, turn)
        block = block_of(at_z, bx, core, by)
        source = wholes[which].at[block] if source is None else source
        slot = (2 * far + (1 if up else 0)) if far else 0
        slot = max(slot - 1, 0)
        out = [(None, send(which, source, block, mate_sems.at[which, (side * 2 + turn) * 7 + slot], mate))]
        if turn == 0:
            tx, ty = near(which, 0, 1)
            out.append(
                (None, send(which, source, block, turn_sems.at[which, side * 7 + slot], device_of(z, tx, core, ty)))
            )
            if side == 0:
                sx, sy = near(which, 1, 0)
                out.append((None, send(which, source, block, side_sems.at[which, slot], device_of(z, sx, core, sy))))
                if far == 0 or not up:
                    out.append(
                        (z < 3, send(which, source, block, up_sems.at[which, far], device_of(z + 1, x, core, y)))
                    )
                if far == 0 or up:
                    out.append(
                        (z > 0, send(which, source, block, down_sems.at[which, far], device_of(z - 1, x, core, y)))
                    )
        return block, out

    def when(condition, action):
        if condition is None:
            action()
        else:
            pl.when(condition)(action)

    def exists(far, up):
        if far == 0:
            return None
        return z + far < 4 if up else z - far >= 0

    def onwards(which, far, up, side, turn, source=None):
        def run():
            block, out = copies(which, far, up, side, turn, source)
            if source is None:
                pltpu.make_async_copy(wholes[which].at[block], wholes[which].at[block], recv_sems.at[which, block]).wait()
            for condition, copy in reversed(out):
                when(condition, copy.start)

        when(exists(far, up), run)

    own = [
        pltpu.make_async_copy(sources[i], wholes[i].at[me], own_sems.at[i]) for i in range(count)
    ]
    own.append(pltpu.make_async_copy(pair_source, pair_whole.at[y], pair_sems.at[0]))
    pair = pltpu.make_async_remote_copy(
        src_ref=pair_source,
        dst_ref=pair_whole.at[y],
        send_sem=pair_sems.at[1],
        recv_sem=pair_sems.at[2],
        device_id=device_of(z, x, core, 1 - y),
        device_id_type=MESH,
    )
    for which in range(count):
        onwards(which, 0, True, 0, 0, sources[which])
    for copy in own[:count]:
        copy.start()
    units = FF // D
    for m in range(FF // 512):
        piece = mm(ffn_in[:, 512 * m : 512 * (m + 1)].astype(bf16), order[...]).astype(bf16)
        for b in range(units):
            first = b * D + 128 * m
            pair_source[:, first : first + 128] = piece[:, 128 * b : 128 * (b + 1)]
    row = lax.broadcasted_iota(jnp.int32, (shard, units * shard), 0) * units
    place = lax.broadcasted_iota(jnp.int32, (shard, units * shard), 1)
    held = ffn_out[...].astype(bf16)
    for b in range(units):
        rows = mm(jnp.where(row + b == place, 1.0, 0.0).astype(bf16), held)
        pair_source[:, FF + b * D : FF + (b + 1) * D] = rows.astype(bf16)
    own[count].start()
    pair.start()
    waves = [[] for _ in range(6)]
    for side in (0, 1):
        for turn in (0, 1):
            for far in range(4):
                for up in (False, True):
                    if far == 0 and (up or (side == 0 and turn == 0)):
                        continue
                    waves[far + side + turn].append((far, up, side, turn))
    for wave in waves:
        for far, up, side, turn in wave:
            for which in range(count):
                onwards(which, far, up, side, turn)
    for side in (0, 1):
        for turn in (0, 1):
            for far in range(4):
                for up in (False, True):
                    if far == 0 and up:
                        continue
                    for which in range(count):

                        def finish(which=which, far=far, up=up, side=side, turn=turn):
                            at_z = z + far if up else z - far
                            bx, by = near(which, side, turn)
                            block = block_of(at_z, bx, 1 - core, by)
                            whole = wholes[which].at[block]
                            pltpu.make_async_copy(whole, whole, recv_sems.at[which, block]).wait()
                            source = sources[which] if (far, side, turn) == (0, 0, 0) else None
                            _, out = copies(which, far, up, side, turn, source)
                            for condition, copy in out:
                                when(condition, copy.wait_send)

                        when(exists(far, up), finish)
    for copy in own:
        copy.wait()
    pair.wait_send()
    came = pair_whole.at[1 - y]
    pltpu.make_async_copy(came, came, pair_sems.at[2]).wait()


def gather_blocks(self_proj, self_out, cross_proj, cross_out, ffn_in, ffn_out, norm_gains, rel_table):
    shard = self_out.shape[0]
    shapes = [(shard, 4 * D + 128), (shard, 4 * D)]
    pair = (shard, 2 * FF)
    dma = pltpu.SemaphoreType.DMA
    return pl.pallas_call(
        gather_body,
        in_specs=[pl.BlockSpec(memory_space=pltpu.VMEM)] * 9,
        out_specs=[pl.BlockSpec(memory_space=pl.ANY)] * 3,
        out_shape=[jax.ShapeDtypeStruct((32, *shape), bf16) for shape in shapes]
        + [jax.ShapeDtypeStruct((2, *pair), bf16)],
        scratch_shapes=[pltpu.VMEM(shape, bf16) for shape in (*shapes, pair)]
        + [dma((3,))]
        + [dma((2, n)) for n in (4, 4, 7, 14, 28, 32)]
        + [dma((3,))],
        compiler_params=pltpu.CompilerParams(collective_id=0, has_side_effects=True),
        name="gather_blocks",
    )(
        self_proj,
        self_out,
        cross_proj,
        cross_out,
        ffn_in,
        ffn_out,
        norm_gains,
        rel_table[None],
        jnp.asarray(unit_order(), bf16),
    )


SELF_PRODUCTS = (((1,), 2, False), ((0, 1), 3, True), ((0, 1), 4, True), ((5,), 6, False))
CROSS_PRODUCTS = (((0,), 1, False), ((2, 3), 4, True), ((2, 3), 5, True), ((6,), 7, False))


def scatter_body(counts, *refs):
    total_in = sum(counts)
    arrays, small = refs[:total_in], refs[total_in]
    weights_ref, tokens_ref, resid_ref, gain_ref = refs[total_in + 1 : total_in + 5]
    refs = refs[total_in + 5 :]
    outs, grad_ref, refs = refs[:5], refs[5], refs[6:]
    held, small_held = refs[:total_in], refs[total_in]
    refs = refs[total_in + 1 :]
    parts, mate_in, first_in, second_in, line_in = (refs[2 * i : 2 * i + 2] for i in range(5))
    load_sems, mate_sems, first_sems, second_sems, line_sems = refs[10:15]
    mate_recv, first_recv, second_recv, line_recv = refs[15:19]
    back_in, back_sems, late_sems = refs[19:]
    z, x, core, y = place_here()
    loads = [
        pltpu.make_async_copy(source, target, load_sems.at[i])
        for i, (source, target) in enumerate(zip((*arrays, small), (*held, small_held)))
    ]
    for load in loads:
        load.start()
    greet_neighbours(z, x, core, y)
    half = z // 2
    order = (3 - 3 * half, 2 - half, 1 - z + 4 * half, z)

    def near(which, first, second):
        if which == 0:
            return (x + first) % 2, (y + second) % 2
        return (x + second) % 2, (y + first) % 2

    def block(which, i, first, second, other_core=0):
        bx, by = near(which, first, second)
        return block_of(order[i], bx, (core + other_core) % 2, by)

    def slot_of(which, i, first, second):
        bx, by = near(which, first, second)
        return (order[i] * 2 + bx) * 2 + by

    def remote(source, target, send_sem, recv_sem, device):
        return pltpu.make_async_remote_copy(
            src_ref=source,
            dst_ref=target,
            send_sem=send_sem,
            recv_sem=recv_sem,
            device_id=device,
            device_id_type=MESH,
        )

    def to_mate(which, i, first, second):
        slot = slot_of(which, i, first, second)
        return remote(
            parts[which].at[block(which, i, first, second, 1)],
            mate_in[which].at[slot],
            mate_sems.at[which, slot],
            mate_recv.at[which, slot],
            device_of(z, x, 1 - core, y),
        )

    def to_first(which, i, second):
        bx, by = near(which, 1, 0)
        return remote(
            parts[which].at[block(which, i, 1, second)],
            first_in[which].at[2 * i + second],
            first_sems.at[which, 2 * i + second],
            first_recv.at[which, 2 * i + second],
            device_of(z, bx, core, by),
        )

    def to_second(which, i):
        bx, by = near(which, 0, 1)
        return remote(
            parts[which].at[block(which, i, 0, 1)],
            second_in[which].at[i],
            second_sems.at[which, i],
            second_recv.at[which, i],
            device_of(z, bx, core, by),
        )

    def line_slot(which, came, at_z, second):
        return (came * 4 + at_z) * 2 + second if which == 0 else came * 4 + at_z

    def along_line(which, i, second=0):
        step = 1 - 2 * half if i < 2 else 1 - 2 * (z % 2)
        came = (1 - step) // 2
        slot = line_slot(which, came, order[i], second)
        return slot, remote(
            parts[which].at[block(which, i, 0, second)],
            line_in[which].at[slot],
            line_sems.at[which, 2 * i + second],
            line_recv.at[which, slot],
            device_of(z + step, x, core, y),
        )

    def arrived(buffer, sem):
        pltpu.make_async_copy(buffer, buffer, sem).wait()

    def wide(ref, index):
        return ref[index].astype(f32)

    every = [(1, 1), (1, 0), (0, 1), (0, 0)]

    def products(which, i):
        first = 0 if which == 0 else counts[0]
        height = 8 * parts[which].shape[1]
        odd = order[i] % 2
        window = pl.ds(pl.multiple_of(order[i] * height - odd * 64, 128), height + 64)
        blocks = pl.ds(order[i] * 8, 8)
        taken = {}
        for column, (lefts, right, turned) in enumerate(SELF_PRODUCTS if which == 0 else CROSS_PRODUCTS):
            if i == 0:
                for needed in (*lefts, right):
                    if needed in waiting[which]:
                        waiting[which].remove(needed)
                        loads[first + needed].wait()
            for left in lefts:
                if left not in taken:
                    rows = held[first + left][:, window].T
                    taken[left] = jnp.where(odd > 0, rows[64:], rows[:height])
            other = held[first + right][...]
            value = mm(jnp.concatenate([taken[left] for left in lefts], axis=1), other, NT if turned else NN)
            value = value.reshape(8, height // 8, value.shape[1]).astype(bf16)
            parts[which][blocks, :, column * D : (column + 1) * D] = value
        if which == 0:
            if i == 0:
                loads[-1].wait()
            parts[0][blocks, :, 4 * D :] = small_held[blocks]

    waiting = [set(range(counts[0])), set(range(counts[1]))]

    def make(i):
        for which in (1, 0):
            products(which, i)
            for first, second in every:
                to_mate(which, i, first, second).start()

    def chip_sum(which, i, first, second):
        here = block(which, i, first, second)
        slot = slot_of(which, i, first, second)
        arrived(mate_in[which].at[slot], mate_recv.at[which, slot])
        return here, wide(parts[which], here) + wide(mate_in[which], slot)

    def send_first(i):
        for second in (1, 0):
            for which in (1, 0):
                here, total = chip_sum(which, i, 1, second)
                parts[which][here] = total.astype(bf16)
                to_first(which, i, second).start()

    middle = (z + 1) // 2 == 1

    def after_first(which, i, second):
        here, total = chip_sum(which, i, 0, second)
        arrived(first_in[which].at[2 * i + second], first_recv.at[which, 2 * i + second])
        return here, total + wide(first_in[which], 2 * i + second)

    def send_second(i):
        here, total = after_first(1, i, 1)
        parts[1][here] = total.astype(bf16)
        to_second(1, i).start()

    def send_line(which, i, second, here, total):
        parts[which][here] = total.astype(bf16)
        slot, copy = along_line(which, i, second)

        @pl.when(middle)
        def _():
            arrived(line_in[which].at[slot], line_recv.at[which, slot])
            total = wide(parts[which], here) + wide(line_in[which], slot)
            parts[which][here] = total.astype(bf16)

        copy.start()

    def line_self(i):
        for second in (1, 0):
            send_line(0, i, second, *after_first(0, i, second))

    def line_cross(i):
        here, total = after_first(1, i, 0)
        arrived(second_in[1].at[i], second_recv.at[1, i])
        total = total + wide(second_in[1], i)
        if i < 3:
            send_line(1, i, 0, here, total)
        else:
            put(1, total, False)

    def from_line(which, second, add):
        for came, there in ((0, z > 0), (1, z < 3)):
            slot = line_slot(which, came, z, second)

            @pl.when(there)
            def _():
                arrived(line_in[which].at[slot], line_recv.at[which, slot])
                add(wide(line_in[which], slot))

    def last_self():
        here, total = after_first(0, 3, 1)
        parts[0][here] = total.astype(bf16)

        def add(value):
            parts[0][here] = (wide(parts[0], here) + value).astype(bf16)

        from_line(0, 1, add)
        to_second(0, 3).start()
        put(0, after_first(0, 3, 0)[1], False)
        from_line(0, 0, lambda value: put(0, value, True))

    def put(which, value, add):
        stacked, single = outs[2 * which : 2 * which + 2]
        targets = [(stacked.at[j], j) for j in range(3)] + [(single, 3)]
        for target, j in targets:
            piece = value[:, j * D : (j + 1) * D]
            target[...] = target[...] + piece if add else piece
        if which == 0:
            piece = value[:, 4 * D :]
            outs[4][...] = outs[4][...] + piece if add else piece


    split = arrays[0].shape[0]
    cross = held[counts[0] :]
    weights_kv, weights_q = cross[4].at[:, : 2 * D], cross[5].at[:, :D]
    rows_held, back_out = cross[0], cross[1]
    late = (
        pltpu.make_async_copy(weights_ref.at[:, D : 3 * D], weights_kv, late_sems.at[0]),
        pltpu.make_async_copy(weights_ref.at[:, :D], weights_q, late_sems.at[1]),
        pltpu.make_async_copy(tokens_ref, rows_held, late_sems.at[2]),
        pltpu.make_async_copy(resid_ref, grad_ref, late_sems.at[3]),
    )
    back = remote(
        back_out, back_in, back_sems.at[0], back_sems.at[1], device_of(z, x, core, 0)
    )

    def key_value_rows(columns):
        value = mm(held[3][:, columns].T, weights_kv[:, :D], NT)
        return value + mm(held[4][:, columns].T, weights_kv[:, D:], NT)

    def rows_before():
        late[0].wait()
        back_out[...] = key_value_rows(slice(0, split)).astype(bf16)

        @pl.when(y == 1)
        def _():
            back.start()

    def rows_here():
        late[1].wait()
        late[2].wait()
        late[3].wait()
        grad = key_value_rows(slice(split, 2 * split)) + mm(held[2][...], weights_q[...], NT)
        add_rows(grad)

    def add_rows(grad):
        value = rows_held[...].astype(f32)
        grad_ref[...] += norm_back(value, inverse_rms(value), gain_ref[...], grad)

    def rows_back():
        @pl.when(y == 0)
        def _():
            arrived(back_in, back_sems.at[1])
            add_rows(back_in[...].astype(f32))

        @pl.when(y == 1)
        def _():
            back.wait_send()

    make(0)
    make(1)
    send_first(0)
    make(2)
    send_first(1)
    send_second(0)
    line_self(0)
    make(3)
    for copy in late:
        copy.start()
    send_first(2)
    send_second(1)
    line_self(1)
    line_cross(0)
    send_first(3)
    rows_before()
    send_second(2)
    line_self(2)
    line_cross(1)
    send_second(3)
    line_cross(2)
    rows_here()
    last_self()
    line_cross(3)
    from_line(1, 0, lambda value: put(1, value, True))
    arrived(second_in[0].at[3], second_recv.at[0, 3])
    put(0, wide(second_in[0], 3), True)
    rows_back()

    for which in (0, 1):
        for i in range(4):
            for first, second in every:
                to_mate(which, i, first, second).wait_send()
            for second in (0, 1):
                to_first(which, i, second).wait_send()
            if which == 1 or i == 3:
                to_second(which, i).wait_send()
            if i < 3:
                for second in (0, 1)[: 2 - which]:
                    along_line(which, i, second)[1].wait_send()


def scatter_products(self_arrays, cross_arrays, small, weights, tokens, resid, gain):
    counts = (len(self_arrays), len(cross_arrays))
    arrays = (*self_arrays, *cross_arrays)
    shard = small.shape[1]
    shapes = [(shard, 4 * D + small.shape[2]), (shard, 4 * D)]
    dma = pltpu.SemaphoreType.DMA

    def buffers(slots):
        return [pltpu.VMEM((slots, *shape), bf16) for shape in shapes]

    return pl.pallas_call(
        functools.partial(scatter_body, counts),
        in_specs=[pl.BlockSpec(memory_space=pl.ANY)] * (len(arrays) + 4)
        + [pl.BlockSpec(memory_space=pltpu.VMEM)],
        out_specs=[pl.BlockSpec(memory_space=pltpu.VMEM)] * 6,
        out_shape=[
            jax.ShapeDtypeStruct(shape, f32)
            for shape in ((3, shard, D), (shard, D), (3, shard, D), (shard, D), (shard, small.shape[2]), resid.shape)
        ],
        scratch_shapes=[pltpu.VMEM(array.shape, array.dtype) for array in (*arrays, small)]
        + buffers(32)
        + buffers(16)
        + buffers(8)
        + buffers(4)
        + [pltpu.VMEM((16 - 8 * i, *shape), bf16) for i, shape in enumerate(shapes)]
        + [
            dma((len(arrays) + 1,)),
            dma((2, 16)),
            dma((2, 8)),
            dma((2, 4)),
            dma((2, 6)),
            dma((2, 16)),
            dma((2, 8)),
            dma((2, 4)),
            dma((2, 16)),
            pltpu.VMEM(tokens.shape, bf16),
            dma((2,)),
            dma((4,)),
        ],
        compiler_params=pltpu.CompilerParams(
            collective_id=1, has_side_effects=True, vmem_limit_bytes=60 << 20
        ),
        name="scatter_products",
    )(*arrays, small, weights, tokens, resid, gain)


def gelu_and_slope(value):
    upper = 0.5 * (1.0 + lax.erf(value * math.sqrt(0.5)))
    density = jnp.exp(-0.5 * value * value) * (1.0 / math.sqrt(2.0 * math.pi))
    return value * upper, upper + value * density


def feed_forward_body(rows, *refs):
    x1_ref, mixed_ref, out_ref, gain_ref, grad_ref, in_ref, back_ref = refs[:7]
    layer_ref, dx_ref, low_ref, mixed_back_ref, weight_ref = refs[7:12]
    x2, h3, h3_t, total, back, act = refs[12:]
    step, part = pl.program_id(0), pl.program_id(1)
    first = jnp.logical_and(step == 0, part == 0)
    last = jnp.logical_and(step == pl.num_programs(0) - 1, part == 1)

    @pl.when(first)
    def _():
        value = x1_ref[...] + mm(mixed_ref[...], out_ref[...])
        x2[...] = value
        normed = (value * inverse_rms(value) * gain_ref[...]).astype(bf16)
        h3[...] = normed
        h3_t[...] = normed.T
        total[...] = value
        back[...] = jnp.zeros_like(back)

    @pl.when(part == 0)
    def _():
        hidden, slope = gelu_and_slope(mm(h3[...], in_ref[...]))
        hidden = hidden.astype(bf16)
        act[...] = hidden
        total[...] += mm(hidden, back_ref[...])
        grad_pre = (slope * mm(grad_ref[...], back_ref[...], NT)).astype(bf16)
        back[...] += mm(grad_pre, in_ref[...], NT)
        weight_ref[...] = mm(h3_t[...], grad_pre).astype(bf16)

    @pl.when(part == 1)
    def _():
        weight_ref[...] = mm(act[...].T, grad_ref[...]).astype(bf16)

    @pl.when(last)
    def _():
        layer_ref[...] = total[...].astype(bf16)
        value = x2[...]
        grad = grad_ref[...].astype(f32)
        grad = grad + norm_back(value, inverse_rms(value), gain_ref[...], back[...])
        dx_ref[...] = grad
        low = grad.astype(bf16)
        low_ref[...] = low
        mixed_back_ref[...] = mm(low, out_ref[...], NT).astype(bf16)


def feed_forward(resid, mixed, all_cross, gain, grad_out, all_ffn):
    rows = resid.shape[0]
    units = FF // D

    def whole(height):
        return pl.BlockSpec((height, D), lambda j, s: (0, 0))

    rows_f32 = jax.ShapeDtypeStruct((rows, D), f32)
    rows_bf16 = jax.ShapeDtypeStruct((rows, D), bf16)
    return pl.pallas_call(
        functools.partial(feed_forward_body, rows),
        grid=(units, 2),
        in_specs=[
            whole(rows),
            whole(rows),
            pl.BlockSpec((D, D), lambda j, s: (0, 3)),
            whole(1),
            whole(rows),
            pl.BlockSpec((D, D), lambda j, s: (0, j)),
            pl.BlockSpec((D, D), lambda j, s: (0, units + j)),
        ],
        out_specs=[
            whole(rows),
            whole(rows),
            whole(rows),
            whole(rows),
            pl.BlockSpec((D, D), lambda j, s: (0, s * units + j)),
        ],
        out_shape=[
            rows_bf16,
            rows_f32,
            rows_bf16,
            rows_bf16,
            jax.ShapeDtypeStruct((D, 2 * FF), bf16),
        ],
        scratch_shapes=[
            pltpu.VMEM((rows, D), f32),
            pltpu.VMEM((rows, D), bf16),
            pltpu.VMEM((D, rows), bf16),
            pltpu.VMEM((rows, D), f32),
            pltpu.VMEM((rows, D), f32),
            pltpu.VMEM((rows, D), bf16),
        ],
        compiler_params=pltpu.CompilerParams(vmem_limit_bytes=48 << 20),
        name="feed_forward",
    )(resid, mixed, all_cross, gain[None], grad_out, all_ffn, all_ffn)


def bias_matrices():
    place = np.arange(256)
    distance = np.where(place <= 128, 128 - place, 384 - place)
    edges = np.array(bucket_edges)
    buckets = np.where(distance < 16, distance, 16 + (distance[:, None] >= edges).sum(axis=1))
    spread = np.zeros((2, 2, BUCKETS, 2, 2, 256), np.float32)
    columns = np.zeros((2, 2, BUCKETS, 128), np.float32)
    sums = np.zeros((2, 2, 128, 2, 2, BUCKETS), np.float32)
    for which in (0, 1):
        for flag in (0, 1):
            spread[which, flag, buckets, which, flag, place] += 1.0
            spread[which, flag, BUCKETS - 1, which, flag, :] -= 1.0
            base = (HDIM if which == 0 else 0) + 3 + 2 * flag
            columns[which, flag, BUCKETS - 1, base : base + 2] = 1.0
            sums[which, flag, HDIM if which == 0 else 0, which, flag, BUCKETS - 1] = 1.0
    spread = spread.reshape(128, 1024)
    forward = np.concatenate((spread, columns.reshape(128, 128)), axis=1)
    backward = np.concatenate((spread.T, sums.reshape(512, 128)), axis=0)
    return forward, backward


def bias_parts(table_low):
    place = np.arange(2 * BUCKETS * HEADS)
    code, head = place // HEADS, place % HEADS
    chosen = (head // 2 == np.arange(PAIRS)[:, None]).astype(np.float32)
    spread = bias_matrices()[0][(head % 2) * 2 * BUCKETS + code]
    both = mm(jnp.asarray(chosen, bf16), table_low * jnp.asarray(spread, bf16)) * LOG2E
    far = both[:, 1024:]
    high = far.astype(bf16)
    rest = (far - high.astype(f32)).astype(bf16)
    odd = lax.broadcasted_iota(jnp.int32, (1, 128), 1) % 2 == 1
    return jnp.where(odd, high, rest).reshape(PAIRS, 1, 128), both[:, :1024].reshape(PAIRS, 4, 256)


def table_gradient(near_sums, row_sums):
    both = jnp.concatenate((near_sums.reshape(PAIRS, -1), row_sums.reshape(PAIRS, -1)), axis=1)
    matrix = jnp.asarray(bias_matrices()[1], f32)
    by_pair = jnp.dot(both, matrix, precision=lax.Precision.HIGHEST, preferred_element_type=f32)
    return by_pair.reshape(HEADS, 2 * BUCKETS).T.reshape(-1)


def seq_shift(array, count):
    length = array.shape[0]
    return lax.dynamic_slice_in_dim(jnp.concatenate((array, array), axis=0), count, length, axis=0)


def others_rows(rows, own_last):
    parts = lax.axis_size("seq")
    if parts == 2:
        return lax.ppermute(rows, "seq", [(0, 1)] if own_last else [(0, 1), (1, 0)])
    whole = lax.all_gather(rows, "seq", axis=0, tiled=True)
    step = rows.shape[0]
    start = lax.rem(lax.axis_index("seq") + 1, parts) * step
    return seq_shift(whole, start)[: (parts - 1) * step]


def to_owners(grads, own_last):
    parts = lax.axis_size("seq")
    if parts == 2:
        return lax.ppermute(grads, "seq", [(1, 0)] if own_last else [(0, 1), (1, 0)])
    step = grads.shape[0] // (parts - 1)
    whole = jnp.concatenate((grads, jnp.zeros((step, grads.shape[1]), grads.dtype)), axis=0)
    start = lax.rem(parts - 1 - lax.axis_index("seq"), parts) * step
    return lax.psum_scatter(seq_shift(whole, start), "seq", scatter_dimension=0, tiled=True)


def on_device(
    decoder_in,
    encoder_out,
    dec_lengths,
    pair_flags,
    enc_segments,
    self_proj,
    self_out,
    cross_proj,
    cross_out,
    ffn_in,
    ffn_out,
    norm_gains,
    rel_table,
    out_grad,
):
    shard = self_out.shape[0]
    units = FF // D
    own_kernels = (lax.axis_size("dp"), lax.axis_size("seq")) == (16, 2)
    if own_kernels:
        all_self, all_cross, pair_ffn = gather_blocks(
            self_proj, self_out, cross_proj, cross_out, ffn_in, ffn_out, norm_gains, rel_table
        )
        all_self = all_self.reshape(-1, all_self.shape[2])
        all_cross = all_cross.reshape(-1, all_cross.shape[2])
        pair_ffn = pair_ffn.reshape(2 * shard, 2 * FF)
        all_ffn = lax.all_gather(pair_ffn, "dp", axis=0, tiled=True)
    else:
        small = jnp.concatenate((norm_gains, rel_table[None]), axis=0).T
        small = jnp.pad(small, ((0, 0), (0, 124)))
        block_self = jnp.concatenate((*self_proj, self_out, small), axis=1).astype(bf16)
        block_cross = jnp.concatenate((*cross_proj, cross_out), axis=1).astype(bf16)
        ffn_in_here = jnp.swapaxes(ffn_in.reshape(shard, D, units), 1, 2).reshape(shard, FF)
        block_ffn = jnp.concatenate((ffn_in_here, ffn_out.reshape(shard, FF)), axis=1).astype(bf16)
        all_self = lax.all_gather(block_self, BOTH, axis=0, tiled=True)
        all_cross = lax.all_gather(block_cross, BOTH, axis=0, tiled=True)
        all_ffn = lax.all_gather(block_ffn, BOTH, axis=0, tiled=True)
    encoder_out = lax.optimization_barrier((encoder_out, all_cross))[0]
    self_q, self_k, self_v, out_self = (all_self[:, i * D : (i + 1) * D] for i in range(4))
    cross_q, cross_k, cross_v = (all_cross[:, i * D : (i + 1) * D] for i in range(3))
    small_all = all_self[:, 4 * D :]
    gains = small_all[:, :3].T.astype(f32)
    far_lanes, near_lines = bias_parts(small_all[:, 3:4])

    tokens = decoder_in[0]
    memory = encoder_out[0]
    grad_out = out_grad[0]
    rows, enc_rows = tokens.shape[0], memory.shape[0]
    seq_count = lax.axis_size("seq")
    seq_index = lax.axis_index("seq")
    keys, enc_keys = rows * seq_count, enc_rows * seq_count

    numbers = (dec_lengths, pair_flags)
    before = others_rows(tokens, True)
    others = others_rows(memory, False)

    scale = 0.125 * LOG2E
    tokens = tokens.astype(f32)
    inverse_one = inverse_rms(tokens)
    normed_one = (tokens * inverse_one * gains[0]).astype(bf16)
    before = before.astype(f32)
    normed_before = (before * inverse_rms(before) * gains[0]).astype(bf16)
    query_one = (mm(normed_one, self_q) * scale).astype(bf16)
    kv_one = mm(normed_one, all_self[:, D : 3 * D]).astype(bf16)
    kv_before = mm(normed_before, all_self[:, D : 3 * D]).astype(bf16)
    parts_one = ((kv_before, 0, PAIRS), (kv_one, 0, PAIRS))
    mixed_one, weights_one, total_one = attend(
        numbers, rows, query_one, parts_one, far=far_lanes, near=near_lines
    )
    resid_one = tokens + mm(mixed_one, out_self)
    inverse_two = inverse_rms(resid_one)
    normed_two = (resid_one * inverse_two * gains[1]).astype(bf16)
    query_two = (mm(normed_two, cross_q) * scale).astype(bf16)
    kv_memory = mm(memory, all_cross[:, D : 3 * D]).astype(bf16)
    kv_others = mm(others, all_cross[:, D : 3 * D]).astype(bf16)
    parts_two = ((kv_memory, 0, PAIRS), (kv_others, 0, PAIRS))
    mixed_two, weights_two, total_two = attend(numbers, rows, query_two, parts_two, segments=enc_segments)
    layer_out, grad_resid, grad_low_two, grad_mixed, grad_ffn = feed_forward(
        resid_one, mixed_two, all_cross, gains[2], grad_out, all_ffn
    )

    grad_query, grad_key, grad_value = attend_back(
        numbers, query_two, parts_two, weights_two, mixed_two, total_two, grad_mixed, False
    )
    turned = (((0,), (1,)), ((), ()))
    kv_other = mm(grad_key[:, enc_rows:], cross_k, turned)
    kv_other = (kv_other + mm(grad_value[:, enc_rows:], cross_v, turned)).astype(bf16)
    grad_memory = mm(grad_key[:, :enc_rows], cross_k, turned)
    grad_memory = grad_memory + mm(grad_value[:, :enc_rows], cross_v, turned)
    grad_two = (grad_query, grad_key, grad_value)
    grad_normed = mm(grad_query, cross_q, NT)
    grad_resid = grad_resid + norm_back(resid_one, inverse_two, gains[1], grad_normed)
    grad_low = grad_resid.astype(bf16)
    grad_mixed = mm(grad_low, out_self, NT).astype(bf16)
    grad_mixed, kv_other = lax.optimization_barrier((grad_mixed, kv_other))
    grad_query, grad_key, grad_value, near_sums, row_sums = attend_back(
        numbers, query_one, parts_one, weights_one, mixed_one, total_one, grad_mixed, True
    )
    grad_others = to_owners(kv_other, False)
    table_grad = table_gradient(near_sums, row_sums)
    small = jnp.broadcast_to(table_grad[:, None], (D, 128)).astype(bf16)

    def owned(array):
        return lax.psum_scatter(array, BOTH, scatter_dimension=0, tiled=True).astype(f32)

    def projections(block):
        return jnp.stack([block[:, i * D : (i + 1) * D] for i in range(3)], axis=0)

    if own_kernels:
        own_self, own_self_out, own_cross, own_cross_out, own_small, grad_input = scatter_products(
            (normed_before, normed_one, grad_query, grad_key, grad_value, mixed_one, grad_low),
            (normed_two, grad_two[0], memory, others, grad_two[1], grad_two[2], mixed_two, grad_low_two),
            small.reshape(-1, shard, small.shape[1]),
            all_self,
            decoder_in[0],
            grad_resid,
            gains[:1],
        )
    else:
        normed_all = jnp.concatenate((normed_before, normed_one), axis=0)
        memory_all = jnp.concatenate((memory, others), axis=0)
        self_grads = (
            mm(normed_one, grad_query, TN),
            mm(normed_all, grad_key, turned),
            mm(normed_all, grad_value, turned),
            mm(mixed_one, grad_low, TN),
        )
        cross_grads = (
            mm(normed_two, grad_two[0], TN),
            mm(memory_all, grad_two[1], turned),
            mm(memory_all, grad_two[2], turned),
            mm(mixed_two, grad_low_two, TN),
        )
        self_grads = jnp.concatenate(self_grads, axis=1).astype(bf16)
        block = owned(jnp.concatenate((self_grads, small), axis=1))
        own_self, own_self_out = projections(block), block[:, 3 * D : 4 * D]
        own_small = block[:, 4 * D :]
        block = owned(jnp.concatenate(cross_grads, axis=1).astype(bf16))
        own_cross, own_cross_out = projections(block), block[:, 3 * D :]
        split = keys - rows
        grad_before = mm(grad_key[:, :split], self_k, turned) + mm(grad_value[:, :split], self_v, turned)
        grad_before = to_owners(grad_before.astype(bf16), True)
        grad_normed = mm(grad_key[:, split:], self_k, turned) + mm(grad_value[:, split:], self_v, turned)
        grad_normed = grad_normed + mm(grad_query, self_q, NT) + grad_before.astype(f32)
        grad_input = grad_resid + norm_back(tokens, inverse_one, gains[0], grad_normed)

    grad_others, own_small = lax.optimization_barrier((grad_others, own_small))
    grad_encoder = grad_memory + grad_others.astype(f32)
    own_ffn = owned(grad_ffn)
    own_ffn_in = jnp.swapaxes(own_ffn[:, :FF].reshape(shard, units, D), 1, 2).reshape(shard, FF)
    own_ffn_out = own_ffn[:, FF:].reshape(ffn_out.shape)

    def products(weight, grad):
        return jnp.sum(weight.astype(bf16).astype(f32) * grad, axis=-1)

    gain_grads = jnp.stack(
        (
            jnp.sum(products(self_proj, own_self), axis=0),
            products(cross_proj[0], own_cross[0]),
            products(ffn_in, own_ffn_in),
        ),
        axis=0,
    )
    gain_grads = gain_grads / norm_gains.astype(bf16).astype(f32)

    return (
        layer_out[None],
        grad_input[None],
        grad_encoder[None],
        own_self,
        own_self_out,
        own_cross,
        own_cross_out,
        own_ffn_in,
        own_ffn_out,
        gain_grads,
        own_small[:, 0],
    )


def solution(mesh):
    hidden = P("dp", "seq", None)
    rows_split = P(BOTH, None)
    stacked = P(None, BOTH, None)
    stream = P("dp", None)
    return jax.shard_map(
        on_device,
        mesh=mesh,
        in_specs=(
            hidden,
            hidden,
            stream,
            stream,
            stream,
            stacked,
            rows_split,
            stacked,
            rows_split,
            rows_split,
            rows_split,
            P(None, BOTH),
            P(BOTH),
            hidden,
        ),
        out_specs=(
            hidden,
            hidden,
            hidden,
            stacked,
            rows_split,
            stacked,
            rows_split,
            rows_split,
            rows_split,
            P(None, BOTH),
            P(BOTH),
        ),
        check_vma=False,
    )
```

```python
import functools
import math

import jax
import jax.numpy as jnp
import numpy as np
from jax import lax
from jax.experimental import pallas as pl
from jax.experimental.pallas import tpu as pltpu
from jax.sharding import PartitionSpec as P

D = 768
HEADS = 12
HDIM = 64
FF = 3072
BUCKETS = 32
PAIRS = HEADS // 2
LOG2E = math.log2(math.e)
LN2 = math.log(2.0)
epsilon = 1e-06
neg_large = -1e30
bucket_edges = (19, 21, 24, 27, 31, 35, 40, 46, 52, 59, 67, 77, 87, 99, 113)
f32 = jnp.float32
bf16 = jnp.bfloat16
NT = (((1,), (1,)), ((), ()))
NN = (((1,), (0,)), ((), ()))
TN = (((0,), (0,)), ((), ()))
BOTH = ("dp", "seq")
MESH = pl.DeviceIdType.MESH


def mm(a, b, dims=NN):
    return lax.dot_general(a, b, dims, preferred_element_type=f32)


def inverse_rms(values):
    return lax.rsqrt(jnp.mean(values * values, axis=-1, keepdims=True) + epsilon)


def norm_back(values, inverse, gain, grad):
    unit = values * inverse
    grad = grad * gain
    return inverse * (grad - unit * jnp.mean(grad * unit, axis=-1, keepdims=True))


def head_lanes(which):
    low = lax.broadcasted_iota(jnp.int32, (1, 128), 1) < HDIM
    return low if which == 0 else jnp.logical_not(low)


def row_chunks(rows, keys, causal, step):
    return [
        (slice(i, i + step), (keys - rows + i + step) if causal else keys)
        for i in range(0, rows, step)
    ]


def near_bias(near_ref, which):
    row = lax.broadcasted_iota(jnp.int32, (128, 256), 0)
    column = lax.broadcasted_iota(jnp.int32, (128, 256), 1)
    tiles = []
    for flag in (0, 1):
        line = near_ref[0, 2 * which + flag : 2 * which + flag + 1, :]
        tile = pltpu.roll(jnp.broadcast_to(line, (128, 256)), 0, 1, stride=1, stride_axis=0)
        tiles.append(jnp.where(column - row > 128, neg_large, tile))
    return tiles


def diagonal_sums(tile):
    for step in (64, 32, 16, 8):
        tile = tile[:step] + pltpu.roll(tile[step:], 256 - step, 1)
    row = lax.broadcasted_iota(jnp.int32, (8, 256), 0)
    for step in (4, 2, 1):
        tile = jnp.where((row & step) != 0, pltpu.roll(tile, 256 - step, 1), tile)
    return jnp.sum(tile, axis=0, keepdims=True)


def pairs_between(place, end_one, end_two):
    return (place >= end_one).astype(jnp.int32) + (place >= end_two).astype(jnp.int32)


def decoder_pairs(lengths, place):
    return pairs_between(place, lengths[0, 0], lengths[0, 0] + lengths[0, 1])


def flagged(numbers, rows, first, count, width):
    lengths, flags = numbers
    place = lax.broadcasted_iota(jnp.int32, (count, width), 0)
    pair = decoder_pairs(lengths, place + (lax.axis_index("seq") * rows + first))
    return jnp.where(pair == 0, flags[0, 0], jnp.where(pair == 1, flags[0, 1], 0)) > 0


def extra_columns(numbers, rows, keys, segments, query_extra, key_extra):
    lengths = numbers[0]
    here = lax.axis_index("seq") * rows
    lane = lax.broadcasted_iota(jnp.int32, (rows, 128), 1) & (HDIM - 1)
    pair = decoder_pairs(lengths, lax.broadcasted_iota(jnp.int32, (rows, 128), 0) + here)
    flag = flagged(numbers, rows, 0, rows, 128).astype(jnp.int32)
    wanted = jnp.where(lane < 3, pair, (flag << 1) + 3)
    chosen = jnp.where(lane < 3, lane, ((lane - 3) & ~1) + 3)
    fits = jnp.logical_and(wanted == chosen, lane < 7)
    query_extra[...] = jnp.where(fits, 1.0, 0.0).astype(bf16)
    lane = lax.broadcasted_iota(jnp.int32, (keys, 128), 1) & (HDIM - 1)
    place = lax.broadcasted_iota(jnp.int32, (keys, 128), 0)
    if segments is None:
        place = place + (here + rows - keys)
        pair = jnp.where(place < 0, 3, decoder_pairs(lengths, place))
    else:
        place = place + lax.axis_index("seq") * (keys // lax.axis_size("seq"))
        place = jnp.where(place >= keys, place - keys, place)

        def below(pair):
            count = jnp.sum((segments[...] < pair).astype(f32), axis=0, keepdims=True)
            return jnp.sum(count, axis=1, keepdims=True).astype(jnp.int32)

        pair = pairs_between(place, below(1), below(2))
    wrong = jnp.logical_and(pair != lane, lane < 3)
    key_extra[...] = jnp.where(wrong, neg_large, 0.0).astype(bf16)


def attend_body(rows, keys, causal, step, parts, *refs):
    numbers, q_ref = refs[:2], refs[2]
    key_refs, value_refs = refs[3 : 3 + parts], refs[3 + parts : 3 + 2 * parts]
    o_ref, e_ref, inv_ref, query_extra, key_extra = refs[-5:]

    @pl.when(pl.program_id(0) == 0)
    def _():
        segments = None if causal else refs[3 + 2 * parts]
        extra_columns(numbers, rows, keys, segments, query_extra, key_extra)

    extra = key_extra[...]
    if causal:
        far_ref, near_ref = refs[3 + 2 * parts : 5 + 2 * parts]
        extra = extra + far_ref[0]
    key_pair = jnp.concatenate([ref[...] for ref in key_refs], axis=0)
    value_pair = jnp.concatenate([ref[...] for ref in value_refs], axis=0)
    chunks = row_chunks(rows, keys, causal, step)
    found = []
    for which in (0, 1):
        mine = head_lanes(which)
        key_head = jnp.where(mine, key_pair, extra)
        value_head = jnp.where(mine, value_pair, jnp.ones_like(value_pair))
        if causal:
            tile_zero, tile_one = near_bias(near_ref, which)
        done = []
        for here, width in chunks:
            query = jnp.where(mine, q_ref[here], query_extra[here])
            scores = mm(query, key_head[:width], NT)
            if causal:
                cut = width - 256
                flag = flagged(numbers, rows, here.start, step, 1)
                near = scores[:, cut:] + jnp.where(flag, tile_one, tile_zero)
                far = scores[:, :cut]
                peak = jnp.maximum(
                    jnp.max(far, axis=1, keepdims=True), jnp.max(near, axis=1, keepdims=True)
                )
                near = jnp.exp2(near - peak).astype(bf16)
                far = jnp.exp2(far - peak).astype(bf16)
                e_ref[which, here, :cut] = far
                e_ref[which, here, cut:width] = near
                mixed = mm(far, value_head[:cut]) + mm(near, value_head[cut:width])
            else:
                peak = jnp.max(scores, axis=1, keepdims=True)
                weights = jnp.exp2(scores - peak).astype(bf16)
                e_ref[which, here, :] = weights
                mixed = mm(weights, value_head)
            total = mixed[:, HDIM : HDIM + 1] if which == 0 else mixed[:, 0:1]
            inverse = 1.0 / total
            done.append((mixed * inverse, jnp.broadcast_to(inverse, mixed.shape)))
        found.append(done)
    low = head_lanes(0)
    for index, (here, _) in enumerate(chunks):
        o_ref[here] = jnp.where(low, found[0][index][0], found[1][index][0]).astype(bf16)
        inv_ref[here] = jnp.where(low, found[0][index][1], found[1][index][1])


def pair_columns(rows, first=0):
    return pl.BlockSpec((rows, 128), lambda p: (0, first + p))


def operands_of(numbers, query, parts):
    arrays = [*numbers, query] + [part[0] for part in parts] * 2
    specs = [pl.BlockSpec(memory_space=pltpu.SMEM)] * 2 + [pair_columns(query.shape[0])]
    for place in (1, 2):
        specs += [pair_columns(part[0].shape[0], part[place]) for part in parts]
    return arrays, specs


def per_pair(height, width):
    return pl.BlockSpec((1, height, width), lambda p: (p, 0, 0))


def attend(numbers, rows, query, parts, segments=None, far=None, near=None):
    keys = sum(part[0].shape[0] for part in parts)
    causal = far is not None
    step = 128 if causal else min(256, rows)
    operands, specs = operands_of(numbers, query, parts)
    if causal:
        operands += [far, near]
        specs += [per_pair(1, 128), per_pair(4, 256)]
    else:
        operands.append(segments)
        specs.append(pl.BlockSpec(segments.shape, lambda p: (0, 0)))
    return pl.pallas_call(
        functools.partial(attend_body, rows, keys, causal, step, len(parts)),
        grid=(PAIRS,),
        in_specs=specs,
        out_specs=(
            pair_columns(rows),
            pl.BlockSpec((2, rows, keys), lambda p: (p, 0, 0)),
            pair_columns(rows),
        ),
        out_shape=(
            jax.ShapeDtypeStruct((rows, D), bf16),
            jax.ShapeDtypeStruct((HEADS, rows, keys), bf16),
            jax.ShapeDtypeStruct((rows, D), f32),
        ),
        scratch_shapes=[pltpu.VMEM((rows, 128), bf16), pltpu.VMEM((keys, 128), bf16)],
        compiler_params=pltpu.CompilerParams(vmem_limit_bytes=56 << 20),
        name="attend_causal" if causal else "attend_cross",
    )(*operands)


def attend_back_body(rows, keys, causal, step, parts, *refs):
    numbers, q_ref = refs[:2], refs[2]
    refs = refs[3:]
    key_refs, value_refs = refs[:parts], refs[parts : 2 * parts]
    e_ref, o_ref, inv_ref, d_ref = refs[2 * parts : 4 + 2 * parts]
    if causal:
        dq_ref, dk_ref, dv_ref, near_ref, sum_ref, ds_ref = refs[4 + 2 * parts :]
    else:
        dq_ref, dk_ref, dv_ref, ds_ref = refs[4 + 2 * parts :]
    lane = lax.broadcasted_iota(jnp.int32, (1, 128), 1)
    key_pair = jnp.concatenate([ref[...] for ref in key_refs], axis=0)
    value_pair = jnp.concatenate([ref[...] for ref in value_refs], axis=0)
    scaled = (d_ref[...].astype(f32) * inv_ref[...]).astype(bf16)
    product = scaled.astype(f32) * o_ref[...].astype(f32)
    scaled_t = scaled.T
    query_t = q_ref[...].T
    chunks = row_chunks(rows, keys, causal, step)
    query_parts = []
    for which in (0, 1):
        mine = head_lanes(which)
        base = HDIM if which == 0 else 0
        value_head = jnp.where(mine, value_pair, jnp.ones_like(value_pair))
        key_head = jnp.where(mine, key_pair, jnp.ones_like(key_pair))
        delta = jnp.sum(jnp.where(mine, product, 0.0), axis=1, keepdims=True)
        high = delta.astype(bf16)
        rest = (delta - high.astype(f32)).astype(bf16)
        extra = jnp.where(
            lane == base, -high, jnp.where(lane == base + 1, -rest, jnp.zeros_like(rest))
        )
        grad_head = jnp.where(mine, scaled, extra)
        done = []
        if causal:
            near_all = jnp.zeros((128, 256), f32)
            near_one = jnp.zeros((128, 256), f32)
        for here, width in chunks:
            centred = mm(grad_head[here], value_head[:width], NT)
            grad_scores = e_ref[which, here, :width].astype(f32) * centred
            if causal:
                near = grad_scores[:, width - 256 :]
                near_all = near_all + near
                flag = flagged(numbers, rows, here.start, step, 1)
                near_one = near_one + jnp.where(flag, near, 0.0)
            grad_scores = grad_scores.astype(bf16)
            ds_ref[here, :width] = grad_scores
            done.append(mm(grad_scores, key_head[:width]))
        query_parts.append(done)
        half = slice(HDIM * which, HDIM * which + HDIM)
        if causal:
            spans = [(slice(0, keys - rows), 0)] if keys > rows else []
            spans += [
                (slice(keys - rows + i, keys - rows + i + step), i) for i in range(0, rows, step)
            ]
        else:
            spans = [(slice(0, keys), 0)]
        for span, first in spans:
            grad_key = mm(query_t[half, first:], ds_ref[first:, span])
            dk_ref[half, span] = (grad_key * LN2).astype(dk_ref.dtype)
            grad_value = mm(scaled_t[half, first:], e_ref[which, first:, span])
            dv_ref[half, span] = grad_value.astype(dv_ref.dtype)
        if causal:
            for flag, tile in ((0, near_all - near_one), (1, near_one)):
                near_ref[0, 2 * which + flag : 2 * which + flag + 1, :] = diagonal_sums(tile)
    low = head_lanes(0)
    for index, (here, _) in enumerate(chunks):
        both = jnp.where(low, query_parts[0][index], query_parts[1][index])
        dq_ref[here] = (both * 0.125).astype(dq_ref.dtype)
    if causal:
        flags = flagged(numbers, rows, 0, rows, 1)
        for which in (0, 1):
            whole = jnp.concatenate(query_parts[which], axis=0)
            one = jnp.sum(jnp.where(flags, whole, 0.0), axis=0, keepdims=True)
            every = jnp.sum(whole, axis=0, keepdims=True)
            sum_ref[0, 2 * which : 2 * which + 1, :] = every - one
            sum_ref[0, 2 * which + 1 : 2 * which + 2, :] = one


def attend_back(numbers, query, parts, weights, mixed, inverse, grad_mixed, causal):
    rows, keys = weights.shape[1:]
    step = 128 if causal else min(256, rows)
    operands, specs = operands_of(numbers, query, parts)
    operands += [weights, mixed, inverse, grad_mixed]
    specs += [pl.BlockSpec((2, rows, keys), lambda p: (p, 0, 0))] + [pair_columns(rows)] * 3
    turned = jax.ShapeDtypeStruct((D, keys), bf16)
    turned_spec = pl.BlockSpec((128, keys), lambda p: (p, 0))
    shapes = [jax.ShapeDtypeStruct((rows, D), bf16), turned, turned]
    out_specs = [pair_columns(rows), turned_spec, turned_spec]
    if causal:
        shapes += [
            jax.ShapeDtypeStruct((PAIRS, 4, 256), f32),
            jax.ShapeDtypeStruct((PAIRS, 4, 128), f32),
        ]
        out_specs += [per_pair(4, 256), per_pair(4, 128)]
    return pl.pallas_call(
        functools.partial(attend_back_body, rows, keys, causal, step, len(parts)),
        grid=(PAIRS,),
        in_specs=specs,
        out_specs=tuple(out_specs),
        out_shape=tuple(shapes),
        scratch_shapes=[pltpu.VMEM((rows, keys), bf16)],
        compiler_params=pltpu.CompilerParams(vmem_limit_bytes=56 << 20),
        name="attend_causal_back" if causal else "attend_cross_back",
    )(*operands)


def place_here():
    index = lax.axis_index("dp")
    return index // 4, (index // 2) % 2, index % 2, lax.axis_index("seq")


def block_of(z, x, core, y):
    return ((z * 2 + x) * 2 + core) * 2 + y


def device_of(z, x, core, y):
    return ((z * 2 + x) * 2 + core, y)


def greet_neighbours(z, x, core, y):
    barrier = pltpu.get_barrier_semaphore()

    def greet(device):
        pl.semaphore_signal(barrier, inc=1, device_id=device, device_id_type=MESH)

    greet(device_of(z, x, 1 - core, y))
    greet(device_of(z, 1 - x, core, y))
    greet(device_of(z, x, core, 1 - y))

    @pl.when(z > 0)
    def _():
        greet(device_of(z - 1, x, core, y))

    @pl.when(z < 3)
    def _():
        greet(device_of(z + 1, x, core, y))

    pl.semaphore_wait(barrier, 4 + ((z + 1) // 2) % 2)


def unit_order():
    place = np.arange(512)
    return (place[:, None] == (place % 128) * 4 + place // 128).astype(np.float32)


def gather_body(*refs):
    masters, refs = refs[:9], refs[9:]
    wholes, pair_whole = refs[:2], refs[2]
    sources, pair_source = refs[3:5], refs[5]
    own_sems, mate_sems, recv_sems, pair_sems = refs[6:10]
    route_sems = dict(zip(("up", "down", "x", "y"), refs[10:]))
    self_proj, self_out, cross_proj, cross_out, ffn_in, ffn_out, norm_gains, table, order = masters
    count = 2
    shard = self_out.shape[0]
    for stacked, single, source in ((self_proj, self_out, sources[0]), (cross_proj, cross_out, sources[1])):
        for j in range(3):
            source[:, j * D : (j + 1) * D] = stacked[j].astype(bf16)
        source[:, 3 * D : 4 * D] = single[...].astype(bf16)
    lane = lax.broadcasted_iota(jnp.int32, (shard, 128), 1)
    row = lax.broadcasted_iota(jnp.int32, (shard, shard), 0)
    same = row == lax.broadcasted_iota(jnp.int32, (shard, shard), 1)
    small = jnp.zeros((shard, 128), f32)
    for j in range(4):
        line = norm_gains[j : j + 1] if j < 3 else table[...]
        column = jnp.sum(jnp.where(same, jnp.broadcast_to(line, same.shape), 0.0), axis=1, keepdims=True)
        small = jnp.where(lane == j, column, small)
    sources[0][:, 4 * D :] = small.astype(bf16)
    z, x, core, y = place_here()
    mate = device_of(z, x, 1 - core, y)
    me = block_of(z, x, core, y)
    greet_neighbours(z, x, core, y)

    routes = (("y", "z", "x"), ("z", "x", "y"))
    slots = {}

    def send(which, source, block, send_sem, device):
        return pltpu.make_async_remote_copy(
            src_ref=source,
            dst_ref=wholes[which].at[block],
            send_sem=send_sem,
            recv_sem=recv_sems.at[which, block],
            device_id=device,
            device_id_type=MESH,
        )

    def copies(which, far, up, dx, dy, source=None):
        at_z = z + far if up else z - far
        block = block_of(at_z, (x + dx) % 2, core, (y + dy) % 2)
        source = wholes[which].at[block] if source is None else source
        route = routes[which]
        moved = [axis for axis, steps in (("z", far), ("x", dx), ("y", dy)) if steps]
        last = max((route.index(axis) for axis in moved), default=-1)
        targets = []
        for axis in route[max(last, 0) :]:
            fresh = route.index(axis) > last
            if axis == "z" and (fresh or not up):
                targets.append((z < 3, "up", device_of(z + 1, x, core, y)))
            if axis == "z" and (fresh or up):
                targets.append((z > 0, "down", device_of(z - 1, x, core, y)))
            if axis == "x" and fresh:
                targets.append((None, "x", device_of(z, 1 - x, core, y)))
            if axis == "y" and fresh:
                targets.append((None, "y", device_of(z, x, core, 1 - y)))
        out = []
        for condition, kind, device in targets:
            taken = slots.setdefault((which, kind), {})
            slot = taken.setdefault((far, up, dx, dy), len(taken))
            out.append((condition, send(which, source, block, route_sems[kind].at[which, slot], device)))
        taken = slots.setdefault((which, "mate"), {})
        slot = taken.setdefault((far, up, dx, dy), len(taken))
        out.append((None, send(which, source, block, mate_sems.at[which, slot], mate)))
        return block, out

    def when(condition, action):
        if condition is None:
            action()
        else:
            pl.when(condition)(action)

    def exists(far, up):
        if far == 0:
            return None
        return z + far < 4 if up else z - far >= 0

    def onwards(which, far, up, dx, dy, source=None):
        def run():
            block, out = copies(which, far, up, dx, dy, source)
            if source is None:
                pltpu.make_async_copy(wholes[which].at[block], wholes[which].at[block], recv_sems.at[which, block]).wait()
            for condition, copy in out:
                when(condition, copy.start)

        when(exists(far, up), run)

    own = [
        pltpu.make_async_copy(sources[i], wholes[i].at[me], own_sems.at[i]) for i in range(count)
    ]
    own.append(pltpu.make_async_copy(pair_source, pair_whole.at[y], pair_sems.at[0]))
    pair = pltpu.make_async_remote_copy(
        src_ref=pair_source,
        dst_ref=pair_whole.at[y],
        send_sem=pair_sems.at[1],
        recv_sem=pair_sems.at[2],
        device_id=device_of(z, x, core, 1 - y),
        device_id_type=MESH,
    )
    for which in range(count):
        onwards(which, 0, False, 0, 0, sources[which])
    for copy in own[:count]:
        copy.start()
    units = FF // D
    for m in range(FF // 512):
        piece = mm(ffn_in[:, 512 * m : 512 * (m + 1)].astype(bf16), order[...]).astype(bf16)
        for b in range(units):
            first = b * D + 128 * m
            pair_source[:, first : first + 128] = piece[:, 128 * b : 128 * (b + 1)]
    row = lax.broadcasted_iota(jnp.int32, (shard, units * shard), 0) * units
    place = lax.broadcasted_iota(jnp.int32, (shard, units * shard), 1)
    held = ffn_out[...].astype(bf16)
    for b in range(units):
        rows = mm(jnp.where(row + b == place, 1.0, 0.0).astype(bf16), held)
        pair_source[:, FF + b * D : FF + (b + 1) * D] = rows.astype(bf16)
    own[count].start()
    pair.start()
    waves = [[] for _ in range(6)]
    for dx in (0, 1):
        for dy in (0, 1):
            for far in range(4):
                for up in (False, True):
                    if far == 0 and (up or (dx == 0 and dy == 0)):
                        continue
                    waves[far + dx + dy].append((far, up, dx, dy))
    for wave in waves:
        for far, up, dx, dy in wave:
            for which in range(count):
                onwards(which, far, up, dx, dy)
    for dx in (0, 1):
        for dy in (0, 1):
            for far in range(4):
                for up in (False, True):
                    if far == 0 and up:
                        continue
                    for which in range(count):

                        def finish(which=which, far=far, up=up, dx=dx, dy=dy):
                            at_z = z + far if up else z - far
                            block = block_of(at_z, (x + dx) % 2, 1 - core, (y + dy) % 2)
                            whole = wholes[which].at[block]
                            pltpu.make_async_copy(whole, whole, recv_sems.at[which, block]).wait()
                            source = sources[which] if (far, dx, dy) == (0, 0, 0) else None
                            _, out = copies(which, far, up, dx, dy, source)
                            for condition, copy in out:
                                when(condition, copy.wait_send)

                        when(exists(far, up), finish)
    for copy in own:
        copy.wait()
    pair.wait_send()
    came = pair_whole.at[1 - y]
    pltpu.make_async_copy(came, came, pair_sems.at[2]).wait()


def gather_blocks(self_proj, self_out, cross_proj, cross_out, ffn_in, ffn_out, norm_gains, rel_table):
    shard = self_out.shape[0]
    shapes = [(shard, 4 * D + 128), (shard, 4 * D)]
    pair = (shard, 2 * FF)
    dma = pltpu.SemaphoreType.DMA
    return pl.pallas_call(
        gather_body,
        in_specs=[pl.BlockSpec(memory_space=pltpu.VMEM)] * 9,
        out_specs=[pl.BlockSpec(memory_space=pl.ANY)] * 3,
        out_shape=[jax.ShapeDtypeStruct((32, *shape), bf16) for shape in shapes]
        + [jax.ShapeDtypeStruct((2, *pair), bf16)],
        scratch_shapes=[pltpu.VMEM(shape, bf16) for shape in (*shapes, pair)]
        + [dma((3,)), dma((2, 28)), dma((2, 32)), dma((3,))]
        + [dma((2, 16))] * 4,
        compiler_params=pltpu.CompilerParams(collective_id=0, has_side_effects=True),
        name="gather_blocks",
    )(
        self_proj,
        self_out,
        cross_proj,
        cross_out,
        ffn_in,
        ffn_out,
        norm_gains,
        rel_table[None],
        jnp.asarray(unit_order(), bf16),
    )


SELF_PRODUCTS = (((1,), 2, False), ((0, 1), 3, True), ((0, 1), 4, True), ((5,), 6, False))
CROSS_PRODUCTS = (((0,), 1, False), ((2, 3), 4, True), ((2, 3), 5, True), ((6,), 7, False))


def scatter_body(counts, *refs):
    total_in = sum(counts)
    arrays, small = refs[:total_in], refs[total_in]
    weights_ref, tokens_ref, resid_ref, gain_ref = refs[total_in + 1 : total_in + 5]
    refs = refs[total_in + 5 :]
    outs, grad_ref, refs = refs[:5], refs[5], refs[6:]
    held, small_held = refs[:total_in], refs[total_in]
    refs = refs[total_in + 1 :]
    parts, mate_in, first_in, second_in, line_in = (refs[2 * i : 2 * i + 2] for i in range(5))
    load_sems, mate_sems, first_sems, second_sems, line_sems = refs[10:15]
    mate_recv, first_recv, second_recv, line_recv = refs[15:19]
    back_in, back_sems, late_sems = refs[19:]
    z, x, core, y = place_here()
    loads = [
        pltpu.make_async_copy(source, target, load_sems.at[i])
        for i, (source, target) in enumerate(zip((*arrays, small), (*held, small_held)))
    ]
    for load in loads:
        load.start()
    greet_neighbours(z, x, core, y)
    half = z // 2
    order = (3 - 3 * half, 2 - half, 1 - z + 4 * half, z)

    def near(which, first, second):
        if which == 0:
            return (x + first) % 2, (y + second) % 2
        return (x + second) % 2, (y + first) % 2

    def block(which, i, first, second, other_core=0):
        bx, by = near(which, first, second)
        return block_of(order[i], bx, (core + other_core) % 2, by)

    def slot_of(which, i, first, second):
        bx, by = near(which, first, second)
        return (order[i] * 2 + bx) * 2 + by

    def remote(source, target, send_sem, recv_sem, device):
        return pltpu.make_async_remote_copy(
            src_ref=source,
            dst_ref=target,
            send_sem=send_sem,
            recv_sem=recv_sem,
            device_id=device,
            device_id_type=MESH,
        )

    def to_mate(which, i, first, second):
        slot = slot_of(which, i, first, second)
        return remote(
            parts[which].at[block(which, i, first, second, 1)],
            mate_in[which].at[slot],
            mate_sems.at[which, slot],
            mate_recv.at[which, slot],
            device_of(z, x, 1 - core, y),
        )

    def to_first(which, i, second):
        bx, by = near(which, 1, 0)
        return remote(
            parts[which].at[block(which, i, 1, second)],
            first_in[which].at[2 * i + second],
            first_sems.at[which, 2 * i + second],
            first_recv.at[which, 2 * i + second],
            device_of(z, bx, core, by),
        )

    def to_second(which, i):
        bx, by = near(which, 0, 1)
        return remote(
            parts[which].at[block(which, i, 0, 1)],
            second_in[which].at[i],
            second_sems.at[which, i],
            second_recv.at[which, i],
            device_of(z, bx, core, by),
        )

    def line_slot(which, came, at_z, second):
        return (came * 4 + at_z) * 2 + second if which == 0 else came * 4 + at_z

    def along_line(which, i, second=0):
        step = 1 - 2 * half if i < 2 else 1 - 2 * (z % 2)
        came = (1 - step) // 2
        slot = line_slot(which, came, order[i], second)
        return slot, remote(
            parts[which].at[block(which, i, 0, second)],
            line_in[which].at[slot],
            line_sems.at[which, 2 * i + second],
            line_recv.at[which, slot],
            device_of(z + step, x, core, y),
        )

    def arrived(buffer, sem):
        pltpu.make_async_copy(buffer, buffer, sem).wait()

    def wide(ref, index):
        return ref[index].astype(f32)

    every = [(1, 1), (1, 0), (0, 1), (0, 0)]

    def products(which, i):
        first = 0 if which == 0 else counts[0]
        height = 8 * parts[which].shape[1]
        odd = order[i] % 2
        window = pl.ds(pl.multiple_of(order[i] * height - odd * 64, 128), height + 64)
        blocks = pl.ds(order[i] * 8, 8)
        taken = {}
        for column, (lefts, right, turned) in enumerate(SELF_PRODUCTS if which == 0 else CROSS_PRODUCTS):
            if i == 0:
                for needed in (*lefts, right):
                    if needed in waiting[which]:
                        waiting[which].remove(needed)
                        loads[first + needed].wait()
            for left in lefts:
                if left not in taken:
                    rows = held[first + left][:, window].T
                    taken[left] = jnp.where(odd > 0, rows[64:], rows[:height])
            other = held[first + right][...]
            value = mm(jnp.concatenate([taken[left] for left in lefts], axis=1), other, NT if turned else NN)
            value = value.reshape(8, height // 8, value.shape[1]).astype(bf16)
            parts[which][blocks, :, column * D : (column + 1) * D] = value
        if which == 0:
            if i == 0:
                loads[-1].wait()
            parts[0][blocks, :, 4 * D :] = small_held[blocks]

    waiting = [set(range(counts[0])), set(range(counts[1]))]

    def make(i):
        for which in (1, 0):
            products(which, i)
            for first, second in every:
                to_mate(which, i, first, second).start()

    def chip_sum(which, i, first, second):
        here = block(which, i, first, second)
        slot = slot_of(which, i, first, second)
        arrived(mate_in[which].at[slot], mate_recv.at[which, slot])
        return here, wide(parts[which], here) + wide(mate_in[which], slot)

    def send_first(i):
        for second in (1, 0):
            for which in (1, 0):
                here, total = chip_sum(which, i, 1, second)
                parts[which][here] = total.astype(bf16)
                to_first(which, i, second).start()

    middle = (z + 1) // 2 == 1

    def after_first(which, i, second):
        here, total = chip_sum(which, i, 0, second)
        arrived(first_in[which].at[2 * i + second], first_recv.at[which, 2 * i + second])
        return here, total + wide(first_in[which], 2 * i + second)

    def send_second(i):
        here, total = after_first(1, i, 1)
        parts[1][here] = total.astype(bf16)
        to_second(1, i).start()

    def send_line(which, i, second, here, total):
        parts[which][here] = total.astype(bf16)
        slot, copy = along_line(which, i, second)

        @pl.when(middle)
        def _():
            arrived(line_in[which].at[slot], line_recv.at[which, slot])
            total = wide(parts[which], here) + wide(line_in[which], slot)
            parts[which][here] = total.astype(bf16)

        copy.start()

    def line_self(i):
        for second in (1, 0):
            send_line(0, i, second, *after_first(0, i, second))

    def line_cross(i):
        here, total = after_first(1, i, 0)
        arrived(second_in[1].at[i], second_recv.at[1, i])
        total = total + wide(second_in[1], i)
        if i < 3:
            send_line(1, i, 0, here, total)
        else:
            put(1, total, False)

    def from_line(which, second, add):
        for came, there in ((0, z > 0), (1, z < 3)):
            slot = line_slot(which, came, z, second)

            @pl.when(there)
            def _():
                arrived(line_in[which].at[slot], line_recv.at[which, slot])
                add(wide(line_in[which], slot))

    def last_self():
        here, total = after_first(0, 3, 1)
        parts[0][here] = total.astype(bf16)

        def add(value):
            parts[0][here] = (wide(parts[0], here) + value).astype(bf16)

        from_line(0, 1, add)
        to_second(0, 3).start()
        put(0, after_first(0, 3, 0)[1], False)
        from_line(0, 0, lambda value: put(0, value, True))

    def put(which, value, add):
        stacked, single = outs[2 * which : 2 * which + 2]
        targets = [(stacked.at[j], j) for j in range(3)] + [(single, 3)]
        for target, j in targets:
            piece = value[:, j * D : (j + 1) * D]
            target[...] = target[...] + piece if add else piece
        if which == 0:
            piece = value[:, 4 * D :]
            outs[4][...] = outs[4][...] + piece if add else piece


    split = arrays[0].shape[0]
    cross = held[counts[0] :]
    weights_kv, weights_q = cross[4].at[:, : 2 * D], cross[5].at[:, :D]
    rows_held, back_out = cross[0], cross[1]
    late = (
        pltpu.make_async_copy(weights_ref.at[:, D : 3 * D], weights_kv, late_sems.at[0]),
        pltpu.make_async_copy(weights_ref.at[:, :D], weights_q, late_sems.at[1]),
        pltpu.make_async_copy(tokens_ref, rows_held, late_sems.at[2]),
        pltpu.make_async_copy(resid_ref, grad_ref, late_sems.at[3]),
    )
    back = remote(
        back_out, back_in, back_sems.at[0], back_sems.at[1], device_of(z, x, core, 0)
    )

    def key_value_rows(columns):
        value = mm(held[3][:, columns].T, weights_kv[:, :D], NT)
        return value + mm(held[4][:, columns].T, weights_kv[:, D:], NT)

    def rows_before():
        late[0].wait()
        back_out[...] = key_value_rows(slice(0, split)).astype(bf16)

        @pl.when(y == 1)
        def _():
            back.start()

    def rows_here():
        late[1].wait()
        late[2].wait()
        late[3].wait()
        grad = key_value_rows(slice(split, 2 * split)) + mm(held[2][...], weights_q[...], NT)
        add_rows(grad)

    def add_rows(grad):
        value = rows_held[...].astype(f32)
        grad_ref[...] += norm_back(value, inverse_rms(value), gain_ref[...], grad)

    def rows_back():
        @pl.when(y == 0)
        def _():
            arrived(back_in, back_sems.at[1])
            add_rows(back_in[...].astype(f32))

        @pl.when(y == 1)
        def _():
            back.wait_send()

    make(0)
    make(1)
    send_first(0)
    make(2)
    send_first(1)
    send_second(0)
    line_self(0)
    make(3)
    for copy in late:
        copy.start()
    send_first(2)
    send_second(1)
    line_self(1)
    line_cross(0)
    send_first(3)
    rows_before()
    send_second(2)
    line_self(2)
    line_cross(1)
    send_second(3)
    line_cross(2)
    rows_here()
    last_self()
    line_cross(3)
    from_line(1, 0, lambda value: put(1, value, True))
    arrived(second_in[0].at[3], second_recv.at[0, 3])
    put(0, wide(second_in[0], 3), True)
    rows_back()

    for which in (0, 1):
        for i in range(4):
            for first, second in every:
                to_mate(which, i, first, second).wait_send()
            for second in (0, 1):
                to_first(which, i, second).wait_send()
            if which == 1 or i == 3:
                to_second(which, i).wait_send()
            if i < 3:
                for second in (0, 1)[: 2 - which]:
                    along_line(which, i, second)[1].wait_send()


def scatter_products(self_arrays, cross_arrays, small, weights, tokens, resid, gain):
    counts = (len(self_arrays), len(cross_arrays))
    arrays = (*self_arrays, *cross_arrays)
    shard = small.shape[1]
    shapes = [(shard, 4 * D + small.shape[2]), (shard, 4 * D)]
    dma = pltpu.SemaphoreType.DMA

    def buffers(slots):
        return [pltpu.VMEM((slots, *shape), bf16) for shape in shapes]

    return pl.pallas_call(
        functools.partial(scatter_body, counts),
        in_specs=[pl.BlockSpec(memory_space=pl.ANY)] * (len(arrays) + 4)
        + [pl.BlockSpec(memory_space=pltpu.VMEM)],
        out_specs=[pl.BlockSpec(memory_space=pltpu.VMEM)] * 6,
        out_shape=[
            jax.ShapeDtypeStruct(shape, f32)
            for shape in ((3, shard, D), (shard, D), (3, shard, D), (shard, D), (shard, small.shape[2]), resid.shape)
        ],
        scratch_shapes=[pltpu.VMEM(array.shape, array.dtype) for array in (*arrays, small)]
        + buffers(32)
        + buffers(16)
        + buffers(8)
        + buffers(4)
        + [pltpu.VMEM((16 - 8 * i, *shape), bf16) for i, shape in enumerate(shapes)]
        + [
            dma((len(arrays) + 1,)),
            dma((2, 16)),
            dma((2, 8)),
            dma((2, 4)),
            dma((2, 6)),
            dma((2, 16)),
            dma((2, 8)),
            dma((2, 4)),
            dma((2, 16)),
            pltpu.VMEM(tokens.shape, bf16),
            dma((2,)),
            dma((4,)),
        ],
        compiler_params=pltpu.CompilerParams(
            collective_id=1, has_side_effects=True, vmem_limit_bytes=60 << 20
        ),
        name="scatter_products",
    )(*arrays, small, weights, tokens, resid, gain)


def gelu_and_slope(value):
    upper = 0.5 * (1.0 + lax.erf(value * math.sqrt(0.5)))
    density = jnp.exp(-0.5 * value * value) * (1.0 / math.sqrt(2.0 * math.pi))
    return value * upper, upper + value * density


def feed_forward_body(rows, *refs):
    x1_ref, mixed_ref, out_ref, gain_ref, grad_ref, in_ref, back_ref = refs[:7]
    layer_ref, dx_ref, low_ref, mixed_back_ref, weight_ref = refs[7:12]
    x2, h3, h3_t, total, back, act = refs[12:]
    step, part = pl.program_id(0), pl.program_id(1)
    first = jnp.logical_and(step == 0, part == 0)
    last = jnp.logical_and(step == pl.num_programs(0) - 1, part == 1)

    @pl.when(first)
    def _():
        value = x1_ref[...] + mm(mixed_ref[...], out_ref[...])
        x2[...] = value
        normed = (value * inverse_rms(value) * gain_ref[...]).astype(bf16)
        h3[...] = normed
        h3_t[...] = normed.T
        total[...] = value
        back[...] = jnp.zeros_like(back)

    @pl.when(part == 0)
    def _():
        hidden, slope = gelu_and_slope(mm(h3[...], in_ref[...]))
        hidden = hidden.astype(bf16)
        act[...] = hidden
        total[...] += mm(hidden, back_ref[...])
        grad_pre = (slope * mm(grad_ref[...], back_ref[...], NT)).astype(bf16)
        back[...] += mm(grad_pre, in_ref[...], NT)
        weight_ref[...] = mm(h3_t[...], grad_pre).astype(bf16)

    @pl.when(part == 1)
    def _():
        weight_ref[...] = mm(act[...].T, grad_ref[...]).astype(bf16)

    @pl.when(last)
    def _():
        layer_ref[...] = total[...].astype(bf16)
        value = x2[...]
        grad = grad_ref[...].astype(f32)
        grad = grad + norm_back(value, inverse_rms(value), gain_ref[...], back[...])
        dx_ref[...] = grad
        low = grad.astype(bf16)
        low_ref[...] = low
        mixed_back_ref[...] = mm(low, out_ref[...], NT).astype(bf16)


def feed_forward(resid, mixed, all_cross, gain, grad_out, all_ffn):
    rows = resid.shape[0]
    units = FF // D

    def whole(height):
        return pl.BlockSpec((height, D), lambda j, s: (0, 0))

    rows_f32 = jax.ShapeDtypeStruct((rows, D), f32)
    rows_bf16 = jax.ShapeDtypeStruct((rows, D), bf16)
    return pl.pallas_call(
        functools.partial(feed_forward_body, rows),
        grid=(units, 2),
        in_specs=[
            whole(rows),
            whole(rows),
            pl.BlockSpec((D, D), lambda j, s: (0, 3)),
            whole(1),
            whole(rows),
            pl.BlockSpec((D, D), lambda j, s: (0, j)),
            pl.BlockSpec((D, D), lambda j, s: (0, units + j)),
        ],
        out_specs=[
            whole(rows),
            whole(rows),
            whole(rows),
            whole(rows),
            pl.BlockSpec((D, D), lambda j, s: (0, s * units + j)),
        ],
        out_shape=[
            rows_bf16,
            rows_f32,
            rows_bf16,
            rows_bf16,
            jax.ShapeDtypeStruct((D, 2 * FF), bf16),
        ],
        scratch_shapes=[
            pltpu.VMEM((rows, D), f32),
            pltpu.VMEM((rows, D), bf16),
            pltpu.VMEM((D, rows), bf16),
            pltpu.VMEM((rows, D), f32),
            pltpu.VMEM((rows, D), f32),
            pltpu.VMEM((rows, D), bf16),
        ],
        compiler_params=pltpu.CompilerParams(vmem_limit_bytes=48 << 20),
        name="feed_forward",
    )(resid, mixed, all_cross, gain[None], grad_out, all_ffn, all_ffn)


def bias_matrices():
    place = np.arange(256)
    distance = np.where(place <= 128, 128 - place, 384 - place)
    edges = np.array(bucket_edges)
    buckets = np.where(distance < 16, distance, 16 + (distance[:, None] >= edges).sum(axis=1))
    spread = np.zeros((2, 2, BUCKETS, 2, 2, 256), np.float32)
    columns = np.zeros((2, 2, BUCKETS, 128), np.float32)
    sums = np.zeros((2, 2, 128, 2, 2, BUCKETS), np.float32)
    for which in (0, 1):
        for flag in (0, 1):
            spread[which, flag, buckets, which, flag, place] += 1.0
            spread[which, flag, BUCKETS - 1, which, flag, :] -= 1.0
            base = (HDIM if which == 0 else 0) + 3 + 2 * flag
            columns[which, flag, BUCKETS - 1, base : base + 2] = 1.0
            sums[which, flag, HDIM if which == 0 else 0, which, flag, BUCKETS - 1] = 1.0
    spread = spread.reshape(128, 1024)
    forward = np.concatenate((spread, columns.reshape(128, 128)), axis=1)
    backward = np.concatenate((spread.T, sums.reshape(512, 128)), axis=0)
    return forward, backward


def bias_parts(table_low):
    place = np.arange(2 * BUCKETS * HEADS)
    code, head = place // HEADS, place % HEADS
    chosen = (head // 2 == np.arange(PAIRS)[:, None]).astype(np.float32)
    spread = bias_matrices()[0][(head % 2) * 2 * BUCKETS + code]
    both = mm(jnp.asarray(chosen, bf16), table_low * jnp.asarray(spread, bf16)) * LOG2E
    far = both[:, 1024:]
    high = far.astype(bf16)
    rest = (far - high.astype(f32)).astype(bf16)
    odd = lax.broadcasted_iota(jnp.int32, (1, 128), 1) % 2 == 1
    return jnp.where(odd, high, rest).reshape(PAIRS, 1, 128), both[:, :1024].reshape(PAIRS, 4, 256)


def table_gradient(near_sums, row_sums):
    both = jnp.concatenate((near_sums.reshape(PAIRS, -1), row_sums.reshape(PAIRS, -1)), axis=1)
    matrix = jnp.asarray(bias_matrices()[1], f32)
    by_pair = jnp.dot(both, matrix, precision=lax.Precision.HIGHEST, preferred_element_type=f32)
    return by_pair.reshape(HEADS, 2 * BUCKETS).T.reshape(-1)


def seq_shift(array, count):
    length = array.shape[0]
    return lax.dynamic_slice_in_dim(jnp.concatenate((array, array), axis=0), count, length, axis=0)


def others_rows(rows, own_last):
    parts = lax.axis_size("seq")
    if parts == 2:
        return lax.ppermute(rows, "seq", [(0, 1)] if own_last else [(0, 1), (1, 0)])
    whole = lax.all_gather(rows, "seq", axis=0, tiled=True)
    step = rows.shape[0]
    start = lax.rem(lax.axis_index("seq") + 1, parts) * step
    return seq_shift(whole, start)[: (parts - 1) * step]


def to_owners(grads, own_last):
    parts = lax.axis_size("seq")
    if parts == 2:
        return lax.ppermute(grads, "seq", [(1, 0)] if own_last else [(0, 1), (1, 0)])
    step = grads.shape[0] // (parts - 1)
    whole = jnp.concatenate((grads, jnp.zeros((step, grads.shape[1]), grads.dtype)), axis=0)
    start = lax.rem(parts - 1 - lax.axis_index("seq"), parts) * step
    return lax.psum_scatter(seq_shift(whole, start), "seq", scatter_dimension=0, tiled=True)


def on_device(
    decoder_in,
    encoder_out,
    dec_lengths,
    pair_flags,
    enc_segments,
    self_proj,
    self_out,
    cross_proj,
    cross_out,
    ffn_in,
    ffn_out,
    norm_gains,
    rel_table,
    out_grad,
):
    shard = self_out.shape[0]
    units = FF // D
    own_kernels = (lax.axis_size("dp"), lax.axis_size("seq")) == (16, 2)
    if own_kernels:
        all_self, all_cross, pair_ffn = gather_blocks(
            self_proj, self_out, cross_proj, cross_out, ffn_in, ffn_out, norm_gains, rel_table
        )
        all_self = all_self.reshape(-1, all_self.shape[2])
        all_cross = all_cross.reshape(-1, all_cross.shape[2])
        pair_ffn = pair_ffn.reshape(2 * shard, 2 * FF)
        all_ffn = lax.all_gather(pair_ffn, "dp", axis=0, tiled=True)
    else:
        small = jnp.concatenate((norm_gains, rel_table[None]), axis=0).T
        small = jnp.pad(small, ((0, 0), (0, 124)))
        block_self = jnp.concatenate((*self_proj, self_out, small), axis=1).astype(bf16)
        block_cross = jnp.concatenate((*cross_proj, cross_out), axis=1).astype(bf16)
        ffn_in_here = jnp.swapaxes(ffn_in.reshape(shard, D, units), 1, 2).reshape(shard, FF)
        block_ffn = jnp.concatenate((ffn_in_here, ffn_out.reshape(shard, FF)), axis=1).astype(bf16)
        all_self = lax.all_gather(block_self, BOTH, axis=0, tiled=True)
        all_cross = lax.all_gather(block_cross, BOTH, axis=0, tiled=True)
        all_ffn = lax.all_gather(block_ffn, BOTH, axis=0, tiled=True)
    encoder_out = lax.optimization_barrier((encoder_out, all_cross))[0]
    self_q, self_k, self_v, out_self = (all_self[:, i * D : (i + 1) * D] for i in range(4))
    cross_q, cross_k, cross_v = (all_cross[:, i * D : (i + 1) * D] for i in range(3))
    small_all = all_self[:, 4 * D :]
    gains = small_all[:, :3].T.astype(f32)
    far_lanes, near_lines = bias_parts(small_all[:, 3:4])

    tokens = decoder_in[0]
    memory = encoder_out[0]
    grad_out = out_grad[0]
    rows, enc_rows = tokens.shape[0], memory.shape[0]
    seq_count = lax.axis_size("seq")
    seq_index = lax.axis_index("seq")
    keys, enc_keys = rows * seq_count, enc_rows * seq_count

    numbers = (dec_lengths, pair_flags)
    before = others_rows(tokens, True)
    others = others_rows(memory, False)

    scale = 0.125 * LOG2E
    tokens = tokens.astype(f32)
    inverse_one = inverse_rms(tokens)
    normed_one = (tokens * inverse_one * gains[0]).astype(bf16)
    before = before.astype(f32)
    normed_before = (before * inverse_rms(before) * gains[0]).astype(bf16)
    query_one = (mm(normed_one, self_q) * scale).astype(bf16)
    kv_one = mm(normed_one, all_self[:, D : 3 * D]).astype(bf16)
    kv_before = mm(normed_before, all_self[:, D : 3 * D]).astype(bf16)
    parts_one = ((kv_before, 0, PAIRS), (kv_one, 0, PAIRS))
    mixed_one, weights_one, total_one = attend(
        numbers, rows, query_one, parts_one, far=far_lanes, near=near_lines
    )
    resid_one = tokens + mm(mixed_one, out_self)
    inverse_two = inverse_rms(resid_one)
    normed_two = (resid_one * inverse_two * gains[1]).astype(bf16)
    query_two = (mm(normed_two, cross_q) * scale).astype(bf16)
    kv_memory = mm(memory, all_cross[:, D : 3 * D]).astype(bf16)
    kv_others = mm(others, all_cross[:, D : 3 * D]).astype(bf16)
    parts_two = ((kv_memory, 0, PAIRS), (kv_others, 0, PAIRS))
    mixed_two, weights_two, total_two = attend(numbers, rows, query_two, parts_two, segments=enc_segments)
    layer_out, grad_resid, grad_low_two, grad_mixed, grad_ffn = feed_forward(
        resid_one, mixed_two, all_cross, gains[2], grad_out, all_ffn
    )

    grad_query, grad_key, grad_value = attend_back(
        numbers, query_two, parts_two, weights_two, mixed_two, total_two, grad_mixed, False
    )
    turned = (((0,), (1,)), ((), ()))
    kv_other = mm(grad_key[:, enc_rows:], cross_k, turned)
    kv_other = (kv_other + mm(grad_value[:, enc_rows:], cross_v, turned)).astype(bf16)
    grad_memory = mm(grad_key[:, :enc_rows], cross_k, turned)
    grad_memory = grad_memory + mm(grad_value[:, :enc_rows], cross_v, turned)
    grad_two = (grad_query, grad_key, grad_value)
    grad_normed = mm(grad_query, cross_q, NT)
    grad_resid = grad_resid + norm_back(resid_one, inverse_two, gains[1], grad_normed)
    grad_low = grad_resid.astype(bf16)
    grad_mixed = mm(grad_low, out_self, NT).astype(bf16)
    grad_mixed, kv_other = lax.optimization_barrier((grad_mixed, kv_other))
    grad_query, grad_key, grad_value, near_sums, row_sums = attend_back(
        numbers, query_one, parts_one, weights_one, mixed_one, total_one, grad_mixed, True
    )
    grad_others = to_owners(kv_other, False)
    table_grad = table_gradient(near_sums, row_sums)
    small = jnp.broadcast_to(table_grad[:, None], (D, 128)).astype(bf16)

    def owned(array):
        return lax.psum_scatter(array, BOTH, scatter_dimension=0, tiled=True).astype(f32)

    def projections(block):
        return jnp.stack([block[:, i * D : (i + 1) * D] for i in range(3)], axis=0)

    if own_kernels:
        own_self, own_self_out, own_cross, own_cross_out, own_small, grad_input = scatter_products(
            (normed_before, normed_one, grad_query, grad_key, grad_value, mixed_one, grad_low),
            (normed_two, grad_two[0], memory, others, grad_two[1], grad_two[2], mixed_two, grad_low_two),
            small.reshape(-1, shard, small.shape[1]),
            all_self,
            decoder_in[0],
            grad_resid,
            gains[:1],
        )
    else:
        normed_all = jnp.concatenate((normed_before, normed_one), axis=0)
        memory_all = jnp.concatenate((memory, others), axis=0)
        self_grads = (
            mm(normed_one, grad_query, TN),
            mm(normed_all, grad_key, turned),
            mm(normed_all, grad_value, turned),
            mm(mixed_one, grad_low, TN),
        )
        cross_grads = (
            mm(normed_two, grad_two[0], TN),
            mm(memory_all, grad_two[1], turned),
            mm(memory_all, grad_two[2], turned),
            mm(mixed_two, grad_low_two, TN),
        )
        self_grads = jnp.concatenate(self_grads, axis=1).astype(bf16)
        block = owned(jnp.concatenate((self_grads, small), axis=1))
        own_self, own_self_out = projections(block), block[:, 3 * D : 4 * D]
        own_small = block[:, 4 * D :]
        block = owned(jnp.concatenate(cross_grads, axis=1).astype(bf16))
        own_cross, own_cross_out = projections(block), block[:, 3 * D :]
        split = keys - rows
        grad_before = mm(grad_key[:, :split], self_k, turned) + mm(grad_value[:, :split], self_v, turned)
        grad_before = to_owners(grad_before.astype(bf16), True)
        grad_normed = mm(grad_key[:, split:], self_k, turned) + mm(grad_value[:, split:], self_v, turned)
        grad_normed = grad_normed + mm(grad_query, self_q, NT) + grad_before.astype(f32)
        grad_input = grad_resid + norm_back(tokens, inverse_one, gains[0], grad_normed)

    grad_others, own_small = lax.optimization_barrier((grad_others, own_small))
    grad_encoder = grad_memory + grad_others.astype(f32)
    own_ffn = owned(grad_ffn)
    own_ffn_in = jnp.swapaxes(own_ffn[:, :FF].reshape(shard, units, D), 1, 2).reshape(shard, FF)
    own_ffn_out = own_ffn[:, FF:].reshape(ffn_out.shape)

    def products(weight, grad):
        return jnp.sum(weight.astype(bf16).astype(f32) * grad, axis=-1)

    gain_grads = jnp.stack(
        (
            jnp.sum(products(self_proj, own_self), axis=0),
            products(cross_proj[0], own_cross[0]),
            products(ffn_in, own_ffn_in),
        ),
        axis=0,
    )
    gain_grads = gain_grads / norm_gains.astype(bf16).astype(f32)

    return (
        layer_out[None],
        grad_input[None],
        grad_encoder[None],
        own_self,
        own_self_out,
        own_cross,
        own_cross_out,
        own_ffn_in,
        own_ffn_out,
        gain_grads,
        own_small[:, 0],
    )


def solution(mesh):
    hidden = P("dp", "seq", None)
    rows_split = P(BOTH, None)
    stacked = P(None, BOTH, None)
    stream = P("dp", None)
    return jax.shard_map(
        on_device,
        mesh=mesh,
        in_specs=(
            hidden,
            hidden,
            stream,
            stream,
            stream,
            stacked,
            rows_split,
            stacked,
            rows_split,
            rows_split,
            rows_split,
            P(None, BOTH),
            P(BOTH),
            hidden,
        ),
        out_specs=(
            hidden,
            hidden,
            hidden,
            stacked,
            rows_split,
            stacked,
            rows_split,
            rows_split,
            rows_split,
            P(None, BOTH),
            P(BOTH),
        ),
        check_vma=False,
    )
```

```python
import functools
import math

import jax
import jax.numpy as jnp
import numpy as np
from jax import lax
from jax.experimental import pallas as pl
from jax.experimental.pallas import tpu as pltpu
from jax.sharding import PartitionSpec as P

D = 768
HEADS = 12
HDIM = 64
FF = 3072
BUCKETS = 32
PAIRS = HEADS // 2
LOG2E = math.log2(math.e)
LN2 = math.log(2.0)
epsilon = 1e-06
neg_large = -1e30
bucket_edges = (19, 21, 24, 27, 31, 35, 40, 46, 52, 59, 67, 77, 87, 99, 113)
f32 = jnp.float32
bf16 = jnp.bfloat16
NT = (((1,), (1,)), ((), ()))
NN = (((1,), (0,)), ((), ()))
TN = (((0,), (0,)), ((), ()))
BOTH = ("dp", "seq")
MESH = pl.DeviceIdType.MESH


def mm(a, b, dims=NN):
    return lax.dot_general(a, b, dims, preferred_element_type=f32)


def inverse_rms(values):
    return lax.rsqrt(jnp.mean(values * values, axis=-1, keepdims=True) + epsilon)


def norm_back(values, inverse, gain, grad):
    unit = values * inverse
    grad = grad * gain
    return inverse * (grad - unit * jnp.mean(grad * unit, axis=-1, keepdims=True))


def head_lanes(which):
    low = lax.broadcasted_iota(jnp.int32, (1, 128), 1) < HDIM
    return low if which == 0 else jnp.logical_not(low)


def row_chunks(rows, keys, causal, step):
    return [
        (slice(i, i + step), (keys - rows + i + step) if causal else keys)
        for i in range(0, rows, step)
    ]


def near_bias(near_ref, which):
    row = lax.broadcasted_iota(jnp.int32, (128, 256), 0)
    column = lax.broadcasted_iota(jnp.int32, (128, 256), 1)
    tiles = []
    for flag in (0, 1):
        line = near_ref[0, 2 * which + flag : 2 * which + flag + 1, :]
        tile = pltpu.roll(jnp.broadcast_to(line, (128, 256)), 0, 1, stride=1, stride_axis=0)
        tiles.append(jnp.where(column - row > 128, neg_large, tile))
    return tiles


def diagonal_sums(tile):
    for step in (64, 32, 16, 8):
        tile = tile[:step] + pltpu.roll(tile[step:], 256 - step, 1)
    row = lax.broadcasted_iota(jnp.int32, (8, 256), 0)
    for step in (4, 2, 1):
        tile = jnp.where((row & step) != 0, pltpu.roll(tile, 256 - step, 1), tile)
    return jnp.sum(tile, axis=0, keepdims=True)


def pairs_between(place, end_one, end_two):
    return (place >= end_one).astype(jnp.int32) + (place >= end_two).astype(jnp.int32)


def decoder_pairs(lengths, place):
    return pairs_between(place, lengths[0, 0], lengths[0, 0] + lengths[0, 1])


def flagged(numbers, rows, first, count, width):
    lengths, flags = numbers
    place = lax.broadcasted_iota(jnp.int32, (count, width), 0)
    pair = decoder_pairs(lengths, place + (lax.axis_index("seq") * rows + first))
    return jnp.where(pair == 0, flags[0, 0], jnp.where(pair == 1, flags[0, 1], 0)) > 0


def extra_columns(numbers, rows, keys, segments, query_extra, key_extra):
    lengths = numbers[0]
    here = lax.axis_index("seq") * rows
    lane = lax.broadcasted_iota(jnp.int32, (rows, 128), 1) & (HDIM - 1)
    pair = decoder_pairs(lengths, lax.broadcasted_iota(jnp.int32, (rows, 128), 0) + here)
    flag = flagged(numbers, rows, 0, rows, 128).astype(jnp.int32)
    wanted = jnp.where(lane < 3, pair, (flag << 1) + 3)
    chosen = jnp.where(lane < 3, lane, ((lane - 3) & ~1) + 3)
    fits = jnp.logical_and(wanted == chosen, lane < 7)
    query_extra[...] = jnp.where(fits, 1.0, 0.0).astype(bf16)
    lane = lax.broadcasted_iota(jnp.int32, (keys, 128), 1) & (HDIM - 1)
    place = lax.broadcasted_iota(jnp.int32, (keys, 128), 0)
    if segments is None:
        place = place + (here + rows - keys)
        pair = jnp.where(place < 0, 3, decoder_pairs(lengths, place))
    else:
        place = place + lax.axis_index("seq") * (keys // lax.axis_size("seq"))
        place = jnp.where(place >= keys, place - keys, place)

        def below(pair):
            count = jnp.sum((segments[...] < pair).astype(f32), axis=0, keepdims=True)
            return jnp.sum(count, axis=1, keepdims=True).astype(jnp.int32)

        pair = pairs_between(place, below(1), below(2))
    wrong = jnp.logical_and(pair != lane, lane < 3)
    key_extra[...] = jnp.where(wrong, neg_large, 0.0).astype(bf16)


def attend_body(rows, keys, causal, step, parts, *refs):
    numbers, q_ref = refs[:2], refs[2]
    key_refs, value_refs = refs[3 : 3 + parts], refs[3 + parts : 3 + 2 * parts]
    o_ref, e_ref, inv_ref, query_extra, key_extra = refs[-5:]

    @pl.when(pl.program_id(0) == 0)
    def _():
        segments = None if causal else refs[3 + 2 * parts]
        extra_columns(numbers, rows, keys, segments, query_extra, key_extra)

    extra = key_extra[...]
    if causal:
        far_ref, near_ref = refs[3 + 2 * parts : 5 + 2 * parts]
        extra = extra + far_ref[0]
    key_pair = jnp.concatenate([ref[...] for ref in key_refs], axis=0)
    value_pair = jnp.concatenate([ref[...] for ref in value_refs], axis=0)
    chunks = row_chunks(rows, keys, causal, step)
    found = []
    for which in (0, 1):
        mine = head_lanes(which)
        key_head = jnp.where(mine, key_pair, extra)
        value_head = jnp.where(mine, value_pair, jnp.ones_like(value_pair))
        if causal:
            tile_zero, tile_one = near_bias(near_ref, which)
        done = []
        for here, width in chunks:
            query = jnp.where(mine, q_ref[here], query_extra[here])
            scores = mm(query, key_head[:width], NT)
            if causal:
                cut = width - 256
                flag = flagged(numbers, rows, here.start, step, 1)
                near = scores[:, cut:] + jnp.where(flag, tile_one, tile_zero)
                far = scores[:, :cut]
                peak = jnp.maximum(
                    jnp.max(far, axis=1, keepdims=True), jnp.max(near, axis=1, keepdims=True)
                )
                near = jnp.exp2(near - peak).astype(bf16)
                far = jnp.exp2(far - peak).astype(bf16)
                e_ref[which, here, :cut] = far
                e_ref[which, here, cut:width] = near
                mixed = mm(far, value_head[:cut]) + mm(near, value_head[cut:width])
            else:
                peak = jnp.max(scores, axis=1, keepdims=True)
                weights = jnp.exp2(scores - peak).astype(bf16)
                e_ref[which, here, :] = weights
                mixed = mm(weights, value_head)
            total = mixed[:, HDIM : HDIM + 1] if which == 0 else mixed[:, 0:1]
            inverse = 1.0 / total
            done.append((mixed * inverse, jnp.broadcast_to(inverse, mixed.shape)))
        found.append(done)
    low = head_lanes(0)
    for index, (here, _) in enumerate(chunks):
        o_ref[here] = jnp.where(low, found[0][index][0], found[1][index][0]).astype(bf16)
        inv_ref[here] = jnp.where(low, found[0][index][1], found[1][index][1])


def pair_columns(rows, first=0):
    return pl.BlockSpec((rows, 128), lambda p: (0, first + p))


def operands_of(numbers, query, parts):
    arrays = [*numbers, query] + [part[0] for part in parts] * 2
    specs = [pl.BlockSpec(memory_space=pltpu.SMEM)] * 2 + [pair_columns(query.shape[0])]
    for place in (1, 2):
        specs += [pair_columns(part[0].shape[0], part[place]) for part in parts]
    return arrays, specs


def per_pair(height, width):
    return pl.BlockSpec((1, height, width), lambda p: (p, 0, 0))


def attend(numbers, rows, query, parts, segments=None, far=None, near=None):
    keys = sum(part[0].shape[0] for part in parts)
    causal = far is not None
    step = 128 if causal else min(256, rows)
    operands, specs = operands_of(numbers, query, parts)
    if causal:
        operands += [far, near]
        specs += [per_pair(1, 128), per_pair(4, 256)]
    else:
        operands.append(segments)
        specs.append(pl.BlockSpec(segments.shape, lambda p: (0, 0)))
    return pl.pallas_call(
        functools.partial(attend_body, rows, keys, causal, step, len(parts)),
        grid=(PAIRS,),
        in_specs=specs,
        out_specs=(
            pair_columns(rows),
            pl.BlockSpec((2, rows, keys), lambda p: (p, 0, 0)),
            pair_columns(rows),
        ),
        out_shape=(
            jax.ShapeDtypeStruct((rows, D), bf16),
            jax.ShapeDtypeStruct((HEADS, rows, keys), bf16),
            jax.ShapeDtypeStruct((rows, D), f32),
        ),
        scratch_shapes=[pltpu.VMEM((rows, 128), bf16), pltpu.VMEM((keys, 128), bf16)],
        compiler_params=pltpu.CompilerParams(vmem_limit_bytes=56 << 20),
        name="attend_causal" if causal else "attend_cross",
    )(*operands)


def attend_back_body(rows, keys, causal, step, parts, *refs):
    numbers, q_ref = refs[:2], refs[2]
    refs = refs[3:]
    key_refs, value_refs = refs[:parts], refs[parts : 2 * parts]
    e_ref, o_ref, inv_ref, d_ref = refs[2 * parts : 4 + 2 * parts]
    if causal:
        dq_ref, dk_ref, dv_ref, near_ref, sum_ref, ds_ref = refs[4 + 2 * parts :]
    else:
        dq_ref, dk_ref, dv_ref, ds_ref = refs[4 + 2 * parts :]
    lane = lax.broadcasted_iota(jnp.int32, (1, 128), 1)
    key_pair = jnp.concatenate([ref[...] for ref in key_refs], axis=0)
    value_pair = jnp.concatenate([ref[...] for ref in value_refs], axis=0)
    scaled = (d_ref[...].astype(f32) * inv_ref[...]).astype(bf16)
    product = scaled.astype(f32) * o_ref[...].astype(f32)
    scaled_t = scaled.T
    query_t = q_ref[...].T
    chunks = row_chunks(rows, keys, causal, step)
    query_parts = []
    for which in (0, 1):
        mine = head_lanes(which)
        base = HDIM if which == 0 else 0
        value_head = jnp.where(mine, value_pair, jnp.ones_like(value_pair))
        key_head = jnp.where(mine, key_pair, jnp.ones_like(key_pair))
        delta = jnp.sum(jnp.where(mine, product, 0.0), axis=1, keepdims=True)
        high = delta.astype(bf16)
        rest = (delta - high.astype(f32)).astype(bf16)
        extra = jnp.where(
            lane == base, -high, jnp.where(lane == base + 1, -rest, jnp.zeros_like(rest))
        )
        grad_head = jnp.where(mine, scaled, extra)
        done = []
        if causal:
            near_all = jnp.zeros((128, 256), f32)
            near_one = jnp.zeros((128, 256), f32)
        for here, width in chunks:
            centred = mm(grad_head[here], value_head[:width], NT)
            grad_scores = e_ref[which, here, :width].astype(f32) * centred
            if causal:
                near = grad_scores[:, width - 256 :]
                near_all = near_all + near
                flag = flagged(numbers, rows, here.start, step, 1)
                near_one = near_one + jnp.where(flag, near, 0.0)
            grad_scores = grad_scores.astype(bf16)
            ds_ref[here, :width] = grad_scores
            done.append(mm(grad_scores, key_head[:width]))
        query_parts.append(done)
        half = slice(HDIM * which, HDIM * which + HDIM)
        if causal:
            spans = [(slice(0, keys - rows), 0)] if keys > rows else []
            spans += [
                (slice(keys - rows + i, keys - rows + i + step), i) for i in range(0, rows, step)
            ]
        else:
            spans = [(slice(0, keys), 0)]
        for span, first in spans:
            grad_key = mm(query_t[half, first:], ds_ref[first:, span])
            dk_ref[half, span] = (grad_key * LN2).astype(dk_ref.dtype)
            grad_value = mm(scaled_t[half, first:], e_ref[which, first:, span])
            dv_ref[half, span] = grad_value.astype(dv_ref.dtype)
        if causal:
            for flag, tile in ((0, near_all - near_one), (1, near_one)):
                near_ref[0, 2 * which + flag : 2 * which + flag + 1, :] = diagonal_sums(tile)
    low = head_lanes(0)
    for index, (here, _) in enumerate(chunks):
        both = jnp.where(low, query_parts[0][index], query_parts[1][index])
        dq_ref[here] = (both * 0.125).astype(dq_ref.dtype)
    if causal:
        flags = flagged(numbers, rows, 0, rows, 1)
        for which in (0, 1):
            whole = jnp.concatenate(query_parts[which], axis=0)
            one = jnp.sum(jnp.where(flags, whole, 0.0), axis=0, keepdims=True)
            every = jnp.sum(whole, axis=0, keepdims=True)
            sum_ref[0, 2 * which : 2 * which + 1, :] = every - one
            sum_ref[0, 2 * which + 1 : 2 * which + 2, :] = one


def attend_back(numbers, query, parts, weights, mixed, inverse, grad_mixed, causal):
    rows, keys = weights.shape[1:]
    step = 128 if causal else min(256, rows)
    operands, specs = operands_of(numbers, query, parts)
    operands += [weights, mixed, inverse, grad_mixed]
    specs += [pl.BlockSpec((2, rows, keys), lambda p: (p, 0, 0))] + [pair_columns(rows)] * 3
    turned = jax.ShapeDtypeStruct((D, keys), bf16)
    turned_spec = pl.BlockSpec((128, keys), lambda p: (p, 0))
    shapes = [jax.ShapeDtypeStruct((rows, D), bf16), turned, turned]
    out_specs = [pair_columns(rows), turned_spec, turned_spec]
    if causal:
        shapes += [
            jax.ShapeDtypeStruct((PAIRS, 4, 256), f32),
            jax.ShapeDtypeStruct((PAIRS, 4, 128), f32),
        ]
        out_specs += [per_pair(4, 256), per_pair(4, 128)]
    return pl.pallas_call(
        functools.partial(attend_back_body, rows, keys, causal, step, len(parts)),
        grid=(PAIRS,),
        in_specs=specs,
        out_specs=tuple(out_specs),
        out_shape=tuple(shapes),
        scratch_shapes=[pltpu.VMEM((rows, keys), bf16)],
        compiler_params=pltpu.CompilerParams(vmem_limit_bytes=56 << 20),
        name="attend_causal_back" if causal else "attend_cross_back",
    )(*operands)


def place_here():
    index = lax.axis_index("dp")
    return index // 4, (index // 2) % 2, index % 2, lax.axis_index("seq")


def block_of(z, x, core, y):
    return ((z * 2 + x) * 2 + core) * 2 + y


def device_of(z, x, core, y):
    return ((z * 2 + x) * 2 + core, y)


def greet_neighbours(z, x, core, y):
    barrier = pltpu.get_barrier_semaphore()

    def greet(device):
        pl.semaphore_signal(barrier, inc=1, device_id=device, device_id_type=MESH)

    greet(device_of(z, x, 1 - core, y))
    greet(device_of(z, 1 - x, core, y))
    greet(device_of(z, x, core, 1 - y))

    @pl.when(z > 0)
    def _():
        greet(device_of(z - 1, x, core, y))

    @pl.when(z < 3)
    def _():
        greet(device_of(z + 1, x, core, y))

    pl.semaphore_wait(barrier, 4 + ((z + 1) // 2) % 2)


def unit_order():
    place = np.arange(512)
    return (place[:, None] == (place % 128) * 4 + place // 128).astype(np.float32)


def gather_body(*refs):
    masters, refs = refs[:9], refs[9:]
    wholes, pair_whole = refs[:2], refs[2]
    sources, pair_source = refs[3:5], refs[5]
    own_sems, mate_sems, recv_sems, pair_sems = refs[6:10]
    route_sems = dict(zip(("up", "down", "x", "y"), refs[10:]))
    self_proj, self_out, cross_proj, cross_out, ffn_in, ffn_out, norm_gains, table, order = masters
    count = 2
    shard = self_out.shape[0]
    for stacked, single, source in ((self_proj, self_out, sources[0]), (cross_proj, cross_out, sources[1])):
        for j in range(3):
            source[:, j * D : (j + 1) * D] = stacked[j].astype(bf16)
        source[:, 3 * D : 4 * D] = single[...].astype(bf16)
    lane = lax.broadcasted_iota(jnp.int32, (shard, 128), 1)
    row = lax.broadcasted_iota(jnp.int32, (shard, shard), 0)
    same = row == lax.broadcasted_iota(jnp.int32, (shard, shard), 1)
    small = jnp.zeros((shard, 128), f32)
    for j in range(4):
        line = norm_gains[j : j + 1] if j < 3 else table[...]
        column = jnp.sum(jnp.where(same, jnp.broadcast_to(line, same.shape), 0.0), axis=1, keepdims=True)
        small = jnp.where(lane == j, column, small)
    sources[0][:, 4 * D :] = small.astype(bf16)
    z, x, core, y = place_here()
    mate = device_of(z, x, 1 - core, y)
    me = block_of(z, x, core, y)
    greet_neighbours(z, x, core, y)

    routes = (("y", "z", "x"), ("z", "x", "y"))
    slots = {}

    def send(which, source, block, send_sem, device):
        return pltpu.make_async_remote_copy(
            src_ref=source,
            dst_ref=wholes[which].at[block],
            send_sem=send_sem,
            recv_sem=recv_sems.at[which, block],
            device_id=device,
            device_id_type=MESH,
        )

    def copies(which, far, up, dx, dy, source=None):
        at_z = z + far if up else z - far
        block = block_of(at_z, (x + dx) % 2, core, (y + dy) % 2)
        source = wholes[which].at[block] if source is None else source
        route = routes[which]
        moved = [axis for axis, steps in (("z", far), ("x", dx), ("y", dy)) if steps]
        last = max((route.index(axis) for axis in moved), default=-1)
        targets = []
        for axis in route[max(last, 0) :]:
            fresh = route.index(axis) > last
            if axis == "z" and (fresh or not up):
                targets.append((z < 3, "up", device_of(z + 1, x, core, y)))
            if axis == "z" and (fresh or up):
                targets.append((z > 0, "down", device_of(z - 1, x, core, y)))
            if axis == "x" and fresh:
                targets.append((None, "x", device_of(z, 1 - x, core, y)))
            if axis == "y" and fresh:
                targets.append((None, "y", device_of(z, x, core, 1 - y)))
        out = []
        for condition, kind, device in targets:
            taken = slots.setdefault((which, kind), {})
            slot = taken.setdefault((far, up, dx, dy), len(taken))
            out.append((condition, send(which, source, block, route_sems[kind].at[which, slot], device)))
        taken = slots.setdefault((which, "mate"), {})
        slot = taken.setdefault((far, up, dx, dy), len(taken))
        out.append((None, send(which, source, block, mate_sems.at[which, slot], mate)))
        return block, out

    def when(condition, action):
        if condition is None:
            action()
        else:
            pl.when(condition)(action)

    def exists(far, up):
        if far == 0:
            return None
        return z + far < 4 if up else z - far >= 0

    def onwards(which, far, up, dx, dy, source=None):
        def run():
            block, out = copies(which, far, up, dx, dy, source)
            if source is None:
                pltpu.make_async_copy(wholes[which].at[block], wholes[which].at[block], recv_sems.at[which, block]).wait()
            for condition, copy in out:
                when(condition, copy.start)

        when(exists(far, up), run)

    own = [
        pltpu.make_async_copy(sources[i], wholes[i].at[me], own_sems.at[i]) for i in range(count)
    ]
    own.append(pltpu.make_async_copy(pair_source, pair_whole.at[y], pair_sems.at[0]))
    pair = pltpu.make_async_remote_copy(
        src_ref=pair_source,
        dst_ref=pair_whole.at[y],
        send_sem=pair_sems.at[1],
        recv_sem=pair_sems.at[2],
        device_id=device_of(z, x, core, 1 - y),
        device_id_type=MESH,
    )
    for which in range(count):
        onwards(which, 0, False, 0, 0, sources[which])
    for copy in own[:count]:
        copy.start()
    units = FF // D
    for m in range(FF // 512):
        piece = mm(ffn_in[:, 512 * m : 512 * (m + 1)].astype(bf16), order[...]).astype(bf16)
        for b in range(units):
            first = b * D + 128 * m
            pair_source[:, first : first + 128] = piece[:, 128 * b : 128 * (b + 1)]
    row = lax.broadcasted_iota(jnp.int32, (shard, units * shard), 0) * units
    place = lax.broadcasted_iota(jnp.int32, (shard, units * shard), 1)
    held = ffn_out[...].astype(bf16)
    for b in range(units):
        rows = mm(jnp.where(row + b == place, 1.0, 0.0).astype(bf16), held)
        pair_source[:, FF + b * D : FF + (b + 1) * D] = rows.astype(bf16)
    own[count].start()
    pair.start()
    waves = [[] for _ in range(6)]
    for dx in (0, 1):
        for dy in (0, 1):
            for far in range(4):
                for up in (False, True):
                    if far == 0 and (up or (dx == 0 and dy == 0)):
                        continue
                    waves[far + dx + dy].append((far, up, dx, dy))
    for wave in waves:
        for far, up, dx, dy in wave:
            for which in range(count):
                onwards(which, far, up, dx, dy)
    for dx in (0, 1):
        for dy in (0, 1):
            for far in range(4):
                for up in (False, True):
                    if far == 0 and up:
                        continue
                    for which in range(count):

                        def finish(which=which, far=far, up=up, dx=dx, dy=dy):
                            at_z = z + far if up else z - far
                            block = block_of(at_z, (x + dx) % 2, 1 - core, (y + dy) % 2)
                            whole = wholes[which].at[block]
                            pltpu.make_async_copy(whole, whole, recv_sems.at[which, block]).wait()
                            source = sources[which] if (far, dx, dy) == (0, 0, 0) else None
                            _, out = copies(which, far, up, dx, dy, source)
                            for condition, copy in out:
                                when(condition, copy.wait_send)

                        when(exists(far, up), finish)
    for copy in own:
        copy.wait()
    pair.wait_send()
    came = pair_whole.at[1 - y]
    pltpu.make_async_copy(came, came, pair_sems.at[2]).wait()


def gather_blocks(self_proj, self_out, cross_proj, cross_out, ffn_in, ffn_out, norm_gains, rel_table):
    shard = self_out.shape[0]
    shapes = [(shard, 4 * D + 128), (shard, 4 * D)]
    pair = (shard, 2 * FF)
    dma = pltpu.SemaphoreType.DMA
    return pl.pallas_call(
        gather_body,
        in_specs=[pl.BlockSpec(memory_space=pltpu.VMEM)] * 9,
        out_specs=[pl.BlockSpec(memory_space=pl.ANY)] * 3,
        out_shape=[jax.ShapeDtypeStruct((32, *shape), bf16) for shape in shapes]
        + [jax.ShapeDtypeStruct((2, *pair), bf16)],
        scratch_shapes=[pltpu.VMEM(shape, bf16) for shape in (*shapes, pair)]
        + [dma((3,)), dma((2, 28)), dma((2, 32)), dma((3,))]
        + [dma((2, 16))] * 4,
        compiler_params=pltpu.CompilerParams(collective_id=0, has_side_effects=True),
        name="gather_blocks",
    )(
        self_proj,
        self_out,
        cross_proj,
        cross_out,
        ffn_in,
        ffn_out,
        norm_gains,
        rel_table[None],
        jnp.asarray(unit_order(), bf16),
    )


SELF_PRODUCTS = (((1,), 2, False), ((0, 1), 3, True), ((0, 1), 4, True), ((5,), 6, False))
CROSS_PRODUCTS = (((0,), 1, False), ((2, 3), 4, True), ((2, 3), 5, True), ((6,), 7, False))


def scatter_body(counts, *refs):
    total_in = sum(counts)
    arrays, small = refs[:total_in], refs[total_in]
    weights_ref, cross_ref, tokens_ref, resid_ref, gain_ref = refs[total_in + 1 : total_in + 6]
    refs = refs[total_in + 6 :]
    outs, grad_ref, memory_ref, refs = refs[:5], refs[5], refs[6], refs[7:]
    held, small_held = refs[:total_in], refs[total_in]
    refs = refs[total_in + 1 :]
    parts, mate_in, first_in, second_in, line_in = (refs[2 * i : 2 * i + 2] for i in range(5))
    load_sems, mate_sems, first_sems, second_sems, line_sems = refs[10:15]
    mate_recv, first_recv, second_recv, line_recv = refs[15:19]
    back_in, back_sems, late_sems, staged, staged_sems = refs[19:]
    z, x, core, y = place_here()
    loads = [
        pltpu.make_async_copy(source, target, load_sems.at[i])
        for i, (source, target) in enumerate(zip((*arrays, small), (*held, small_held)))
    ]
    for load in loads:
        load.start()
    greet_neighbours(z, x, core, y)
    half = z // 2
    order = (3 - 3 * half, 2 - half, 1 - z + 4 * half, z)

    def near(which, first, second):
        if which == 0:
            return (x + first) % 2, (y + second) % 2
        return (x + second) % 2, (y + first) % 2

    def block(which, i, first, second, other_core=0):
        bx, by = near(which, first, second)
        return block_of(order[i], bx, (core + other_core) % 2, by)

    def slot_of(which, i, first, second):
        bx, by = near(which, first, second)
        return (order[i] * 2 + bx) * 2 + by

    def remote(source, target, send_sem, recv_sem, device):
        return pltpu.make_async_remote_copy(
            src_ref=source,
            dst_ref=target,
            send_sem=send_sem,
            recv_sem=recv_sem,
            device_id=device,
            device_id_type=MESH,
        )

    def to_mate(which, i, first, second):
        slot = slot_of(which, i, first, second)
        return remote(
            parts[which].at[block(which, i, first, second, 1)],
            mate_in[which].at[slot],
            mate_sems.at[which, slot],
            mate_recv.at[which, slot],
            device_of(z, x, 1 - core, y),
        )

    def to_first(which, i, second):
        bx, by = near(which, 1, 0)
        return remote(
            parts[which].at[block(which, i, 1, second)],
            first_in[which].at[2 * i + second],
            first_sems.at[which, 2 * i + second],
            first_recv.at[which, 2 * i + second],
            device_of(z, bx, core, by),
        )

    def to_second(which, i):
        bx, by = near(which, 0, 1)
        return remote(
            parts[which].at[block(which, i, 0, 1)],
            second_in[which].at[i],
            second_sems.at[which, i],
            second_recv.at[which, i],
            device_of(z, bx, core, by),
        )

    def line_slot(which, came, at_z, second):
        return (came * 4 + at_z) * 2 + second if which == 0 else came * 4 + at_z

    def along_line(which, i, second=0):
        step = 1 - 2 * half if i < 2 else 1 - 2 * (z % 2)
        came = (1 - step) // 2
        slot = line_slot(which, came, order[i], second)
        return slot, remote(
            parts[which].at[block(which, i, 0, second)],
            line_in[which].at[slot],
            line_sems.at[which, 2 * i + second],
            line_recv.at[which, slot],
            device_of(z + step, x, core, y),
        )

    def arrived(buffer, sem):
        pltpu.make_async_copy(buffer, buffer, sem).wait()

    def wide(ref, index):
        return ref[index].astype(f32)

    every = [(1, 1), (1, 0), (0, 1), (0, 0)]

    def products(which, i):
        first = 0 if which == 0 else counts[0]
        height = 8 * parts[which].shape[1]
        odd = order[i] % 2
        window = pl.ds(pl.multiple_of(order[i] * height - odd * 64, 128), height + 64)
        blocks = pl.ds(order[i] * 8, 8)
        taken = {}
        for column, (lefts, right, turned) in enumerate(SELF_PRODUCTS if which == 0 else CROSS_PRODUCTS):
            if i == 0:
                for needed in (*lefts, right):
                    if needed in waiting[which]:
                        waiting[which].remove(needed)
                        loads[first + needed].wait()
            for left in lefts:
                if left not in taken:
                    rows = held[first + left][:, window].T
                    taken[left] = jnp.where(odd > 0, rows[64:], rows[:height])
            other = held[first + right][...]
            value = mm(jnp.concatenate([taken[left] for left in lefts], axis=1), other, NT if turned else NN)
            value = value.reshape(8, height // 8, value.shape[1]).astype(bf16)
            parts[which][blocks, :, column * D : (column + 1) * D] = value
        if which == 0:
            if i == 0:
                loads[-1].wait()
            parts[0][blocks, :, 4 * D :] = small_held[blocks]

    waiting = [set(range(counts[0])), set(range(counts[1]))]

    def make(i):
        for which in (1, 0):
            products(which, i)
            for first, second in every:
                to_mate(which, i, first, second).start()

    def chip_sum(which, i, first, second):
        here = block(which, i, first, second)
        slot = slot_of(which, i, first, second)
        arrived(mate_in[which].at[slot], mate_recv.at[which, slot])
        return here, wide(parts[which], here) + wide(mate_in[which], slot)

    def send_first(i):
        for second in (1, 0):
            for which in (1, 0):
                here, total = chip_sum(which, i, 1, second)
                parts[which][here] = total.astype(bf16)
                to_first(which, i, second).start()

    middle = (z + 1) // 2 == 1

    def after_first(which, i, second):
        here, total = chip_sum(which, i, 0, second)
        arrived(first_in[which].at[2 * i + second], first_recv.at[which, 2 * i + second])
        return here, total + wide(first_in[which], 2 * i + second)

    def send_second(i):
        here, total = after_first(1, i, 1)
        parts[1][here] = total.astype(bf16)
        to_second(1, i).start()

    def send_line(which, i, second, here, total):
        parts[which][here] = total.astype(bf16)
        slot, copy = along_line(which, i, second)

        @pl.when(middle)
        def _():
            arrived(line_in[which].at[slot], line_recv.at[which, slot])
            total = wide(parts[which], here) + wide(line_in[which], slot)
            parts[which][here] = total.astype(bf16)

        copy.start()

    def line_self(i):
        for second in (1, 0):
            send_line(0, i, second, *after_first(0, i, second))

    def line_cross(i):
        here, total = after_first(1, i, 0)
        arrived(second_in[1].at[i], second_recv.at[1, i])
        total = total + wide(second_in[1], i)
        if i < 3:
            send_line(1, i, 0, here, total)
        else:
            put(1, total, False)

    def from_line(which, second, add):
        for came, there in ((0, z > 0), (1, z < 3)):
            slot = line_slot(which, came, z, second)

            @pl.when(there)
            def _():
                arrived(line_in[which].at[slot], line_recv.at[which, slot])
                add(wide(line_in[which], slot))

    def last_self():
        here, total = after_first(0, 3, 1)
        parts[0][here] = total.astype(bf16)

        def add(value):
            parts[0][here] = (wide(parts[0], here) + value).astype(bf16)

        from_line(0, 1, add)
        to_second(0, 3).start()
        put(0, after_first(0, 3, 0)[1], False)
        from_line(0, 0, lambda value: put(0, value, True))

    def put(which, value, add):
        stacked, single = outs[2 * which : 2 * which + 2]
        targets = [(stacked.at[j], j) for j in range(3)] + [(single, 3)]
        for target, j in targets:
            piece = value[:, j * D : (j + 1) * D]
            target[...] = target[...] + piece if add else piece
        if which == 0:
            piece = value[:, 4 * D :]
            outs[4][...] = outs[4][...] + piece if add else piece


    split = arrays[0].shape[0]
    cross = held[counts[0] :]
    own_memory = cross[2].shape[0]
    self_k, self_v = cross[2].at[:D], cross[3].at[:D]
    cross_k = cross[4].at[:, own_memory : own_memory + D]
    cross_v = cross[5].at[:, own_memory : own_memory + D]
    top = cross[6].shape[0]
    self_q = (cross[6], cross[7].at[: D - top])
    rows_held, back_out = cross[0], cross[1]
    sources = (
        weights_ref.at[:, D : 2 * D],
        weights_ref.at[:, 2 * D : 3 * D],
        weights_ref.at[:top, :D],
        weights_ref.at[top:, :D],
        tokens_ref,
        resid_ref,
        cross_ref.at[:, D : 2 * D],
        cross_ref.at[:, 2 * D : 3 * D],
    )
    targets = (self_k, self_v, *self_q, rows_held, grad_ref, cross_k, cross_v)
    late = [
        pltpu.make_async_copy(source, target, late_sems.at[i])
        for i, (source, target) in enumerate(zip(sources, targets))
    ]
    back = remote(
        back_out, back_in, back_sems.at[0], back_sems.at[1], device_of(z, x, core, 0)
    )

    def key_value_rows(columns):
        value = mm(held[3][:, columns].T, self_k[...], NT)
        return value + mm(held[4][:, columns].T, self_v[...], NT)

    def memory_copy(i):
        rows = pl.ds(256 * i, 256)
        return pltpu.make_async_copy(staged.at[i % 2], memory_ref.at[rows], staged_sems.at[i % 2])

    def memory_rows(i):
        if i == 0:
            late[6].wait()
            late[7].wait()
        if i > 1:
            memory_copy(i - 2).wait()
        columns = slice(256 * i, 256 * (i + 1))
        value = mm(cross[4][:, columns].T, cross_k[...], NT)
        staged[i % 2] = value + mm(cross[5][:, columns].T, cross_v[...], NT)
        memory_copy(i).start()

    def rows_before():
        late[0].wait()
        late[1].wait()
        back_out[...] = key_value_rows(slice(0, split)).astype(bf16)

        @pl.when(y == 1)
        def _():
            back.start()

    def rows_here():
        for copy in late[2:6]:
            copy.wait()
        query = held[2][...]
        grad = jnp.concatenate([mm(query, part[...], NT) for part in self_q], axis=1)
        add_rows(grad + key_value_rows(slice(split, 2 * split)))

    def add_rows(grad):
        value = rows_held[...].astype(f32)
        grad_ref[...] += norm_back(value, inverse_rms(value), gain_ref[...], grad)

    def rows_back():
        @pl.when(y == 0)
        def _():
            arrived(back_in, back_sems.at[1])
            add_rows(back_in[...].astype(f32))

        @pl.when(y == 1)
        def _():
            back.wait_send()

    make(0)
    make(1)
    send_first(0)
    make(2)
    send_first(1)
    send_second(0)
    line_self(0)
    make(3)
    for copy in late:
        copy.start()
    send_first(2)
    send_second(1)
    line_self(1)
    line_cross(0)
    send_first(3)
    rows_before()
    send_second(2)
    line_self(2)
    line_cross(1)
    memory_rows(0)
    memory_rows(1)
    send_second(3)
    line_cross(2)
    memory_rows(2)
    memory_rows(3)
    rows_here()
    last_self()
    line_cross(3)
    from_line(1, 0, lambda value: put(1, value, True))
    arrived(second_in[0].at[3], second_recv.at[0, 3])
    put(0, wide(second_in[0], 3), True)
    rows_back()
    memory_copy(2).wait()
    memory_copy(3).wait()

    for which in (0, 1):
        for i in range(4):
            for first, second in every:
                to_mate(which, i, first, second).wait_send()
            for second in (0, 1):
                to_first(which, i, second).wait_send()
            if which == 1 or i == 3:
                to_second(which, i).wait_send()
            if i < 3:
                for second in (0, 1)[: 2 - which]:
                    along_line(which, i, second)[1].wait_send()


def scatter_products(self_arrays, cross_arrays, small, weights, cross_weights, tokens, resid, gain):
    counts = (len(self_arrays), len(cross_arrays))
    arrays = (*self_arrays, *cross_arrays)
    shard = small.shape[1]
    shapes = [(shard, 4 * D + small.shape[2]), (shard, 4 * D)]
    dma = pltpu.SemaphoreType.DMA

    def buffers(slots):
        return [pltpu.VMEM((slots, *shape), bf16) for shape in shapes]

    return pl.pallas_call(
        functools.partial(scatter_body, counts),
        in_specs=[pl.BlockSpec(memory_space=pl.ANY)] * (len(arrays) + 5)
        + [pl.BlockSpec(memory_space=pltpu.VMEM)],
        out_specs=[pl.BlockSpec(memory_space=pltpu.VMEM)] * 6 + [pl.BlockSpec(memory_space=pl.ANY)],
        out_shape=[
            jax.ShapeDtypeStruct(shape, f32)
            for shape in (
                (3, shard, D),
                (shard, D),
                (3, shard, D),
                (shard, D),
                (shard, small.shape[2]),
                resid.shape,
                cross_arrays[2].shape,
            )
        ],
        scratch_shapes=[pltpu.VMEM(array.shape, array.dtype) for array in (*arrays, small)]
        + buffers(32)
        + buffers(16)
        + buffers(8)
        + buffers(4)
        + [pltpu.VMEM((16 - 8 * i, *shape), bf16) for i, shape in enumerate(shapes)]
        + [
            dma((len(arrays) + 1,)),
            dma((2, 16)),
            dma((2, 8)),
            dma((2, 4)),
            dma((2, 6)),
            dma((2, 16)),
            dma((2, 8)),
            dma((2, 4)),
            dma((2, 16)),
            pltpu.VMEM(tokens.shape, bf16),
            dma((2,)),
            dma((8,)),
            pltpu.VMEM((2, 256, D), f32),
            dma((2,)),
        ],
        compiler_params=pltpu.CompilerParams(
            collective_id=1, has_side_effects=True, vmem_limit_bytes=60 << 20
        ),
        name="scatter_products",
    )(*arrays, small, weights, cross_weights, tokens, resid, gain)


def gelu_and_slope(value):
    upper = 0.5 * (1.0 + lax.erf(value * math.sqrt(0.5)))
    density = jnp.exp(-0.5 * value * value) * (1.0 / math.sqrt(2.0 * math.pi))
    return value * upper, upper + value * density


def feed_forward_body(rows, *refs):
    x1_ref, mixed_ref, out_ref, gain_ref, grad_ref, in_ref, back_ref = refs[:7]
    layer_ref, dx_ref, low_ref, mixed_back_ref, weight_ref = refs[7:12]
    x2, h3, h3_t, total, back, act = refs[12:]
    step, part = pl.program_id(0), pl.program_id(1)
    first = jnp.logical_and(step == 0, part == 0)
    last = jnp.logical_and(step == pl.num_programs(0) - 1, part == 1)

    @pl.when(first)
    def _():
        value = x1_ref[...] + mm(mixed_ref[...], out_ref[...])
        x2[...] = value
        normed = (value * inverse_rms(value) * gain_ref[...]).astype(bf16)
        h3[...] = normed
        h3_t[...] = normed.T
        total[...] = value
        back[...] = jnp.zeros_like(back)

    @pl.when(part == 0)
    def _():
        hidden, slope = gelu_and_slope(mm(h3[...], in_ref[...]))
        hidden = hidden.astype(bf16)
        act[...] = hidden
        total[...] += mm(hidden, back_ref[...])
        grad_pre = (slope * mm(grad_ref[...], back_ref[...], NT)).astype(bf16)
        back[...] += mm(grad_pre, in_ref[...], NT)
        weight_ref[...] = mm(h3_t[...], grad_pre).astype(bf16)

    @pl.when(part == 1)
    def _():
        weight_ref[...] = mm(act[...].T, grad_ref[...]).astype(bf16)

    @pl.when(last)
    def _():
        layer_ref[...] = total[...].astype(bf16)
        value = x2[...]
        grad = grad_ref[...].astype(f32)
        grad = grad + norm_back(value, inverse_rms(value), gain_ref[...], back[...])
        dx_ref[...] = grad
        low = grad.astype(bf16)
        low_ref[...] = low
        mixed_back_ref[...] = mm(low, out_ref[...], NT).astype(bf16)


def feed_forward(resid, mixed, all_cross, gain, grad_out, all_ffn):
    rows = resid.shape[0]
    units = FF // D

    def whole(height):
        return pl.BlockSpec((height, D), lambda j, s: (0, 0))

    rows_f32 = jax.ShapeDtypeStruct((rows, D), f32)
    rows_bf16 = jax.ShapeDtypeStruct((rows, D), bf16)
    return pl.pallas_call(
        functools.partial(feed_forward_body, rows),
        grid=(units, 2),
        in_specs=[
            whole(rows),
            whole(rows),
            pl.BlockSpec((D, D), lambda j, s: (0, 3)),
            whole(1),
            whole(rows),
            pl.BlockSpec((D, D), lambda j, s: (0, j)),
            pl.BlockSpec((D, D), lambda j, s: (0, units + j)),
        ],
        out_specs=[
            whole(rows),
            whole(rows),
            whole(rows),
            whole(rows),
            pl.BlockSpec((D, D), lambda j, s: (0, s * units + j)),
        ],
        out_shape=[
            rows_bf16,
            rows_f32,
            rows_bf16,
            rows_bf16,
            jax.ShapeDtypeStruct((D, 2 * FF), bf16),
        ],
        scratch_shapes=[
            pltpu.VMEM((rows, D), f32),
            pltpu.VMEM((rows, D), bf16),
            pltpu.VMEM((D, rows), bf16),
            pltpu.VMEM((rows, D), f32),
            pltpu.VMEM((rows, D), f32),
            pltpu.VMEM((rows, D), bf16),
        ],
        compiler_params=pltpu.CompilerParams(vmem_limit_bytes=48 << 20),
        name="feed_forward",
    )(resid, mixed, all_cross, gain[None], grad_out, all_ffn, all_ffn)


def bias_matrices():
    place = np.arange(256)
    distance = np.where(place <= 128, 128 - place, 384 - place)
    edges = np.array(bucket_edges)
    buckets = np.where(distance < 16, distance, 16 + (distance[:, None] >= edges).sum(axis=1))
    spread = np.zeros((2, 2, BUCKETS, 2, 2, 256), np.float32)
    columns = np.zeros((2, 2, BUCKETS, 128), np.float32)
    sums = np.zeros((2, 2, 128, 2, 2, BUCKETS), np.float32)
    for which in (0, 1):
        for flag in (0, 1):
            spread[which, flag, buckets, which, flag, place] += 1.0
            spread[which, flag, BUCKETS - 1, which, flag, :] -= 1.0
            base = (HDIM if which == 0 else 0) + 3 + 2 * flag
            columns[which, flag, BUCKETS - 1, base : base + 2] = 1.0
            sums[which, flag, HDIM if which == 0 else 0, which, flag, BUCKETS - 1] = 1.0
    spread = spread.reshape(128, 1024)
    forward = np.concatenate((spread, columns.reshape(128, 128)), axis=1)
    backward = np.concatenate((spread.T, sums.reshape(512, 128)), axis=0)
    return forward, backward


def bias_parts(table_low):
    place = np.arange(2 * BUCKETS * HEADS)
    code, head = place // HEADS, place % HEADS
    chosen = (head // 2 == np.arange(PAIRS)[:, None]).astype(np.float32)
    spread = bias_matrices()[0][(head % 2) * 2 * BUCKETS + code]
    both = mm(jnp.asarray(chosen, bf16), table_low * jnp.asarray(spread, bf16)) * LOG2E
    far = both[:, 1024:]
    high = far.astype(bf16)
    rest = (far - high.astype(f32)).astype(bf16)
    odd = lax.broadcasted_iota(jnp.int32, (1, 128), 1) % 2 == 1
    return jnp.where(odd, high, rest).reshape(PAIRS, 1, 128), both[:, :1024].reshape(PAIRS, 4, 256)


def table_gradient(near_sums, row_sums):
    both = jnp.concatenate((near_sums.reshape(PAIRS, -1), row_sums.reshape(PAIRS, -1)), axis=1)
    matrix = jnp.asarray(bias_matrices()[1], f32)
    by_pair = jnp.dot(both, matrix, precision=lax.Precision.HIGHEST, preferred_element_type=f32)
    return by_pair.reshape(HEADS, 2 * BUCKETS).T.reshape(-1)


def seq_shift(array, count):
    length = array.shape[0]
    return lax.dynamic_slice_in_dim(jnp.concatenate((array, array), axis=0), count, length, axis=0)


def others_rows(rows, own_last):
    parts = lax.axis_size("seq")
    if parts == 2:
        return lax.ppermute(rows, "seq", [(0, 1)] if own_last else [(0, 1), (1, 0)])
    whole = lax.all_gather(rows, "seq", axis=0, tiled=True)
    step = rows.shape[0]
    start = lax.rem(lax.axis_index("seq") + 1, parts) * step
    return seq_shift(whole, start)[: (parts - 1) * step]


def to_owners(grads, own_last):
    parts = lax.axis_size("seq")
    if parts == 2:
        return lax.ppermute(grads, "seq", [(1, 0)] if own_last else [(0, 1), (1, 0)])
    step = grads.shape[0] // (parts - 1)
    whole = jnp.concatenate((grads, jnp.zeros((step, grads.shape[1]), grads.dtype)), axis=0)
    start = lax.rem(parts - 1 - lax.axis_index("seq"), parts) * step
    return lax.psum_scatter(seq_shift(whole, start), "seq", scatter_dimension=0, tiled=True)


def on_device(
    decoder_in,
    encoder_out,
    dec_lengths,
    pair_flags,
    enc_segments,
    self_proj,
    self_out,
    cross_proj,
    cross_out,
    ffn_in,
    ffn_out,
    norm_gains,
    rel_table,
    out_grad,
):
    shard = self_out.shape[0]
    units = FF // D
    own_kernels = (lax.axis_size("dp"), lax.axis_size("seq")) == (16, 2)
    if own_kernels:
        all_self, all_cross, pair_ffn = gather_blocks(
            self_proj, self_out, cross_proj, cross_out, ffn_in, ffn_out, norm_gains, rel_table
        )
        all_self = all_self.reshape(-1, all_self.shape[2])
        all_cross = all_cross.reshape(-1, all_cross.shape[2])
        pair_ffn = pair_ffn.reshape(2 * shard, 2 * FF)
        all_ffn = lax.all_gather(pair_ffn, "dp", axis=0, tiled=True)
    else:
        small = jnp.concatenate((norm_gains, rel_table[None]), axis=0).T
        small = jnp.pad(small, ((0, 0), (0, 124)))
        block_self = jnp.concatenate((*self_proj, self_out, small), axis=1).astype(bf16)
        block_cross = jnp.concatenate((*cross_proj, cross_out), axis=1).astype(bf16)
        ffn_in_here = jnp.swapaxes(ffn_in.reshape(shard, D, units), 1, 2).reshape(shard, FF)
        block_ffn = jnp.concatenate((ffn_in_here, ffn_out.reshape(shard, FF)), axis=1).astype(bf16)
        all_self = lax.all_gather(block_self, BOTH, axis=0, tiled=True)
        all_cross = lax.all_gather(block_cross, BOTH, axis=0, tiled=True)
        all_ffn = lax.all_gather(block_ffn, BOTH, axis=0, tiled=True)
    encoder_out = lax.optimization_barrier((encoder_out, all_cross))[0]
    self_q, self_k, self_v, out_self = (all_self[:, i * D : (i + 1) * D] for i in range(4))
    cross_q, cross_k, cross_v = (all_cross[:, i * D : (i + 1) * D] for i in range(3))
    small_all = all_self[:, 4 * D :]
    gains = small_all[:, :3].T.astype(f32)
    far_lanes, near_lines = bias_parts(small_all[:, 3:4])

    tokens = decoder_in[0]
    memory = encoder_out[0]
    grad_out = out_grad[0]
    rows, enc_rows = tokens.shape[0], memory.shape[0]
    seq_count = lax.axis_size("seq")
    seq_index = lax.axis_index("seq")
    keys, enc_keys = rows * seq_count, enc_rows * seq_count

    numbers = (dec_lengths, pair_flags)
    before = others_rows(tokens, True)
    others = others_rows(memory, False)

    scale = 0.125 * LOG2E
    tokens = tokens.astype(f32)
    inverse_one = inverse_rms(tokens)
    normed_one = (tokens * inverse_one * gains[0]).astype(bf16)
    before = before.astype(f32)
    normed_before = (before * inverse_rms(before) * gains[0]).astype(bf16)
    query_one = (mm(normed_one, self_q) * scale).astype(bf16)
    kv_one = mm(normed_one, all_self[:, D : 3 * D]).astype(bf16)
    kv_before = mm(normed_before, all_self[:, D : 3 * D]).astype(bf16)
    parts_one = ((kv_before, 0, PAIRS), (kv_one, 0, PAIRS))
    mixed_one, weights_one, total_one = attend(
        numbers, rows, query_one, parts_one, far=far_lanes, near=near_lines
    )
    resid_one = tokens + mm(mixed_one, out_self)
    inverse_two = inverse_rms(resid_one)
    normed_two = (resid_one * inverse_two * gains[1]).astype(bf16)
    query_two = (mm(normed_two, cross_q) * scale).astype(bf16)
    kv_memory = mm(memory, all_cross[:, D : 3 * D]).astype(bf16)
    kv_others = mm(others, all_cross[:, D : 3 * D]).astype(bf16)
    parts_two = ((kv_memory, 0, PAIRS), (kv_others, 0, PAIRS))
    mixed_two, weights_two, total_two = attend(numbers, rows, query_two, parts_two, segments=enc_segments)
    layer_out, grad_resid, grad_low_two, grad_mixed, grad_ffn = feed_forward(
        resid_one, mixed_two, all_cross, gains[2], grad_out, all_ffn
    )

    grad_query, grad_key, grad_value = attend_back(
        numbers, query_two, parts_two, weights_two, mixed_two, total_two, grad_mixed, False
    )
    turned = (((0,), (1,)), ((), ()))
    kv_other = mm(grad_key[:, enc_rows:], cross_k, turned)
    kv_other = (kv_other + mm(grad_value[:, enc_rows:], cross_v, turned)).astype(bf16)
    grad_two = (grad_query, grad_key, grad_value)
    grad_normed = mm(grad_query, cross_q, NT)
    grad_resid = grad_resid + norm_back(resid_one, inverse_two, gains[1], grad_normed)
    grad_low = grad_resid.astype(bf16)
    grad_mixed = mm(grad_low, out_self, NT).astype(bf16)
    grad_mixed, kv_other = lax.optimization_barrier((grad_mixed, kv_other))
    grad_query, grad_key, grad_value, near_sums, row_sums = attend_back(
        numbers, query_one, parts_one, weights_one, mixed_one, total_one, grad_mixed, True
    )
    grad_others = to_owners(kv_other, False)
    table_grad = table_gradient(near_sums, row_sums)
    small = jnp.broadcast_to(table_grad[:, None], (D, 128)).astype(bf16)

    def owned(array):
        return lax.psum_scatter(array, BOTH, scatter_dimension=0, tiled=True).astype(f32)

    def projections(block):
        return jnp.stack([block[:, i * D : (i + 1) * D] for i in range(3)], axis=0)

    if own_kernels:
        own_self, own_self_out, own_cross, own_cross_out, own_small, grad_input, grad_memory = scatter_products(
            (normed_before, normed_one, grad_query, grad_key, grad_value, mixed_one, grad_low),
            (normed_two, grad_two[0], memory, others, grad_two[1], grad_two[2], mixed_two, grad_low_two),
            small.reshape(-1, shard, small.shape[1]),
            all_self,
            all_cross,
            decoder_in[0],
            grad_resid,
            gains[:1],
        )
    else:
        normed_all = jnp.concatenate((normed_before, normed_one), axis=0)
        memory_all = jnp.concatenate((memory, others), axis=0)
        self_grads = (
            mm(normed_one, grad_query, TN),
            mm(normed_all, grad_key, turned),
            mm(normed_all, grad_value, turned),
            mm(mixed_one, grad_low, TN),
        )
        cross_grads = (
            mm(normed_two, grad_two[0], TN),
            mm(memory_all, grad_two[1], turned),
            mm(memory_all, grad_two[2], turned),
            mm(mixed_two, grad_low_two, TN),
        )
        self_grads = jnp.concatenate(self_grads, axis=1).astype(bf16)
        block = owned(jnp.concatenate((self_grads, small), axis=1))
        own_self, own_self_out = projections(block), block[:, 3 * D : 4 * D]
        own_small = block[:, 4 * D :]
        block = owned(jnp.concatenate(cross_grads, axis=1).astype(bf16))
        own_cross, own_cross_out = projections(block), block[:, 3 * D :]
        split = keys - rows
        grad_before = mm(grad_key[:, :split], self_k, turned) + mm(grad_value[:, :split], self_v, turned)
        grad_before = to_owners(grad_before.astype(bf16), True)
        grad_normed = mm(grad_key[:, split:], self_k, turned) + mm(grad_value[:, split:], self_v, turned)
        grad_normed = grad_normed + mm(grad_query, self_q, NT) + grad_before.astype(f32)
        grad_input = grad_resid + norm_back(tokens, inverse_one, gains[0], grad_normed)
        grad_memory = mm(grad_two[1][:, :enc_rows], cross_k, turned)
        grad_memory = grad_memory + mm(grad_two[2][:, :enc_rows], cross_v, turned)

    grad_others, own_small = lax.optimization_barrier((grad_others, own_small))
    grad_encoder = grad_memory + grad_others.astype(f32)
    if own_kernels:
        both_ffn = lax.psum_scatter(grad_ffn, "dp", scatter_dimension=0, tiled=True)
        both_ffn, own_small = lax.optimization_barrier((both_ffn, own_small))
        theirs = lax.dynamic_slice_in_dim(both_ffn, (1 - seq_index) * shard, shard, axis=0)
        own_ffn = lax.dynamic_slice_in_dim(both_ffn, seq_index * shard, shard, axis=0)
        came = lax.ppermute(theirs, "seq", [(0, 1), (1, 0)])
        own_ffn = own_ffn.astype(f32) + came.astype(f32)
    else:
        own_ffn = owned(grad_ffn)
    own_ffn_in = jnp.swapaxes(own_ffn[:, :FF].reshape(shard, units, D), 1, 2).reshape(shard, FF)
    own_ffn_out = own_ffn[:, FF:].reshape(ffn_out.shape)

    def products(weight, grad):
        return jnp.sum(weight.astype(bf16).astype(f32) * grad, axis=-1)

    gain_grads = jnp.stack(
        (
            jnp.sum(products(self_proj, own_self), axis=0),
            products(cross_proj[0], own_cross[0]),
            products(ffn_in, own_ffn_in),
        ),
        axis=0,
    )
    gain_grads = gain_grads / norm_gains.astype(bf16).astype(f32)

    return (
        layer_out[None],
        grad_input[None],
        grad_encoder[None],
        own_self,
        own_self_out,
        own_cross,
        own_cross_out,
        own_ffn_in,
        own_ffn_out,
        gain_grads,
        own_small[:, 0],
    )


def solution(mesh):
    hidden = P("dp", "seq", None)
    rows_split = P(BOTH, None)
    stacked = P(None, BOTH, None)
    stream = P("dp", None)
    return jax.shard_map(
        on_device,
        mesh=mesh,
        in_specs=(
            hidden,
            hidden,
            stream,
            stream,
            stream,
            stacked,
            rows_split,
            stacked,
            rows_split,
            rows_split,
            rows_split,
            P(None, BOTH),
            P(BOTH),
            hidden,
        ),
        out_specs=(
            hidden,
            hidden,
            hidden,
            stacked,
            rows_split,
            stacked,
            rows_split,
            rows_split,
            rows_split,
            P(None, BOTH),
            P(BOTH),
        ),
        check_vma=False,
    )
```

```python
import functools
import math

import jax
import jax.numpy as jnp
import numpy as np
from jax import lax
from jax.experimental import pallas as pl
from jax.experimental.pallas import tpu as pltpu
from jax.sharding import PartitionSpec as P

D = 768
HEADS = 12
HDIM = 64
FF = 3072
BUCKETS = 32
PAIRS = HEADS // 2
LOG2E = math.log2(math.e)
LN2 = math.log(2.0)
epsilon = 1e-06
neg_large = -1e30
bucket_edges = (19, 21, 24, 27, 31, 35, 40, 46, 52, 59, 67, 77, 87, 99, 113)
f32 = jnp.float32
bf16 = jnp.bfloat16
NT = (((1,), (1,)), ((), ()))
NN = (((1,), (0,)), ((), ()))
TN = (((0,), (0,)), ((), ()))
BOTH = ("dp", "seq")
MESH = pl.DeviceIdType.MESH


def mm(a, b, dims=NN):
    return lax.dot_general(a, b, dims, preferred_element_type=f32)


def inverse_rms(values):
    return lax.rsqrt(jnp.mean(values * values, axis=-1, keepdims=True) + epsilon)


def norm_back(values, inverse, gain, grad):
    unit = values * inverse
    grad = grad * gain
    return inverse * (grad - unit * jnp.mean(grad * unit, axis=-1, keepdims=True))


def head_lanes(which):
    low = lax.broadcasted_iota(jnp.int32, (1, 128), 1) < HDIM
    return low if which == 0 else jnp.logical_not(low)


def row_chunks(rows, keys, causal, step):
    return [
        (slice(i, i + step), (keys - rows + i + step) if causal else keys)
        for i in range(0, rows, step)
    ]


def near_bias(near_ref, which):
    row = lax.broadcasted_iota(jnp.int32, (128, 256), 0)
    column = lax.broadcasted_iota(jnp.int32, (128, 256), 1)
    tiles = []
    for flag in (0, 1):
        line = near_ref[0, 2 * which + flag : 2 * which + flag + 1, :]
        tile = pltpu.roll(jnp.broadcast_to(line, (128, 256)), 0, 1, stride=1, stride_axis=0)
        tiles.append(jnp.where(column - row > 128, neg_large, tile))
    return tiles


def diagonal_sums(tile):
    for step in (64, 32, 16, 8):
        tile = tile[:step] + pltpu.roll(tile[step:], 256 - step, 1)
    row = lax.broadcasted_iota(jnp.int32, (8, 256), 0)
    for step in (4, 2, 1):
        tile = jnp.where((row & step) != 0, pltpu.roll(tile, 256 - step, 1), tile)
    return jnp.sum(tile, axis=0, keepdims=True)


def pairs_between(place, end_one, end_two):
    return (place >= end_one).astype(jnp.int32) + (place >= end_two).astype(jnp.int32)


def decoder_pairs(lengths, place):
    return pairs_between(place, lengths[0, 0], lengths[0, 0] + lengths[0, 1])


def flagged(numbers, rows, first, count, width):
    lengths, flags = numbers
    place = lax.broadcasted_iota(jnp.int32, (count, width), 0)
    pair = decoder_pairs(lengths, place + (lax.axis_index("seq") * rows + first))
    return jnp.where(pair == 0, flags[0, 0], jnp.where(pair == 1, flags[0, 1], 0)) > 0


def extra_columns(numbers, rows, keys, segments, query_extra, key_extra):
    lengths = numbers[0]
    here = lax.axis_index("seq") * rows
    lane = lax.broadcasted_iota(jnp.int32, (rows, 128), 1) & (HDIM - 1)
    pair = decoder_pairs(lengths, lax.broadcasted_iota(jnp.int32, (rows, 128), 0) + here)
    flag = flagged(numbers, rows, 0, rows, 128).astype(jnp.int32)
    wanted = jnp.where(lane < 3, pair, (flag << 1) + 3)
    chosen = jnp.where(lane < 3, lane, ((lane - 3) & ~1) + 3)
    fits = jnp.logical_and(wanted == chosen, lane < 7)
    query_extra[...] = jnp.where(fits, 1.0, 0.0).astype(bf16)
    lane = lax.broadcasted_iota(jnp.int32, (keys, 128), 1) & (HDIM - 1)
    place = lax.broadcasted_iota(jnp.int32, (keys, 128), 0)
    if segments is None:
        place = place + (here + rows - keys)
        pair = jnp.where(place < 0, 3, decoder_pairs(lengths, place))
    else:
        place = place + lax.axis_index("seq") * (keys // lax.axis_size("seq"))
        place = jnp.where(place >= keys, place - keys, place)

        def below(pair):
            count = jnp.sum((segments[...] < pair).astype(f32), axis=0, keepdims=True)
            return jnp.sum(count, axis=1, keepdims=True).astype(jnp.int32)

        pair = pairs_between(place, below(1), below(2))
    wrong = jnp.logical_and(pair != lane, lane < 3)
    key_extra[...] = jnp.where(wrong, neg_large, 0.0).astype(bf16)


def attend_body(rows, keys, causal, step, parts, *refs):
    numbers, q_ref = refs[:2], refs[2]
    key_refs, value_refs = refs[3 : 3 + parts], refs[3 + parts : 3 + 2 * parts]
    o_ref, e_ref, inv_ref, query_extra, key_extra = refs[-5:]

    @pl.when(pl.program_id(0) == 0)
    def _():
        segments = None if causal else refs[3 + 2 * parts]
        extra_columns(numbers, rows, keys, segments, query_extra, key_extra)

    extra = key_extra[...]
    if causal:
        far_ref, near_ref = refs[3 + 2 * parts : 5 + 2 * parts]
        extra = extra + far_ref[0]
    key_pair = jnp.concatenate([ref[...] for ref in key_refs], axis=0)
    value_pair = jnp.concatenate([ref[...] for ref in value_refs], axis=0)
    chunks = row_chunks(rows, keys, causal, step)
    found = []
    for which in (0, 1):
        mine = head_lanes(which)
        key_head = jnp.where(mine, key_pair, extra)
        value_head = jnp.where(mine, value_pair, jnp.ones_like(value_pair))
        if causal:
            tile_zero, tile_one = near_bias(near_ref, which)
        done = []
        for here, width in chunks:
            query = jnp.where(mine, q_ref[here], query_extra[here])
            scores = mm(query, key_head[:width], NT)
            if causal:
                cut = width - 256
                flag = flagged(numbers, rows, here.start, step, 1)
                near = scores[:, cut:] + jnp.where(flag, tile_one, tile_zero)
                far = scores[:, :cut]
                peak = jnp.maximum(
                    jnp.max(far, axis=1, keepdims=True), jnp.max(near, axis=1, keepdims=True)
                )
                near = jnp.exp2(near - peak).astype(bf16)
                far = jnp.exp2(far - peak).astype(bf16)
                e_ref[which, here, :cut] = far
                e_ref[which, here, cut:width] = near
                mixed = mm(far, value_head[:cut]) + mm(near, value_head[cut:width])
            else:
                peak = jnp.max(scores, axis=1, keepdims=True)
                weights = jnp.exp2(scores - peak).astype(bf16)
                e_ref[which, here, :] = weights
                mixed = mm(weights, value_head)
            total = mixed[:, HDIM : HDIM + 1] if which == 0 else mixed[:, 0:1]
            inverse = 1.0 / total
            done.append((mixed * inverse, jnp.broadcast_to(inverse, mixed.shape)))
        found.append(done)
    low = head_lanes(0)
    for index, (here, _) in enumerate(chunks):
        o_ref[here] = jnp.where(low, found[0][index][0], found[1][index][0]).astype(bf16)
        inv_ref[here] = jnp.where(low, found[0][index][1], found[1][index][1])


def pair_columns(rows, first=0):
    return pl.BlockSpec((rows, 128), lambda p: (0, first + p))


def operands_of(numbers, query, parts):
    arrays = [*numbers, query] + [part[0] for part in parts] * 2
    specs = [pl.BlockSpec(memory_space=pltpu.SMEM)] * 2 + [pair_columns(query.shape[0])]
    for place in (1, 2):
        specs += [pair_columns(part[0].shape[0], part[place]) for part in parts]
    return arrays, specs


def per_pair(height, width):
    return pl.BlockSpec((1, height, width), lambda p: (p, 0, 0))


def attend(numbers, rows, query, parts, segments=None, far=None, near=None):
    keys = sum(part[0].shape[0] for part in parts)
    causal = far is not None
    step = 128 if causal else min(256, rows)
    operands, specs = operands_of(numbers, query, parts)
    if causal:
        operands += [far, near]
        specs += [per_pair(1, 128), per_pair(4, 256)]
    else:
        operands.append(segments)
        specs.append(pl.BlockSpec(segments.shape, lambda p: (0, 0)))
    return pl.pallas_call(
        functools.partial(attend_body, rows, keys, causal, step, len(parts)),
        grid=(PAIRS,),
        in_specs=specs,
        out_specs=(
            pair_columns(rows),
            pl.BlockSpec((2, rows, keys), lambda p: (p, 0, 0)),
            pair_columns(rows),
        ),
        out_shape=(
            jax.ShapeDtypeStruct((rows, D), bf16),
            jax.ShapeDtypeStruct((HEADS, rows, keys), bf16),
            jax.ShapeDtypeStruct((rows, D), f32),
        ),
        scratch_shapes=[pltpu.VMEM((rows, 128), bf16), pltpu.VMEM((keys, 128), bf16)],
        compiler_params=pltpu.CompilerParams(vmem_limit_bytes=56 << 20),
        name="attend_causal" if causal else "attend_cross",
    )(*operands)


def attend_back_body(rows, keys, causal, step, parts, *refs):
    numbers, q_ref = refs[:2], refs[2]
    refs = refs[3:]
    key_refs, value_refs = refs[:parts], refs[parts : 2 * parts]
    e_ref, o_ref, inv_ref, d_ref = refs[2 * parts : 4 + 2 * parts]
    if causal:
        dq_ref, dk_ref, dv_ref, near_ref, sum_ref, ds_ref = refs[4 + 2 * parts :]
    else:
        dq_ref, dk_ref, dv_ref, ds_ref = refs[4 + 2 * parts :]
    lane = lax.broadcasted_iota(jnp.int32, (1, 128), 1)
    key_pair = jnp.concatenate([ref[...] for ref in key_refs], axis=0)
    value_pair = jnp.concatenate([ref[...] for ref in value_refs], axis=0)
    scaled = (d_ref[...].astype(f32) * inv_ref[...]).astype(bf16)
    product = scaled.astype(f32) * o_ref[...].astype(f32)
    scaled_t = scaled.T
    query_t = q_ref[...].T
    chunks = row_chunks(rows, keys, causal, step)
    query_parts = []
    for which in (0, 1):
        mine = head_lanes(which)
        base = HDIM if which == 0 else 0
        value_head = jnp.where(mine, value_pair, jnp.ones_like(value_pair))
        key_head = jnp.where(mine, key_pair, jnp.ones_like(key_pair))
        delta = jnp.sum(jnp.where(mine, product, 0.0), axis=1, keepdims=True)
        high = delta.astype(bf16)
        rest = (delta - high.astype(f32)).astype(bf16)
        extra = jnp.where(
            lane == base, -high, jnp.where(lane == base + 1, -rest, jnp.zeros_like(rest))
        )
        grad_head = jnp.where(mine, scaled, extra)
        done = []
        if causal:
            near_all = jnp.zeros((128, 256), f32)
            near_one = jnp.zeros((128, 256), f32)
        for here, width in chunks:
            centred = mm(grad_head[here], value_head[:width], NT)
            grad_scores = e_ref[which, here, :width].astype(f32) * centred
            if causal:
                near = grad_scores[:, width - 256 :]
                near_all = near_all + near
                flag = flagged(numbers, rows, here.start, step, 1)
                near_one = near_one + jnp.where(flag, near, 0.0)
            grad_scores = grad_scores.astype(bf16)
            ds_ref[here, :width] = grad_scores
            done.append(mm(grad_scores, key_head[:width]))
        query_parts.append(done)
        half = slice(HDIM * which, HDIM * which + HDIM)
        if causal:
            spans = [(slice(0, keys - rows), 0)] if keys > rows else []
            spans += [
                (slice(keys - rows + i, keys - rows + i + step), i) for i in range(0, rows, step)
            ]
        else:
            spans = [(slice(0, keys), 0)]
        for span, first in spans:
            grad_key = mm(query_t[half, first:], ds_ref[first:, span])
            dk_ref[half, span] = (grad_key * LN2).astype(dk_ref.dtype)
            grad_value = mm(scaled_t[half, first:], e_ref[which, first:, span])
            dv_ref[half, span] = grad_value.astype(dv_ref.dtype)
        if causal:
            for flag, tile in ((0, near_all - near_one), (1, near_one)):
                near_ref[0, 2 * which + flag : 2 * which + flag + 1, :] = diagonal_sums(tile)
    low = head_lanes(0)
    for index, (here, _) in enumerate(chunks):
        both = jnp.where(low, query_parts[0][index], query_parts[1][index])
        dq_ref[here] = (both * 0.125).astype(dq_ref.dtype)
    if causal:
        flags = flagged(numbers, rows, 0, rows, 1)
        for which in (0, 1):
            whole = jnp.concatenate(query_parts[which], axis=0)
            one = jnp.sum(jnp.where(flags, whole, 0.0), axis=0, keepdims=True)
            every = jnp.sum(whole, axis=0, keepdims=True)
            sum_ref[0, 2 * which : 2 * which + 1, :] = every - one
            sum_ref[0, 2 * which + 1 : 2 * which + 2, :] = one


def attend_back(numbers, query, parts, weights, mixed, inverse, grad_mixed, causal):
    rows, keys = weights.shape[1:]
    step = 128 if causal else min(256, rows)
    operands, specs = operands_of(numbers, query, parts)
    operands += [weights, mixed, inverse, grad_mixed]
    specs += [pl.BlockSpec((2, rows, keys), lambda p: (p, 0, 0))] + [pair_columns(rows)] * 3
    turned = jax.ShapeDtypeStruct((D, keys), bf16)
    turned_spec = pl.BlockSpec((128, keys), lambda p: (p, 0))
    shapes = [jax.ShapeDtypeStruct((rows, D), bf16), turned, turned]
    out_specs = [pair_columns(rows), turned_spec, turned_spec]
    if causal:
        shapes += [
            jax.ShapeDtypeStruct((PAIRS, 4, 256), f32),
            jax.ShapeDtypeStruct((PAIRS, 4, 128), f32),
        ]
        out_specs += [per_pair(4, 256), per_pair(4, 128)]
    return pl.pallas_call(
        functools.partial(attend_back_body, rows, keys, causal, step, len(parts)),
        grid=(PAIRS,),
        in_specs=specs,
        out_specs=tuple(out_specs),
        out_shape=tuple(shapes),
        scratch_shapes=[pltpu.VMEM((rows, keys), bf16)],
        compiler_params=pltpu.CompilerParams(vmem_limit_bytes=56 << 20),
        name="attend_causal_back" if causal else "attend_cross_back",
    )(*operands)


def place_here():
    index = lax.axis_index("dp")
    return index // 4, (index // 2) % 2, index % 2, lax.axis_index("seq")


def block_of(z, x, core, y):
    return ((z * 2 + x) * 2 + core) * 2 + y


def device_of(z, x, core, y):
    return ((z * 2 + x) * 2 + core, y)


def greet_neighbours(z, x, core, y):
    barrier = pltpu.get_barrier_semaphore()

    def greet(device):
        pl.semaphore_signal(barrier, inc=1, device_id=device, device_id_type=MESH)

    greet(device_of(z, x, 1 - core, y))
    greet(device_of(z, 1 - x, core, y))
    greet(device_of(z, x, core, 1 - y))

    @pl.when(z > 0)
    def _():
        greet(device_of(z - 1, x, core, y))

    @pl.when(z < 3)
    def _():
        greet(device_of(z + 1, x, core, y))

    pl.semaphore_wait(barrier, 4 + ((z + 1) // 2) % 2)


def unit_order():
    place = np.arange(512)
    return (place[:, None] == (place % 128) * 4 + place // 128).astype(np.float32)


def gather_body(*refs):
    masters, refs = refs[:9], refs[9:]
    wholes, pair_whole = refs[:2], refs[2]
    sources, pair_source = refs[3:5], refs[5]
    own_sems, mate_sems, recv_sems, pair_sems = refs[6:10]
    route_sems = dict(zip(("up", "down", "x", "y"), refs[10:]))
    self_proj, self_out, cross_proj, cross_out, ffn_in, ffn_out, norm_gains, table, order = masters
    count = 2
    shard = self_out.shape[0]
    for stacked, single, source in ((self_proj, self_out, sources[0]), (cross_proj, cross_out, sources[1])):
        for j in range(3):
            source[:, j * D : (j + 1) * D] = stacked[j].astype(bf16)
        source[:, 3 * D : 4 * D] = single[...].astype(bf16)
    lane = lax.broadcasted_iota(jnp.int32, (shard, 128), 1)
    row = lax.broadcasted_iota(jnp.int32, (shard, shard), 0)
    same = row == lax.broadcasted_iota(jnp.int32, (shard, shard), 1)
    small = jnp.zeros((shard, 128), f32)
    for j in range(4):
        line = norm_gains[j : j + 1] if j < 3 else table[...]
        column = jnp.sum(jnp.where(same, jnp.broadcast_to(line, same.shape), 0.0), axis=1, keepdims=True)
        small = jnp.where(lane == j, column, small)
    sources[0][:, 4 * D :] = small.astype(bf16)
    z, x, core, y = place_here()
    mate = device_of(z, x, 1 - core, y)
    me = block_of(z, x, core, y)
    greet_neighbours(z, x, core, y)

    routes = (("y", "z", "x"), ("z", "x", "y"))
    slots = {}

    def send(which, source, block, send_sem, device):
        return pltpu.make_async_remote_copy(
            src_ref=source,
            dst_ref=wholes[which].at[block],
            send_sem=send_sem,
            recv_sem=recv_sems.at[which, block],
            device_id=device,
            device_id_type=MESH,
        )

    def copies(which, far, up, dx, dy, source=None):
        at_z = z + far if up else z - far
        block = block_of(at_z, (x + dx) % 2, core, (y + dy) % 2)
        source = wholes[which].at[block] if source is None else source
        route = routes[which]
        moved = [axis for axis, steps in (("z", far), ("x", dx), ("y", dy)) if steps]
        last = max((route.index(axis) for axis in moved), default=-1)
        targets = []
        for axis in route[max(last, 0) :]:
            fresh = route.index(axis) > last
            if axis == "z" and (fresh or not up):
                targets.append((z < 3, "up", device_of(z + 1, x, core, y)))
            if axis == "z" and (fresh or up):
                targets.append((z > 0, "down", device_of(z - 1, x, core, y)))
            if axis == "x" and fresh:
                targets.append((None, "x", device_of(z, 1 - x, core, y)))
            if axis == "y" and fresh:
                targets.append((None, "y", device_of(z, x, core, 1 - y)))
        out = []
        for condition, kind, device in targets:
            taken = slots.setdefault((which, kind), {})
            slot = taken.setdefault((far, up, dx, dy), len(taken))
            out.append((condition, send(which, source, block, route_sems[kind].at[which, slot], device)))
        taken = slots.setdefault((which, "mate"), {})
        slot = taken.setdefault((far, up, dx, dy), len(taken))
        out.append((None, send(which, source, block, mate_sems.at[which, slot], mate)))
        return block, out

    def when(condition, action):
        if condition is None:
            action()
        else:
            pl.when(condition)(action)

    def exists(far, up):
        if far == 0:
            return None
        return z + far < 4 if up else z - far >= 0

    def onwards(which, far, up, dx, dy, source=None):
        def run():
            block, out = copies(which, far, up, dx, dy, source)
            if source is None:
                pltpu.make_async_copy(wholes[which].at[block], wholes[which].at[block], recv_sems.at[which, block]).wait()
            for condition, copy in out:
                when(condition, copy.start)

        when(exists(far, up), run)

    own = [
        pltpu.make_async_copy(sources[i], wholes[i].at[me], own_sems.at[i]) for i in range(count)
    ]
    own.append(pltpu.make_async_copy(pair_source, pair_whole.at[y], pair_sems.at[0]))
    pair = pltpu.make_async_remote_copy(
        src_ref=pair_source,
        dst_ref=pair_whole.at[y],
        send_sem=pair_sems.at[1],
        recv_sem=pair_sems.at[2],
        device_id=device_of(z, x, core, 1 - y),
        device_id_type=MESH,
    )
    for which in range(count):
        onwards(which, 0, False, 0, 0, sources[which])
    for copy in own[:count]:
        copy.start()
    units = FF // D
    for m in range(FF // 512):
        piece = mm(ffn_in[:, 512 * m : 512 * (m + 1)].astype(bf16), order[...]).astype(bf16)
        for b in range(units):
            first = b * D + 128 * m
            pair_source[:, first : first + 128] = piece[:, 128 * b : 128 * (b + 1)]
    row = lax.broadcasted_iota(jnp.int32, (shard, units * shard), 0) * units
    place = lax.broadcasted_iota(jnp.int32, (shard, units * shard), 1)
    held = ffn_out[...].astype(bf16)
    for b in range(units):
        rows = mm(jnp.where(row + b == place, 1.0, 0.0).astype(bf16), held)
        pair_source[:, FF + b * D : FF + (b + 1) * D] = rows.astype(bf16)
    own[count].start()
    pair.start()
    waves = [[] for _ in range(6)]
    for dx in (0, 1):
        for dy in (0, 1):
            for far in range(4):
                for up in (False, True):
                    if far == 0 and (up or (dx == 0 and dy == 0)):
                        continue
                    waves[far + dx + dy].append((far, up, dx, dy))
    for wave in waves:
        for far, up, dx, dy in wave:
            for which in range(count):
                onwards(which, far, up, dx, dy)
    for dx in (0, 1):
        for dy in (0, 1):
            for far in range(4):
                for up in (False, True):
                    if far == 0 and up:
                        continue
                    for which in range(count):

                        def finish(which=which, far=far, up=up, dx=dx, dy=dy):
                            at_z = z + far if up else z - far
                            block = block_of(at_z, (x + dx) % 2, 1 - core, (y + dy) % 2)
                            whole = wholes[which].at[block]
                            pltpu.make_async_copy(whole, whole, recv_sems.at[which, block]).wait()
                            source = sources[which] if (far, dx, dy) == (0, 0, 0) else None
                            _, out = copies(which, far, up, dx, dy, source)
                            for condition, copy in out:
                                when(condition, copy.wait_send)

                        when(exists(far, up), finish)
    for copy in own:
        copy.wait()
    pair.wait_send()
    came = pair_whole.at[1 - y]
    pltpu.make_async_copy(came, came, pair_sems.at[2]).wait()


def gather_blocks(self_proj, self_out, cross_proj, cross_out, ffn_in, ffn_out, norm_gains, rel_table):
    shard = self_out.shape[0]
    shapes = [(shard, 4 * D + 128), (shard, 4 * D)]
    pair = (shard, 2 * FF)
    dma = pltpu.SemaphoreType.DMA
    return pl.pallas_call(
        gather_body,
        in_specs=[pl.BlockSpec(memory_space=pltpu.VMEM)] * 9,
        out_specs=[pl.BlockSpec(memory_space=pl.ANY)] * 3,
        out_shape=[jax.ShapeDtypeStruct((32, *shape), bf16) for shape in shapes]
        + [jax.ShapeDtypeStruct((2, *pair), bf16)],
        scratch_shapes=[pltpu.VMEM(shape, bf16) for shape in (*shapes, pair)]
        + [dma((3,)), dma((2, 28)), dma((2, 32)), dma((3,))]
        + [dma((2, 16))] * 4,
        compiler_params=pltpu.CompilerParams(collective_id=0, has_side_effects=True),
        name="gather_blocks",
    )(
        self_proj,
        self_out,
        cross_proj,
        cross_out,
        ffn_in,
        ffn_out,
        norm_gains,
        rel_table[None],
        jnp.asarray(unit_order(), bf16),
    )


SELF_PRODUCTS = (((1,), 2, False), ((0, 1), 3, True), ((0, 1), 4, True), ((5,), 6, False))
CROSS_PRODUCTS = (((0,), 1, False), ((2, 3), 4, True), ((2, 3), 5, True), ((6,), 7, False))


def scatter_body(counts, *refs):
    total_in = sum(counts)
    arrays, small = refs[:total_in], refs[total_in]
    weights_ref, cross_ref, tokens_ref, resid_ref, gain_ref = refs[total_in + 1 : total_in + 6]
    refs = refs[total_in + 6 :]
    outs, grad_ref, memory_ref, refs = refs[:5], refs[5], refs[6], refs[7:]
    held, small_held = refs[:total_in], refs[total_in]
    refs = refs[total_in + 1 :]
    parts, mate_in, first_in, second_in, line_in = (refs[2 * i : 2 * i + 2] for i in range(5))
    load_sems, mate_sems, first_sems, second_sems, line_sems = refs[10:15]
    mate_recv, first_recv, second_recv, line_recv = refs[15:19]
    back_in, back_sems, late_sems, staged, staged_sems = refs[19:]
    z, x, core, y = place_here()
    loads = [
        pltpu.make_async_copy(source, target, load_sems.at[i])
        for i, (source, target) in enumerate(zip((*arrays, small), (*held, small_held)))
    ]
    for load in (*loads[counts[0] :], *loads[: counts[0]]):
        load.start()
    greet_neighbours(z, x, core, y)
    half = z // 2
    order = (3 - 3 * half, 2 - half, 1 - z + 4 * half, z)

    def near(which, first, second):
        if which == 0:
            return (x + first) % 2, (y + second) % 2
        return (x + second) % 2, (y + first) % 2

    def block(which, i, first, second, other_core=0):
        bx, by = near(which, first, second)
        return block_of(order[i], bx, (core + other_core) % 2, by)

    def slot_of(which, i, first, second):
        bx, by = near(which, first, second)
        return (order[i] * 2 + bx) * 2 + by

    def remote(source, target, send_sem, recv_sem, device):
        return pltpu.make_async_remote_copy(
            src_ref=source,
            dst_ref=target,
            send_sem=send_sem,
            recv_sem=recv_sem,
            device_id=device,
            device_id_type=MESH,
        )

    def to_mate(which, i, first, second):
        slot = slot_of(which, i, first, second)
        return remote(
            parts[which].at[block(which, i, first, second, 1)],
            mate_in[which].at[slot],
            mate_sems.at[which, slot],
            mate_recv.at[which, slot],
            device_of(z, x, 1 - core, y),
        )

    def to_first(which, i, second):
        bx, by = near(which, 1, 0)
        return remote(
            parts[which].at[block(which, i, 1, second)],
            first_in[which].at[2 * i + second],
            first_sems.at[which, 2 * i + second],
            first_recv.at[which, 2 * i + second],
            device_of(z, bx, core, by),
        )

    def to_second(which, i):
        bx, by = near(which, 0, 1)
        return remote(
            parts[which].at[block(which, i, 0, 1)],
            second_in[which].at[i],
            second_sems.at[which, i],
            second_recv.at[which, i],
            device_of(z, bx, core, by),
        )

    def line_slot(which, came, at_z, second):
        return (came * 4 + at_z) * 2 + second if which == 0 else came * 4 + at_z

    def along_line(which, i, second=0):
        step = 1 - 2 * half if i < 2 else 1 - 2 * (z % 2)
        came = (1 - step) // 2
        slot = line_slot(which, came, order[i], second)
        return slot, remote(
            parts[which].at[block(which, i, 0, second)],
            line_in[which].at[slot],
            line_sems.at[which, 2 * i + second],
            line_recv.at[which, slot],
            device_of(z + step, x, core, y),
        )

    def arrived(buffer, sem):
        pltpu.make_async_copy(buffer, buffer, sem).wait()

    def wide(ref, index):
        return ref[index].astype(f32)

    every = [(1, 1), (1, 0), (0, 1), (0, 0)]

    def products(which, i):
        first = 0 if which == 0 else counts[0]
        height = 8 * parts[which].shape[1]
        odd = order[i] % 2
        window = pl.ds(pl.multiple_of(order[i] * height - odd * 64, 128), height + 64)
        blocks = pl.ds(order[i] * 8, 8)
        taken = {}
        for column, (lefts, right, turned) in enumerate(SELF_PRODUCTS if which == 0 else CROSS_PRODUCTS):
            if i == 0:
                for needed in (*lefts, right):
                    if needed in waiting[which]:
                        waiting[which].remove(needed)
                        loads[first + needed].wait()
            for left in lefts:
                if left not in taken:
                    rows = held[first + left][:, window].T
                    taken[left] = jnp.where(odd > 0, rows[64:], rows[:height])
            other = held[first + right][...]
            value = mm(jnp.concatenate([taken[left] for left in lefts], axis=1), other, NT if turned else NN)
            value = value.reshape(8, height // 8, value.shape[1]).astype(bf16)
            parts[which][blocks, :, column * D : (column + 1) * D] = value
        if which == 0:
            if i == 0:
                loads[-1].wait()
            parts[0][blocks, :, 4 * D :] = small_held[blocks]

    waiting = [set(range(counts[0])), set(range(counts[1]))]

    def make(i):
        for which in (1, 0):
            products(which, i)
            for first, second in every:
                to_mate(which, i, first, second).start()

    def chip_sum(which, i, first, second):
        here = block(which, i, first, second)
        slot = slot_of(which, i, first, second)
        arrived(mate_in[which].at[slot], mate_recv.at[which, slot])
        return here, wide(parts[which], here) + wide(mate_in[which], slot)

    def send_first(i):
        for second in (1, 0):
            for which in (1, 0):
                here, total = chip_sum(which, i, 1, second)
                parts[which][here] = total.astype(bf16)
                to_first(which, i, second).start()

    middle = (z + 1) // 2 == 1

    def after_first(which, i, second):
        here, total = chip_sum(which, i, 0, second)
        arrived(first_in[which].at[2 * i + second], first_recv.at[which, 2 * i + second])
        return here, total + wide(first_in[which], 2 * i + second)

    def send_second(i):
        here, total = after_first(1, i, 1)
        parts[1][here] = total.astype(bf16)
        to_second(1, i).start()

    def send_line(which, i, second, here, total):
        parts[which][here] = total.astype(bf16)
        slot, copy = along_line(which, i, second)

        @pl.when(middle)
        def _():
            arrived(line_in[which].at[slot], line_recv.at[which, slot])
            total = wide(parts[which], here) + wide(line_in[which], slot)
            parts[which][here] = total.astype(bf16)

        copy.start()

    def line_self(i):
        for second in (1, 0):
            send_line(0, i, second, *after_first(0, i, second))

    def line_cross(i):
        here, total = after_first(1, i, 0)
        arrived(second_in[1].at[i], second_recv.at[1, i])
        total = total + wide(second_in[1], i)
        if i < 3:
            send_line(1, i, 0, here, total)
        else:
            put(1, total, False)

    def from_line(which, second, add):
        for came, there in ((0, z > 0), (1, z < 3)):
            slot = line_slot(which, came, z, second)

            @pl.when(there)
            def _():
                arrived(line_in[which].at[slot], line_recv.at[which, slot])
                add(wide(line_in[which], slot))

    def last_self():
        here, total = after_first(0, 3, 1)
        parts[0][here] = total.astype(bf16)

        def add(value):
            parts[0][here] = (wide(parts[0], here) + value).astype(bf16)

        from_line(0, 1, add)
        to_second(0, 3).start()
        put(0, after_first(0, 3, 0)[1], False)
        from_line(0, 0, lambda value: put(0, value, True))

    def put(which, value, add):
        stacked, single = outs[2 * which : 2 * which + 2]
        targets = [(stacked.at[j], j) for j in range(3)] + [(single, 3)]
        for target, j in targets:
            piece = value[:, j * D : (j + 1) * D]
            target[...] = target[...] + piece if add else piece
        if which == 0:
            piece = value[:, 4 * D :]
            outs[4][...] = outs[4][...] + piece if add else piece


    split = arrays[0].shape[0]
    cross = held[counts[0] :]
    own_memory = cross[2].shape[0]
    self_k, self_v = cross[2].at[:D], cross[3].at[:D]
    cross_k = cross[4].at[:, own_memory : own_memory + D]
    cross_v = cross[5].at[:, own_memory : own_memory + D]
    top = cross[6].shape[0]
    self_q = (cross[6], cross[7].at[: D - top])
    rows_held, back_out = cross[0], cross[1]
    sources = (
        weights_ref.at[:, D : 2 * D],
        weights_ref.at[:, 2 * D : 3 * D],
        weights_ref.at[:top, :D],
        weights_ref.at[top:, :D],
        tokens_ref,
        resid_ref,
        cross_ref.at[:, D : 2 * D],
        cross_ref.at[:, 2 * D : 3 * D],
    )
    targets = (self_k, self_v, *self_q, rows_held, grad_ref, cross_k, cross_v)
    late = [
        pltpu.make_async_copy(source, target, late_sems.at[i])
        for i, (source, target) in enumerate(zip(sources, targets))
    ]
    back = remote(
        back_out, back_in, back_sems.at[0], back_sems.at[1], device_of(z, x, core, 0)
    )

    def key_value_rows(columns):
        value = mm(held[3][:, columns].T, self_k[...], NT)
        return value + mm(held[4][:, columns].T, self_v[...], NT)

    def memory_copy(i):
        rows = pl.ds(256 * i, 256)
        return pltpu.make_async_copy(staged.at[i % 2], memory_ref.at[rows], staged_sems.at[i % 2])

    def memory_rows(i):
        if i == 0:
            late[6].wait()
            late[7].wait()
        if i > 1:
            memory_copy(i - 2).wait()
        columns = slice(256 * i, 256 * (i + 1))
        value = mm(cross[4][:, columns].T, cross_k[...], NT)
        staged[i % 2] = value + mm(cross[5][:, columns].T, cross_v[...], NT)
        memory_copy(i).start()

    def rows_before():
        late[0].wait()
        late[1].wait()
        back_out[...] = key_value_rows(slice(0, split)).astype(bf16)

        @pl.when(y == 1)
        def _():
            back.start()

    def rows_here():
        for copy in late[2:6]:
            copy.wait()
        query = held[2][...]
        grad = jnp.concatenate([mm(query, part[...], NT) for part in self_q], axis=1)
        add_rows(grad + key_value_rows(slice(split, 2 * split)))

    def add_rows(grad):
        value = rows_held[...].astype(f32)
        grad_ref[...] += norm_back(value, inverse_rms(value), gain_ref[...], grad)

    def rows_back():
        @pl.when(y == 0)
        def _():
            arrived(back_in, back_sems.at[1])
            add_rows(back_in[...].astype(f32))

        @pl.when(y == 1)
        def _():
            back.wait_send()

    make(0)
    make(1)
    send_first(0)
    make(2)
    send_first(1)
    send_second(0)
    line_self(0)
    make(3)
    for copy in late:
        copy.start()
    send_first(2)
    send_second(1)
    line_self(1)
    line_cross(0)
    send_first(3)
    rows_before()
    send_second(2)
    line_self(2)
    line_cross(1)
    memory_rows(0)
    send_second(3)
    line_cross(2)
    rows_here()
    memory_rows(1)
    last_self()
    line_cross(3)
    memory_rows(2)
    memory_rows(3)
    from_line(1, 0, lambda value: put(1, value, True))
    arrived(second_in[0].at[3], second_recv.at[0, 3])
    put(0, wide(second_in[0], 3), True)
    rows_back()
    memory_copy(2).wait()
    memory_copy(3).wait()

    for which in (0, 1):
        for i in range(4):
            for first, second in every:
                to_mate(which, i, first, second).wait_send()
            for second in (0, 1):
                to_first(which, i, second).wait_send()
            if which == 1 or i == 3:
                to_second(which, i).wait_send()
            if i < 3:
                for second in (0, 1)[: 2 - which]:
                    along_line(which, i, second)[1].wait_send()


def scatter_products(self_arrays, cross_arrays, small, weights, cross_weights, tokens, resid, gain):
    counts = (len(self_arrays), len(cross_arrays))
    arrays = (*self_arrays, *cross_arrays)
    shard = small.shape[1]
    shapes = [(shard, 4 * D + small.shape[2]), (shard, 4 * D)]
    dma = pltpu.SemaphoreType.DMA

    def buffers(slots):
        return [pltpu.VMEM((slots, *shape), bf16) for shape in shapes]

    return pl.pallas_call(
        functools.partial(scatter_body, counts),
        in_specs=[pl.BlockSpec(memory_space=pl.ANY)] * (len(arrays) + 5)
        + [pl.BlockSpec(memory_space=pltpu.VMEM)],
        out_specs=[pl.BlockSpec(memory_space=pltpu.VMEM)] * 6 + [pl.BlockSpec(memory_space=pl.ANY)],
        out_shape=[
            jax.ShapeDtypeStruct(shape, f32)
            for shape in (
                (3, shard, D),
                (shard, D),
                (3, shard, D),
                (shard, D),
                (shard, small.shape[2]),
                resid.shape,
                cross_arrays[2].shape,
            )
        ],
        scratch_shapes=[pltpu.VMEM(array.shape, array.dtype) for array in (*arrays, small)]
        + buffers(32)
        + buffers(16)
        + buffers(8)
        + buffers(4)
        + [pltpu.VMEM((16 - 8 * i, *shape), bf16) for i, shape in enumerate(shapes)]
        + [
            dma((len(arrays) + 1,)),
            dma((2, 16)),
            dma((2, 8)),
            dma((2, 4)),
            dma((2, 6)),
            dma((2, 16)),
            dma((2, 8)),
            dma((2, 4)),
            dma((2, 16)),
            pltpu.VMEM(tokens.shape, bf16),
            dma((2,)),
            dma((8,)),
            pltpu.VMEM((2, 256, D), f32),
            dma((2,)),
        ],
        compiler_params=pltpu.CompilerParams(
            collective_id=1, has_side_effects=True, vmem_limit_bytes=60 << 20
        ),
        name="scatter_products",
    )(*arrays, small, weights, cross_weights, tokens, resid, gain)


def gelu_and_slope(value):
    upper = 0.5 * (1.0 + lax.erf(value * math.sqrt(0.5)))
    density = jnp.exp(-0.5 * value * value) * (1.0 / math.sqrt(2.0 * math.pi))
    return value * upper, upper + value * density


def feed_forward_body(rows, *refs):
    x1_ref, mixed_ref, out_ref, gain_ref, grad_ref, in_ref, back_ref = refs[:7]
    layer_ref, dx_ref, low_ref, mixed_back_ref, weight_ref = refs[7:12]
    x2, h3, h3_t, total, back, act = refs[12:]
    step, part = pl.program_id(0), pl.program_id(1)
    first = jnp.logical_and(step == 0, part == 0)
    last = jnp.logical_and(step == pl.num_programs(0) - 1, part == 1)

    @pl.when(first)
    def _():
        value = x1_ref[...] + mm(mixed_ref[...], out_ref[...])
        x2[...] = value
        normed = (value * inverse_rms(value) * gain_ref[...]).astype(bf16)
        h3[...] = normed
        h3_t[...] = normed.T
        total[...] = value
        back[...] = jnp.zeros_like(back)

    @pl.when(part == 0)
    def _():
        hidden, slope = gelu_and_slope(mm(h3[...], in_ref[...]))
        hidden = hidden.astype(bf16)
        act[...] = hidden
        total[...] += mm(hidden, back_ref[...])
        grad_pre = (slope * mm(grad_ref[...], back_ref[...], NT)).astype(bf16)
        back[...] += mm(grad_pre, in_ref[...], NT)
        weight_ref[...] = mm(h3_t[...], grad_pre).astype(bf16)

    @pl.when(part == 1)
    def _():
        weight_ref[...] = mm(act[...].T, grad_ref[...]).astype(bf16)

    @pl.when(last)
    def _():
        layer_ref[...] = total[...].astype(bf16)
        value = x2[...]
        grad = grad_ref[...].astype(f32)
        grad = grad + norm_back(value, inverse_rms(value), gain_ref[...], back[...])
        dx_ref[...] = grad
        low = grad.astype(bf16)
        low_ref[...] = low
        mixed_back_ref[...] = mm(low, out_ref[...], NT).astype(bf16)


def feed_forward(resid, mixed, all_cross, gain, grad_out, all_ffn):
    rows = resid.shape[0]
    units = FF // D

    def whole(height):
        return pl.BlockSpec((height, D), lambda j, s: (0, 0))

    rows_f32 = jax.ShapeDtypeStruct((rows, D), f32)
    rows_bf16 = jax.ShapeDtypeStruct((rows, D), bf16)
    return pl.pallas_call(
        functools.partial(feed_forward_body, rows),
        grid=(units, 2),
        in_specs=[
            whole(rows),
            whole(rows),
            pl.BlockSpec((D, D), lambda j, s: (0, 3)),
            whole(1),
            whole(rows),
            pl.BlockSpec((D, D), lambda j, s: (0, j)),
            pl.BlockSpec((D, D), lambda j, s: (0, units + j)),
        ],
        out_specs=[
            whole(rows),
            whole(rows),
            whole(rows),
            whole(rows),
            pl.BlockSpec((D, D), lambda j, s: (0, s * units + j)),
        ],
        out_shape=[
            rows_bf16,
            rows_f32,
            rows_bf16,
            rows_bf16,
            jax.ShapeDtypeStruct((D, 2 * FF), bf16),
        ],
        scratch_shapes=[
            pltpu.VMEM((rows, D), f32),
            pltpu.VMEM((rows, D), bf16),
            pltpu.VMEM((D, rows), bf16),
            pltpu.VMEM((rows, D), f32),
            pltpu.VMEM((rows, D), f32),
            pltpu.VMEM((rows, D), bf16),
        ],
        compiler_params=pltpu.CompilerParams(vmem_limit_bytes=48 << 20),
        name="feed_forward",
    )(resid, mixed, all_cross, gain[None], grad_out, all_ffn, all_ffn)


def bias_matrices():
    place = np.arange(256)
    distance = np.where(place <= 128, 128 - place, 384 - place)
    edges = np.array(bucket_edges)
    buckets = np.where(distance < 16, distance, 16 + (distance[:, None] >= edges).sum(axis=1))
    spread = np.zeros((2, 2, BUCKETS, 2, 2, 256), np.float32)
    columns = np.zeros((2, 2, BUCKETS, 128), np.float32)
    sums = np.zeros((2, 2, 128, 2, 2, BUCKETS), np.float32)
    for which in (0, 1):
        for flag in (0, 1):
            spread[which, flag, buckets, which, flag, place] += 1.0
            spread[which, flag, BUCKETS - 1, which, flag, :] -= 1.0
            base = (HDIM if which == 0 else 0) + 3 + 2 * flag
            columns[which, flag, BUCKETS - 1, base : base + 2] = 1.0
            sums[which, flag, HDIM if which == 0 else 0, which, flag, BUCKETS - 1] = 1.0
    spread = spread.reshape(128, 1024)
    forward = np.concatenate((spread, columns.reshape(128, 128)), axis=1)
    backward = np.concatenate((spread.T, sums.reshape(512, 128)), axis=0)
    return forward, backward


def bias_parts(table_low):
    place = np.arange(2 * BUCKETS * HEADS)
    code, head = place // HEADS, place % HEADS
    chosen = (head // 2 == np.arange(PAIRS)[:, None]).astype(np.float32)
    spread = bias_matrices()[0][(head % 2) * 2 * BUCKETS + code]
    both = mm(jnp.asarray(chosen, bf16), table_low * jnp.asarray(spread, bf16)) * LOG2E
    far = both[:, 1024:]
    high = far.astype(bf16)
    rest = (far - high.astype(f32)).astype(bf16)
    odd = lax.broadcasted_iota(jnp.int32, (1, 128), 1) % 2 == 1
    return jnp.where(odd, high, rest).reshape(PAIRS, 1, 128), both[:, :1024].reshape(PAIRS, 4, 256)


def table_gradient(near_sums, row_sums):
    both = jnp.concatenate((near_sums.reshape(PAIRS, -1), row_sums.reshape(PAIRS, -1)), axis=1)
    matrix = jnp.asarray(bias_matrices()[1], f32)
    by_pair = jnp.dot(both, matrix, precision=lax.Precision.HIGHEST, preferred_element_type=f32)
    return by_pair.reshape(HEADS, 2 * BUCKETS).T.reshape(-1)


def seq_shift(array, count):
    length = array.shape[0]
    return lax.dynamic_slice_in_dim(jnp.concatenate((array, array), axis=0), count, length, axis=0)


def others_rows(rows, own_last):
    parts = lax.axis_size("seq")
    if parts == 2:
        return lax.ppermute(rows, "seq", [(0, 1)] if own_last else [(0, 1), (1, 0)])
    whole = lax.all_gather(rows, "seq", axis=0, tiled=True)
    step = rows.shape[0]
    start = lax.rem(lax.axis_index("seq") + 1, parts) * step
    return seq_shift(whole, start)[: (parts - 1) * step]


def to_owners(grads, own_last):
    parts = lax.axis_size("seq")
    if parts == 2:
        return lax.ppermute(grads, "seq", [(1, 0)] if own_last else [(0, 1), (1, 0)])
    step = grads.shape[0] // (parts - 1)
    whole = jnp.concatenate((grads, jnp.zeros((step, grads.shape[1]), grads.dtype)), axis=0)
    start = lax.rem(parts - 1 - lax.axis_index("seq"), parts) * step
    return lax.psum_scatter(seq_shift(whole, start), "seq", scatter_dimension=0, tiled=True)


def on_device(
    decoder_in,
    encoder_out,
    dec_lengths,
    pair_flags,
    enc_segments,
    self_proj,
    self_out,
    cross_proj,
    cross_out,
    ffn_in,
    ffn_out,
    norm_gains,
    rel_table,
    out_grad,
):
    shard = self_out.shape[0]
    units = FF // D
    own_kernels = (lax.axis_size("dp"), lax.axis_size("seq")) == (16, 2)
    if own_kernels:
        all_self, all_cross, pair_ffn = gather_blocks(
            self_proj, self_out, cross_proj, cross_out, ffn_in, ffn_out, norm_gains, rel_table
        )
        all_self = all_self.reshape(-1, all_self.shape[2])
        all_cross = all_cross.reshape(-1, all_cross.shape[2])
        pair_ffn = pair_ffn.reshape(2 * shard, 2 * FF)
        all_ffn = lax.all_gather(pair_ffn, "dp", axis=0, tiled=True)
    else:
        small = jnp.concatenate((norm_gains, rel_table[None]), axis=0).T
        small = jnp.pad(small, ((0, 0), (0, 124)))
        block_self = jnp.concatenate((*self_proj, self_out, small), axis=1).astype(bf16)
        block_cross = jnp.concatenate((*cross_proj, cross_out), axis=1).astype(bf16)
        ffn_in_here = jnp.swapaxes(ffn_in.reshape(shard, D, units), 1, 2).reshape(shard, FF)
        block_ffn = jnp.concatenate((ffn_in_here, ffn_out.reshape(shard, FF)), axis=1).astype(bf16)
        all_self = lax.all_gather(block_self, BOTH, axis=0, tiled=True)
        all_cross = lax.all_gather(block_cross, BOTH, axis=0, tiled=True)
        all_ffn = lax.all_gather(block_ffn, BOTH, axis=0, tiled=True)
    encoder_out = lax.optimization_barrier((encoder_out, all_cross))[0]
    self_q, self_k, self_v, out_self = (all_self[:, i * D : (i + 1) * D] for i in range(4))
    cross_q, cross_k, cross_v = (all_cross[:, i * D : (i + 1) * D] for i in range(3))
    small_all = all_self[:, 4 * D :]
    gains = small_all[:, :3].T.astype(f32)
    far_lanes, near_lines = bias_parts(small_all[:, 3:4])

    tokens = decoder_in[0]
    memory = encoder_out[0]
    grad_out = out_grad[0]
    rows, enc_rows = tokens.shape[0], memory.shape[0]
    seq_count = lax.axis_size("seq")
    seq_index = lax.axis_index("seq")
    keys, enc_keys = rows * seq_count, enc_rows * seq_count

    numbers = (dec_lengths, pair_flags)
    before = others_rows(tokens, True)
    others = others_rows(memory, False)

    scale = 0.125 * LOG2E
    tokens = tokens.astype(f32)
    inverse_one = inverse_rms(tokens)
    normed_one = (tokens * inverse_one * gains[0]).astype(bf16)
    before = before.astype(f32)
    normed_before = (before * inverse_rms(before) * gains[0]).astype(bf16)
    query_one = (mm(normed_one, self_q) * scale).astype(bf16)
    kv_one = mm(normed_one, all_self[:, D : 3 * D]).astype(bf16)
    kv_before = mm(normed_before, all_self[:, D : 3 * D]).astype(bf16)
    parts_one = ((kv_before, 0, PAIRS), (kv_one, 0, PAIRS))
    mixed_one, weights_one, total_one = attend(
        numbers, rows, query_one, parts_one, far=far_lanes, near=near_lines
    )
    resid_one = tokens + mm(mixed_one, out_self)
    inverse_two = inverse_rms(resid_one)
    normed_two = (resid_one * inverse_two * gains[1]).astype(bf16)
    query_two = (mm(normed_two, cross_q) * scale).astype(bf16)
    kv_memory = mm(memory, all_cross[:, D : 3 * D]).astype(bf16)
    kv_others = mm(others, all_cross[:, D : 3 * D]).astype(bf16)
    parts_two = ((kv_memory, 0, PAIRS), (kv_others, 0, PAIRS))
    mixed_two, weights_two, total_two = attend(numbers, rows, query_two, parts_two, segments=enc_segments)
    layer_out, grad_resid, grad_low_two, grad_mixed, grad_ffn = feed_forward(
        resid_one, mixed_two, all_cross, gains[2], grad_out, all_ffn
    )

    grad_query, grad_key, grad_value = attend_back(
        numbers, query_two, parts_two, weights_two, mixed_two, total_two, grad_mixed, False
    )
    turned = (((0,), (1,)), ((), ()))
    kv_other = mm(grad_key[:, enc_rows:], cross_k, turned)
    kv_other = (kv_other + mm(grad_value[:, enc_rows:], cross_v, turned)).astype(bf16)
    grad_two = (grad_query, grad_key, grad_value)
    grad_normed = mm(grad_query, cross_q, NT)
    grad_resid = grad_resid + norm_back(resid_one, inverse_two, gains[1], grad_normed)
    grad_low = grad_resid.astype(bf16)
    grad_mixed = mm(grad_low, out_self, NT).astype(bf16)
    grad_mixed, kv_other = lax.optimization_barrier((grad_mixed, kv_other))
    grad_query, grad_key, grad_value, near_sums, row_sums = attend_back(
        numbers, query_one, parts_one, weights_one, mixed_one, total_one, grad_mixed, True
    )
    grad_others = to_owners(kv_other, False)
    table_grad = table_gradient(near_sums, row_sums)
    small = jnp.broadcast_to(table_grad[:, None], (D, 128)).astype(bf16)

    def owned(array):
        return lax.psum_scatter(array, BOTH, scatter_dimension=0, tiled=True).astype(f32)

    def projections(block):
        return jnp.stack([block[:, i * D : (i + 1) * D] for i in range(3)], axis=0)

    if own_kernels:
        own_self, own_self_out, own_cross, own_cross_out, own_small, grad_input, grad_memory = scatter_products(
            (normed_before, normed_one, grad_query, grad_key, grad_value, mixed_one, grad_low),
            (normed_two, grad_two[0], memory, others, grad_two[1], grad_two[2], mixed_two, grad_low_two),
            small.reshape(-1, shard, small.shape[1]),
            all_self,
            all_cross,
            decoder_in[0],
            grad_resid,
            gains[:1],
        )
    else:
        normed_all = jnp.concatenate((normed_before, normed_one), axis=0)
        memory_all = jnp.concatenate((memory, others), axis=0)
        self_grads = (
            mm(normed_one, grad_query, TN),
            mm(normed_all, grad_key, turned),
            mm(normed_all, grad_value, turned),
            mm(mixed_one, grad_low, TN),
        )
        cross_grads = (
            mm(normed_two, grad_two[0], TN),
            mm(memory_all, grad_two[1], turned),
            mm(memory_all, grad_two[2], turned),
            mm(mixed_two, grad_low_two, TN),
        )
        self_grads = jnp.concatenate(self_grads, axis=1).astype(bf16)
        block = owned(jnp.concatenate((self_grads, small), axis=1))
        own_self, own_self_out = projections(block), block[:, 3 * D : 4 * D]
        own_small = block[:, 4 * D :]
        block = owned(jnp.concatenate(cross_grads, axis=1).astype(bf16))
        own_cross, own_cross_out = projections(block), block[:, 3 * D :]
        split = keys - rows
        grad_before = mm(grad_key[:, :split], self_k, turned) + mm(grad_value[:, :split], self_v, turned)
        grad_before = to_owners(grad_before.astype(bf16), True)
        grad_normed = mm(grad_key[:, split:], self_k, turned) + mm(grad_value[:, split:], self_v, turned)
        grad_normed = grad_normed + mm(grad_query, self_q, NT) + grad_before.astype(f32)
        grad_input = grad_resid + norm_back(tokens, inverse_one, gains[0], grad_normed)
        grad_memory = mm(grad_two[1][:, :enc_rows], cross_k, turned)
        grad_memory = grad_memory + mm(grad_two[2][:, :enc_rows], cross_v, turned)

    grad_others, own_small = lax.optimization_barrier((grad_others, own_small))
    grad_encoder = grad_memory + grad_others.astype(f32)
    if own_kernels:
        both_ffn = lax.psum_scatter(grad_ffn, "dp", scatter_dimension=0, tiled=True)
        both_ffn, own_small = lax.optimization_barrier((both_ffn, own_small))
        theirs = lax.dynamic_slice_in_dim(both_ffn, (1 - seq_index) * shard, shard, axis=0)
        own_ffn = lax.dynamic_slice_in_dim(both_ffn, seq_index * shard, shard, axis=0)
        came = lax.ppermute(theirs, "seq", [(0, 1), (1, 0)])
        own_ffn = own_ffn.astype(f32) + came.astype(f32)
    else:
        own_ffn = owned(grad_ffn)
    own_ffn_in = jnp.swapaxes(own_ffn[:, :FF].reshape(shard, units, D), 1, 2).reshape(shard, FF)
    own_ffn_out = own_ffn[:, FF:].reshape(ffn_out.shape)

    def products(weight, grad):
        return jnp.sum(weight.astype(bf16).astype(f32) * grad, axis=-1)

    gain_grads = jnp.stack(
        (
            jnp.sum(products(self_proj, own_self), axis=0),
            products(cross_proj[0], own_cross[0]),
            products(ffn_in, own_ffn_in),
        ),
        axis=0,
    )
    gain_grads = gain_grads / norm_gains.astype(bf16).astype(f32)

    return (
        layer_out[None],
        grad_input[None],
        grad_encoder[None],
        own_self,
        own_self_out,
        own_cross,
        own_cross_out,
        own_ffn_in,
        own_ffn_out,
        gain_grads,
        own_small[:, 0],
    )


def solution(mesh):
    hidden = P("dp", "seq", None)
    rows_split = P(BOTH, None)
    stacked = P(None, BOTH, None)
    stream = P("dp", None)
    return jax.shard_map(
        on_device,
        mesh=mesh,
        in_specs=(
            hidden,
            hidden,
            stream,
            stream,
            stream,
            stacked,
            rows_split,
            stacked,
            rows_split,
            rows_split,
            rows_split,
            P(None, BOTH),
            P(BOTH),
            hidden,
        ),
        out_specs=(
            hidden,
            hidden,
            hidden,
            stacked,
            rows_split,
            stacked,
            rows_split,
            rows_split,
            rows_split,
            P(None, BOTH),
            P(BOTH),
        ),
        check_vma=False,
    )
```

```python
import functools
import math

import jax
import jax.numpy as jnp
import numpy as np
from jax import lax
from jax.experimental import pallas as pl
from jax.experimental.pallas import tpu as pltpu
from jax.sharding import PartitionSpec as P

D = 768
HEADS = 12
HDIM = 64
FF = 3072
BUCKETS = 32
PAIRS = HEADS // 2
LOG2E = math.log2(math.e)
LN2 = math.log(2.0)
epsilon = 1e-06
neg_large = -1e30
bucket_edges = (19, 21, 24, 27, 31, 35, 40, 46, 52, 59, 67, 77, 87, 99, 113)
f32 = jnp.float32
bf16 = jnp.bfloat16
NT = (((1,), (1,)), ((), ()))
NN = (((1,), (0,)), ((), ()))
TN = (((0,), (0,)), ((), ()))
BOTH = ("dp", "seq")
MESH = pl.DeviceIdType.MESH


def mm(a, b, dims=NN):
    return lax.dot_general(a, b, dims, preferred_element_type=f32)


def inverse_rms(values):
    return lax.rsqrt(jnp.mean(values * values, axis=-1, keepdims=True) + epsilon)


def norm_back(values, inverse, gain, grad):
    unit = values * inverse
    grad = grad * gain
    return inverse * (grad - unit * jnp.mean(grad * unit, axis=-1, keepdims=True))


def head_lanes(which):
    low = lax.broadcasted_iota(jnp.int32, (1, 128), 1) < HDIM
    return low if which == 0 else jnp.logical_not(low)


def row_chunks(rows, keys, causal, step):
    return [
        (slice(i, i + step), (keys - rows + i + step) if causal else keys)
        for i in range(0, rows, step)
    ]


def near_bias(near_ref, which):
    row = lax.broadcasted_iota(jnp.int32, (128, 256), 0)
    column = lax.broadcasted_iota(jnp.int32, (128, 256), 1)
    tiles = []
    for flag in (0, 1):
        line = near_ref[0, 2 * which + flag : 2 * which + flag + 1, :]
        tile = pltpu.roll(jnp.broadcast_to(line, (128, 256)), 0, 1, stride=1, stride_axis=0)
        tiles.append(jnp.where(column - row > 128, neg_large, tile))
    return tiles


def diagonal_sums(tile):
    for step in (64, 32, 16, 8):
        tile = tile[:step] + pltpu.roll(tile[step:], 256 - step, 1)
    row = lax.broadcasted_iota(jnp.int32, (8, 256), 0)
    for step in (4, 2, 1):
        tile = jnp.where((row & step) != 0, pltpu.roll(tile, 256 - step, 1), tile)
    return jnp.sum(tile, axis=0, keepdims=True)


def pairs_between(place, end_one, end_two):
    return (place >= end_one).astype(jnp.int32) + (place >= end_two).astype(jnp.int32)


def decoder_pairs(lengths, place):
    return pairs_between(place, lengths[0, 0], lengths[0, 0] + lengths[0, 1])


def flagged(numbers, rows, first, count, width):
    lengths, flags = numbers
    place = lax.broadcasted_iota(jnp.int32, (count, width), 0)
    pair = decoder_pairs(lengths, place + (lax.axis_index("seq") * rows + first))
    return jnp.where(pair == 0, flags[0, 0], jnp.where(pair == 1, flags[0, 1], 0)) > 0


def extra_columns(numbers, rows, keys, segments, query_extra, key_extra):
    lengths = numbers[0]
    here = lax.axis_index("seq") * rows
    lane = lax.broadcasted_iota(jnp.int32, (rows, 128), 1) & (HDIM - 1)
    pair = decoder_pairs(lengths, lax.broadcasted_iota(jnp.int32, (rows, 128), 0) + here)
    flag = flagged(numbers, rows, 0, rows, 128).astype(jnp.int32)
    wanted = jnp.where(lane < 3, pair, (flag << 1) + 3)
    chosen = jnp.where(lane < 3, lane, ((lane - 3) & ~1) + 3)
    fits = jnp.logical_and(wanted == chosen, lane < 7)
    query_extra[...] = jnp.where(fits, 1.0, 0.0).astype(bf16)
    lane = lax.broadcasted_iota(jnp.int32, (keys, 128), 1) & (HDIM - 1)
    place = lax.broadcasted_iota(jnp.int32, (keys, 128), 0)
    if segments is None:
        place = place + (here + rows - keys)
        pair = jnp.where(place < 0, 3, decoder_pairs(lengths, place))
    else:
        place = place + lax.axis_index("seq") * (keys // lax.axis_size("seq"))
        place = jnp.where(place >= keys, place - keys, place)

        def below(pair):
            count = jnp.sum((segments[...] < pair).astype(f32), axis=0, keepdims=True)
            return jnp.sum(count, axis=1, keepdims=True).astype(jnp.int32)

        pair = pairs_between(place, below(1), below(2))
    wrong = jnp.logical_and(pair != lane, lane < 3)
    key_extra[...] = jnp.where(wrong, neg_large, 0.0).astype(bf16)


def attend_body(rows, keys, causal, step, parts, *refs):
    numbers, q_ref = refs[:2], refs[2]
    key_refs, value_refs = refs[3 : 3 + parts], refs[3 + parts : 3 + 2 * parts]
    o_ref, e_ref, inv_ref, query_extra, key_extra = refs[-5:]

    @pl.when(pl.program_id(0) == 0)
    def _():
        segments = None if causal else refs[3 + 2 * parts]
        extra_columns(numbers, rows, keys, segments, query_extra, key_extra)

    extra = key_extra[...]
    if causal:
        far_ref, near_ref = refs[3 + 2 * parts : 5 + 2 * parts]
        extra = extra + far_ref[0]
    key_pair = jnp.concatenate([ref[...] for ref in key_refs], axis=0)
    value_pair = jnp.concatenate([ref[...] for ref in value_refs], axis=0)
    chunks = row_chunks(rows, keys, causal, step)
    found = []
    for which in (0, 1):
        mine = head_lanes(which)
        key_head = jnp.where(mine, key_pair, extra)
        value_head = jnp.where(mine, value_pair, jnp.ones_like(value_pair))
        if causal:
            tile_zero, tile_one = near_bias(near_ref, which)
        done = []
        for here, width in chunks:
            query = jnp.where(mine, q_ref[here], query_extra[here])
            scores = mm(query, key_head[:width], NT)
            if causal:
                cut = width - 256
                flag = flagged(numbers, rows, here.start, step, 1)
                near = scores[:, cut:] + jnp.where(flag, tile_one, tile_zero)
                far = scores[:, :cut]
                peak = jnp.maximum(
                    jnp.max(far, axis=1, keepdims=True), jnp.max(near, axis=1, keepdims=True)
                )
                near = jnp.exp2(near - peak).astype(bf16)
                far = jnp.exp2(far - peak).astype(bf16)
                e_ref[which, here, :cut] = far
                e_ref[which, here, cut:width] = near
                mixed = mm(far, value_head[:cut]) + mm(near, value_head[cut:width])
            else:
                peak = jnp.max(scores, axis=1, keepdims=True)
                weights = jnp.exp2(scores - peak).astype(bf16)
                e_ref[which, here, :] = weights
                mixed = mm(weights, value_head)
            total = mixed[:, HDIM : HDIM + 1] if which == 0 else mixed[:, 0:1]
            inverse = 1.0 / total
            done.append((mixed * inverse, jnp.broadcast_to(inverse, mixed.shape)))
        found.append(done)
    low = head_lanes(0)
    for index, (here, _) in enumerate(chunks):
        o_ref[here] = jnp.where(low, found[0][index][0], found[1][index][0]).astype(bf16)
        inv_ref[here] = jnp.where(low, found[0][index][1], found[1][index][1])


def pair_columns(rows, first=0):
    return pl.BlockSpec((rows, 128), lambda p: (0, first + p))


def operands_of(numbers, query, parts):
    arrays = [*numbers, query] + [part[0] for part in parts] * 2
    specs = [pl.BlockSpec(memory_space=pltpu.SMEM)] * 2 + [pair_columns(query.shape[0])]
    for place in (1, 2):
        specs += [pair_columns(part[0].shape[0], part[place]) for part in parts]
    return arrays, specs


def per_pair(height, width):
    return pl.BlockSpec((1, height, width), lambda p: (p, 0, 0))


def attend(numbers, rows, query, parts, segments=None, far=None, near=None):
    keys = sum(part[0].shape[0] for part in parts)
    causal = far is not None
    step = 128 if causal else min(256, rows)
    operands, specs = operands_of(numbers, query, parts)
    if causal:
        operands += [far, near]
        specs += [per_pair(1, 128), per_pair(4, 256)]
    else:
        operands.append(segments)
        specs.append(pl.BlockSpec(segments.shape, lambda p: (0, 0)))
    return pl.pallas_call(
        functools.partial(attend_body, rows, keys, causal, step, len(parts)),
        grid=(PAIRS,),
        in_specs=specs,
        out_specs=(
            pair_columns(rows),
            pl.BlockSpec((2, rows, keys), lambda p: (p, 0, 0)),
            pair_columns(rows),
        ),
        out_shape=(
            jax.ShapeDtypeStruct((rows, D), bf16),
            jax.ShapeDtypeStruct((HEADS, rows, keys), bf16),
            jax.ShapeDtypeStruct((rows, D), f32),
        ),
        scratch_shapes=[pltpu.VMEM((rows, 128), bf16), pltpu.VMEM((keys, 128), bf16)],
        compiler_params=pltpu.CompilerParams(vmem_limit_bytes=56 << 20),
        name="attend_causal" if causal else "attend_cross",
    )(*operands)


def attend_back_body(rows, keys, causal, step, parts, *refs):
    numbers, q_ref = refs[:2], refs[2]
    refs = refs[3:]
    key_refs, value_refs = refs[:parts], refs[parts : 2 * parts]
    e_ref, o_ref, inv_ref, d_ref = refs[2 * parts : 4 + 2 * parts]
    if causal:
        dq_ref, dk_ref, dv_ref, near_ref, sum_ref, ds_ref = refs[4 + 2 * parts :]
    else:
        dq_ref, dk_ref, dv_ref, ds_ref = refs[4 + 2 * parts :]
    lane = lax.broadcasted_iota(jnp.int32, (1, 128), 1)
    key_pair = jnp.concatenate([ref[...] for ref in key_refs], axis=0)
    value_pair = jnp.concatenate([ref[...] for ref in value_refs], axis=0)
    scaled = (d_ref[...].astype(f32) * inv_ref[...]).astype(bf16)
    product = scaled.astype(f32) * o_ref[...].astype(f32)
    scaled_t = scaled.T
    query_t = q_ref[...].T
    chunks = row_chunks(rows, keys, causal, step)
    query_parts = []
    for which in (0, 1):
        mine = head_lanes(which)
        base = HDIM if which == 0 else 0
        value_head = jnp.where(mine, value_pair, jnp.ones_like(value_pair))
        key_head = jnp.where(mine, key_pair, jnp.ones_like(key_pair))
        delta = jnp.sum(jnp.where(mine, product, 0.0), axis=1, keepdims=True)
        high = delta.astype(bf16)
        rest = (delta - high.astype(f32)).astype(bf16)
        extra = jnp.where(
            lane == base, -high, jnp.where(lane == base + 1, -rest, jnp.zeros_like(rest))
        )
        grad_head = jnp.where(mine, scaled, extra)
        done = []
        if causal:
            near_all = jnp.zeros((128, 256), f32)
            near_one = jnp.zeros((128, 256), f32)
        for here, width in chunks:
            centred = mm(grad_head[here], value_head[:width], NT)
            grad_scores = e_ref[which, here, :width].astype(f32) * centred
            if causal:
                near = grad_scores[:, width - 256 :]
                near_all = near_all + near
                flag = flagged(numbers, rows, here.start, step, 1)
                near_one = near_one + jnp.where(flag, near, 0.0)
            grad_scores = grad_scores.astype(bf16)
            ds_ref[here, :width] = grad_scores
            done.append(mm(grad_scores, key_head[:width]))
        query_parts.append(done)
        half = slice(HDIM * which, HDIM * which + HDIM)
        if causal:
            spans = [(slice(0, keys - rows), 0)] if keys > rows else []
            spans += [
                (slice(keys - rows + i, keys - rows + i + step), i) for i in range(0, rows, step)
            ]
        else:
            spans = [(slice(0, keys), 0)]
        for span, first in spans:
            grad_key = mm(query_t[half, first:], ds_ref[first:, span])
            dk_ref[half, span] = (grad_key * LN2).astype(dk_ref.dtype)
            grad_value = mm(scaled_t[half, first:], e_ref[which, first:, span])
            dv_ref[half, span] = grad_value.astype(dv_ref.dtype)
        if causal:
            for flag, tile in ((0, near_all - near_one), (1, near_one)):
                near_ref[0, 2 * which + flag : 2 * which + flag + 1, :] = diagonal_sums(tile)
    low = head_lanes(0)
    for index, (here, _) in enumerate(chunks):
        both = jnp.where(low, query_parts[0][index], query_parts[1][index])
        dq_ref[here] = (both * 0.125).astype(dq_ref.dtype)
    if causal:
        flags = flagged(numbers, rows, 0, rows, 1)
        for which in (0, 1):
            whole = jnp.concatenate(query_parts[which], axis=0)
            one = jnp.sum(jnp.where(flags, whole, 0.0), axis=0, keepdims=True)
            every = jnp.sum(whole, axis=0, keepdims=True)
            sum_ref[0, 2 * which : 2 * which + 1, :] = every - one
            sum_ref[0, 2 * which + 1 : 2 * which + 2, :] = one


def attend_back(numbers, query, parts, weights, mixed, inverse, grad_mixed, causal):
    rows, keys = weights.shape[1:]
    step = 128 if causal else min(256, rows)
    operands, specs = operands_of(numbers, query, parts)
    operands += [weights, mixed, inverse, grad_mixed]
    specs += [pl.BlockSpec((2, rows, keys), lambda p: (p, 0, 0))] + [pair_columns(rows)] * 3
    turned = jax.ShapeDtypeStruct((D, keys), bf16)
    turned_spec = pl.BlockSpec((128, keys), lambda p: (p, 0))
    shapes = [jax.ShapeDtypeStruct((rows, D), bf16), turned, turned]
    out_specs = [pair_columns(rows), turned_spec, turned_spec]
    if causal:
        shapes += [
            jax.ShapeDtypeStruct((PAIRS, 4, 256), f32),
            jax.ShapeDtypeStruct((PAIRS, 4, 128), f32),
        ]
        out_specs += [per_pair(4, 256), per_pair(4, 128)]
    return pl.pallas_call(
        functools.partial(attend_back_body, rows, keys, causal, step, len(parts)),
        grid=(PAIRS,),
        in_specs=specs,
        out_specs=tuple(out_specs),
        out_shape=tuple(shapes),
        scratch_shapes=[pltpu.VMEM((rows, keys), bf16)],
        compiler_params=pltpu.CompilerParams(vmem_limit_bytes=56 << 20),
        name="attend_causal_back" if causal else "attend_cross_back",
    )(*operands)


def place_here():
    index = lax.axis_index("dp")
    return index // 4, (index // 2) % 2, index % 2, lax.axis_index("seq")


def block_of(z, x, core, y):
    return ((z * 2 + x) * 2 + core) * 2 + y


def device_of(z, x, core, y):
    return ((z * 2 + x) * 2 + core, y)


def greet_neighbours(z, x, core, y):
    barrier = pltpu.get_barrier_semaphore()

    def greet(device):
        pl.semaphore_signal(barrier, inc=1, device_id=device, device_id_type=MESH)

    greet(device_of(z, x, 1 - core, y))
    greet(device_of(z, 1 - x, core, y))
    greet(device_of(z, x, core, 1 - y))

    @pl.when(z > 0)
    def _():
        greet(device_of(z - 1, x, core, y))

    @pl.when(z < 3)
    def _():
        greet(device_of(z + 1, x, core, y))

    pl.semaphore_wait(barrier, 4 + ((z + 1) // 2) % 2)


def unit_order():
    place = np.arange(512)
    return (place[:, None] == (place % 128) * 4 + place // 128).astype(np.float32)


def gather_body(*refs):
    masters, refs = refs[:9], refs[9:]
    wholes, pair_whole = refs[:2], refs[2]
    sources, pair_source = refs[3:5], refs[5]
    own_sems, mate_sems, recv_sems, pair_sems = refs[6:10]
    route_sems = dict(zip(("up", "down", "x", "y"), refs[10:]))
    self_proj, self_out, cross_proj, cross_out, ffn_in, ffn_out, norm_gains, table, order = masters
    count = 2
    shard = self_out.shape[0]
    for stacked, single, source in ((self_proj, self_out, sources[0]), (cross_proj, cross_out, sources[1])):
        for j in range(3):
            source[:, j * D : (j + 1) * D] = stacked[j].astype(bf16)
        source[:, 3 * D : 4 * D] = single[...].astype(bf16)
    lane = lax.broadcasted_iota(jnp.int32, (shard, 128), 1)
    row = lax.broadcasted_iota(jnp.int32, (shard, shard), 0)
    same = row == lax.broadcasted_iota(jnp.int32, (shard, shard), 1)
    small = jnp.zeros((shard, 128), f32)
    for j in range(4):
        line = norm_gains[j : j + 1] if j < 3 else table[...]
        column = jnp.sum(jnp.where(same, jnp.broadcast_to(line, same.shape), 0.0), axis=1, keepdims=True)
        small = jnp.where(lane == j, column, small)
    sources[0][:, 4 * D :] = small.astype(bf16)
    z, x, core, y = place_here()
    mate = device_of(z, x, 1 - core, y)
    me = block_of(z, x, core, y)
    greet_neighbours(z, x, core, y)

    routes = (("y", "z", "x"), ("z", "x", "y"))
    slots = {}

    def send(which, source, block, send_sem, device):
        return pltpu.make_async_remote_copy(
            src_ref=source,
            dst_ref=wholes[which].at[block],
            send_sem=send_sem,
            recv_sem=recv_sems.at[which, block],
            device_id=device,
            device_id_type=MESH,
        )

    def copies(which, far, up, dx, dy, source=None):
        at_z = z + far if up else z - far
        block = block_of(at_z, (x + dx) % 2, core, (y + dy) % 2)
        source = wholes[which].at[block] if source is None else source
        route = routes[which]
        moved = [axis for axis, steps in (("z", far), ("x", dx), ("y", dy)) if steps]
        last = max((route.index(axis) for axis in moved), default=-1)
        targets = []
        for axis in route[max(last, 0) :]:
            fresh = route.index(axis) > last
            if axis == "z" and (fresh or not up):
                targets.append((z < 3, "up", device_of(z + 1, x, core, y)))
            if axis == "z" and (fresh or up):
                targets.append((z > 0, "down", device_of(z - 1, x, core, y)))
            if axis == "x" and fresh:
                targets.append((None, "x", device_of(z, 1 - x, core, y)))
            if axis == "y" and fresh:
                targets.append((None, "y", device_of(z, x, core, 1 - y)))
        out = []
        for condition, kind, device in targets:
            taken = slots.setdefault((which, kind), {})
            slot = taken.setdefault((far, up, dx, dy), len(taken))
            out.append((condition, send(which, source, block, route_sems[kind].at[which, slot], device)))
        taken = slots.setdefault((which, "mate"), {})
        slot = taken.setdefault((far, up, dx, dy), len(taken))
        out.append((None, send(which, source, block, mate_sems.at[which, slot], mate)))
        return block, out

    def when(condition, action):
        if condition is None:
            action()
        else:
            pl.when(condition)(action)

    def exists(far, up):
        if far == 0:
            return None
        return z + far < 4 if up else z - far >= 0

    def onwards(which, far, up, dx, dy, source=None):
        def run():
            block, out = copies(which, far, up, dx, dy, source)
            if source is None:
                pltpu.make_async_copy(wholes[which].at[block], wholes[which].at[block], recv_sems.at[which, block]).wait()
            for condition, copy in out:
                when(condition, copy.start)

        when(exists(far, up), run)

    own = [
        pltpu.make_async_copy(sources[i], wholes[i].at[me], own_sems.at[i]) for i in range(count)
    ]
    own.append(pltpu.make_async_copy(pair_source, pair_whole.at[y], pair_sems.at[0]))
    pair = pltpu.make_async_remote_copy(
        src_ref=pair_source,
        dst_ref=pair_whole.at[y],
        send_sem=pair_sems.at[1],
        recv_sem=pair_sems.at[2],
        device_id=device_of(z, x, core, 1 - y),
        device_id_type=MESH,
    )
    for which in range(count):
        onwards(which, 0, False, 0, 0, sources[which])
    for copy in own[:count]:
        copy.start()
    units = FF // D
    for m in range(FF // 512):
        piece = mm(ffn_in[:, 512 * m : 512 * (m + 1)].astype(bf16), order[...]).astype(bf16)
        for b in range(units):
            first = b * D + 128 * m
            pair_source[:, first : first + 128] = piece[:, 128 * b : 128 * (b + 1)]
    row = lax.broadcasted_iota(jnp.int32, (shard, units * shard), 0) * units
    place = lax.broadcasted_iota(jnp.int32, (shard, units * shard), 1)
    held = ffn_out[...].astype(bf16)
    for b in range(units):
        rows = mm(jnp.where(row + b == place, 1.0, 0.0).astype(bf16), held)
        pair_source[:, FF + b * D : FF + (b + 1) * D] = rows.astype(bf16)
    own[count].start()
    pair.start()
    waves = [[] for _ in range(6)]
    for dx in (0, 1):
        for dy in (0, 1):
            for far in range(4):
                for up in (False, True):
                    if far == 0 and (up or (dx == 0 and dy == 0)):
                        continue
                    waves[far + dx + dy].append((far, up, dx, dy))
    for wave in waves:
        for far, up, dx, dy in wave:
            for which in range(count):
                onwards(which, far, up, dx, dy)
    for dx in (0, 1):
        for dy in (0, 1):
            for far in range(4):
                for up in (False, True):
                    if far == 0 and up:
                        continue
                    for which in range(count):

                        def finish(which=which, far=far, up=up, dx=dx, dy=dy):
                            at_z = z + far if up else z - far
                            block = block_of(at_z, (x + dx) % 2, 1 - core, (y + dy) % 2)
                            whole = wholes[which].at[block]
                            pltpu.make_async_copy(whole, whole, recv_sems.at[which, block]).wait()
                            source = sources[which] if (far, dx, dy) == (0, 0, 0) else None
                            _, out = copies(which, far, up, dx, dy, source)
                            for condition, copy in out:
                                when(condition, copy.wait_send)

                        when(exists(far, up), finish)
    for copy in own:
        copy.wait()
    pair.wait_send()
    came = pair_whole.at[1 - y]
    pltpu.make_async_copy(came, came, pair_sems.at[2]).wait()


def gather_blocks(self_proj, self_out, cross_proj, cross_out, ffn_in, ffn_out, norm_gains, rel_table):
    shard = self_out.shape[0]
    shapes = [(shard, 4 * D + 128), (shard, 4 * D)]
    pair = (shard, 2 * FF)
    dma = pltpu.SemaphoreType.DMA
    return pl.pallas_call(
        gather_body,
        in_specs=[pl.BlockSpec(memory_space=pltpu.VMEM)] * 9,
        out_specs=[pl.BlockSpec(memory_space=pl.ANY)] * 3,
        out_shape=[jax.ShapeDtypeStruct((32, *shape), bf16) for shape in shapes]
        + [jax.ShapeDtypeStruct((2, *pair), bf16)],
        scratch_shapes=[pltpu.VMEM(shape, bf16) for shape in (*shapes, pair)]
        + [dma((3,)), dma((2, 28)), dma((2, 32)), dma((3,))]
        + [dma((2, 16))] * 4,
        compiler_params=pltpu.CompilerParams(collective_id=0, has_side_effects=True),
        name="gather_blocks",
    )(
        self_proj,
        self_out,
        cross_proj,
        cross_out,
        ffn_in,
        ffn_out,
        norm_gains,
        rel_table[None],
        jnp.asarray(unit_order(), bf16),
    )


SELF_PRODUCTS = (((1,), 2, False), ((0, 1), 3, True), ((0, 1), 4, True), ((5,), 6, False))
CROSS_PRODUCTS = (((0,), 1, False), ((2, 3), 4, True), ((2, 3), 5, True), ((6,), 7, False))


def scatter_body(counts, *refs):
    total_in = sum(counts)
    arrays, small = refs[:total_in], refs[total_in]
    weights_ref, cross_ref, tokens_ref, resid_ref, gain_ref = refs[total_in + 1 : total_in + 6]
    own_weights = refs[total_in + 6 : total_in + 8]
    refs = refs[total_in + 8 :]
    outs, grad_ref, memory_ref, refs = refs[:5], refs[5], refs[6], refs[7:]
    held, small_held = refs[:total_in], refs[total_in]
    refs = refs[total_in + 1 :]
    parts, mate_in, first_in, second_in, line_in = (refs[2 * i : 2 * i + 2] for i in range(5))
    load_sems, mate_sems, first_sems, second_sems, line_sems = refs[10:15]
    mate_recv, first_recv, second_recv, line_recv = refs[15:19]
    back_in, back_sems, late_sems, staged, staged_sems = refs[19:]
    z, x, core, y = place_here()
    loads = [
        pltpu.make_async_copy(source, target, load_sems.at[i])
        for i, (source, target) in enumerate(zip((*arrays, small), (*held, small_held)))
    ]
    for load in (*loads[counts[0] :], *loads[: counts[0]]):
        load.start()
    greet_neighbours(z, x, core, y)
    half = z // 2
    order = (3 - 3 * half, 2 - half, 1 - z + 4 * half, z)

    def near(which, first, second):
        if which == 0:
            return (x + first) % 2, (y + second) % 2
        return (x + second) % 2, (y + first) % 2

    def block(which, i, first, second, other_core=0):
        bx, by = near(which, first, second)
        return block_of(order[i], bx, (core + other_core) % 2, by)

    def slot_of(which, i, first, second):
        bx, by = near(which, first, second)
        return (order[i] * 2 + bx) * 2 + by

    def remote(source, target, send_sem, recv_sem, device):
        return pltpu.make_async_remote_copy(
            src_ref=source,
            dst_ref=target,
            send_sem=send_sem,
            recv_sem=recv_sem,
            device_id=device,
            device_id_type=MESH,
        )

    def to_mate(which, i, first, second):
        slot = slot_of(which, i, first, second)
        return remote(
            parts[which].at[block(which, i, first, second, 1)],
            mate_in[which].at[slot],
            mate_sems.at[which, slot],
            mate_recv.at[which, slot],
            device_of(z, x, 1 - core, y),
        )

    def to_first(which, i, second):
        bx, by = near(which, 1, 0)
        return remote(
            parts[which].at[block(which, i, 1, second)],
            first_in[which].at[2 * i + second],
            first_sems.at[which, 2 * i + second],
            first_recv.at[which, 2 * i + second],
            device_of(z, bx, core, by),
        )

    def to_second(which, i):
        bx, by = near(which, 0, 1)
        return remote(
            parts[which].at[block(which, i, 0, 1)],
            second_in[which].at[i],
            second_sems.at[which, i],
            second_recv.at[which, i],
            device_of(z, bx, core, by),
        )

    def line_slot(which, came, at_z, second):
        return (came * 4 + at_z) * 2 + second if which == 0 else came * 4 + at_z

    def along_line(which, i, second=0):
        step = 1 - 2 * half if i < 2 else 1 - 2 * (z % 2)
        came = (1 - step) // 2
        slot = line_slot(which, came, order[i], second)
        return slot, remote(
            parts[which].at[block(which, i, 0, second)],
            line_in[which].at[slot],
            line_sems.at[which, 2 * i + second],
            line_recv.at[which, slot],
            device_of(z + step, x, core, y),
        )

    def arrived(buffer, sem):
        pltpu.make_async_copy(buffer, buffer, sem).wait()

    def wide(ref, index):
        return ref[index].astype(f32)

    every = [(1, 1), (1, 0), (0, 1), (0, 0)]

    def products(which, i):
        first = 0 if which == 0 else counts[0]
        height = 8 * parts[which].shape[1]
        odd = order[i] % 2
        window = pl.ds(pl.multiple_of(order[i] * height - odd * 64, 128), height + 64)
        blocks = pl.ds(order[i] * 8, 8)
        taken = {}
        for column, (lefts, right, turned) in enumerate(SELF_PRODUCTS if which == 0 else CROSS_PRODUCTS):
            if i == 0:
                for needed in (*lefts, right):
                    if needed in waiting[which]:
                        waiting[which].remove(needed)
                        loads[first + needed].wait()
            for left in lefts:
                if left not in taken:
                    rows = held[first + left][:, window].T
                    taken[left] = jnp.where(odd > 0, rows[64:], rows[:height])
            other = held[first + right][...]
            value = mm(jnp.concatenate([taken[left] for left in lefts], axis=1), other, NT if turned else NN)
            value = value.reshape(8, height // 8, value.shape[1]).astype(bf16)
            parts[which][blocks, :, column * D : (column + 1) * D] = value
        if which == 0:
            if i == 0:
                loads[-1].wait()
            parts[0][blocks, :, 4 * D :] = small_held[blocks]

    waiting = [set(range(counts[0])), set(range(counts[1]))]

    def make(i):
        for which in (1, 0):
            products(which, i)
            for first, second in every:
                to_mate(which, i, first, second).start()

    def chip_sum(which, i, first, second):
        here = block(which, i, first, second)
        slot = slot_of(which, i, first, second)
        arrived(mate_in[which].at[slot], mate_recv.at[which, slot])
        return here, wide(parts[which], here) + wide(mate_in[which], slot)

    def send_first(i):
        for second in (1, 0):
            for which in (1, 0):
                here, total = chip_sum(which, i, 1, second)
                parts[which][here] = total.astype(bf16)
                to_first(which, i, second).start()

    middle = (z + 1) // 2 == 1

    def after_first(which, i, second):
        here, total = chip_sum(which, i, 0, second)
        arrived(first_in[which].at[2 * i + second], first_recv.at[which, 2 * i + second])
        return here, total + wide(first_in[which], 2 * i + second)

    def send_second(i):
        here, total = after_first(1, i, 1)
        parts[1][here] = total.astype(bf16)
        to_second(1, i).start()

    def send_line(which, i, second, here, total):
        parts[which][here] = total.astype(bf16)
        slot, copy = along_line(which, i, second)

        @pl.when(middle)
        def _():
            arrived(line_in[which].at[slot], line_recv.at[which, slot])
            total = wide(parts[which], here) + wide(line_in[which], slot)
            parts[which][here] = total.astype(bf16)

        copy.start()

    def line_self(i):
        for second in (1, 0):
            send_line(0, i, second, *after_first(0, i, second))

    def line_cross(i):
        here, total = after_first(1, i, 0)
        arrived(second_in[1].at[i], second_recv.at[1, i])
        total = total + wide(second_in[1], i)
        if i < 3:
            send_line(1, i, 0, here, total)
        else:
            put(1, total, False)

    def from_line(which, second, add):
        for came, there in ((0, z > 0), (1, z < 3)):
            slot = line_slot(which, came, z, second)

            @pl.when(there)
            def _():
                arrived(line_in[which].at[slot], line_recv.at[which, slot])
                add(wide(line_in[which], slot))

    def last_self():
        here, total = after_first(0, 3, 1)
        parts[0][here] = total.astype(bf16)

        def add(value):
            parts[0][here] = (wide(parts[0], here) + value).astype(bf16)

        from_line(0, 1, add)
        to_second(0, 3).start()
        put(0, after_first(0, 3, 0)[1], False)
        from_line(0, 0, lambda value: put(0, value, True))

    def put(which, value, add):
        stacked, single = outs[2 * which : 2 * which + 2]
        targets = [(stacked.at[j], j) for j in range(3)] + [(single, 3)]
        for target, j in targets:
            piece = value[:, j * D : (j + 1) * D]
            target[...] = target[...] + piece if add else piece
        if which == 0:
            piece = value[:, 4 * D :]
            outs[4][...] = outs[4][...] + piece if add else piece


    split = arrays[0].shape[0]
    cross = held[counts[0] :]
    own_memory = cross[2].shape[0]
    self_k, self_v = cross[2].at[:D], cross[3].at[:D]
    cross_k = cross[4].at[:, own_memory : own_memory + D]
    cross_v = cross[5].at[:, own_memory : own_memory + D]
    top = cross[6].shape[0]
    self_q = (cross[6], cross[7].at[: D - top])
    rows_held, back_out = cross[0], cross[1]
    sources = (
        weights_ref.at[:, D : 2 * D],
        weights_ref.at[:, 2 * D : 3 * D],
        weights_ref.at[:top, :D],
        weights_ref.at[top:, :D],
        tokens_ref,
        resid_ref,
        cross_ref.at[:, D : 2 * D],
        cross_ref.at[:, 2 * D : 3 * D],
    )
    targets = (self_k, self_v, *self_q, rows_held, grad_ref, cross_k, cross_v)
    late = [
        pltpu.make_async_copy(source, target, late_sems.at[i])
        for i, (source, target) in enumerate(zip(sources, targets))
    ]
    back = remote(
        back_out, back_in, back_sems.at[0], back_sems.at[1], device_of(z, x, core, 0)
    )

    def key_value_rows(columns):
        value = mm(held[3][:, columns].T, self_k[...], NT)
        return value + mm(held[4][:, columns].T, self_v[...], NT)

    def memory_copy(i):
        rows = pl.ds(256 * i, 256)
        return pltpu.make_async_copy(staged.at[i % 2], memory_ref.at[rows], staged_sems.at[i % 2])

    def memory_rows(i):
        if i == 0:
            late[6].wait()
            late[7].wait()
        if i > 1:
            memory_copy(i - 2).wait()
        columns = slice(256 * i, 256 * (i + 1))
        value = mm(cross[4][:, columns].T, cross_k[...], NT)
        staged[i % 2] = value + mm(cross[5][:, columns].T, cross_v[...], NT)
        memory_copy(i).start()

    def rows_before():
        late[0].wait()
        late[1].wait()
        back_out[...] = key_value_rows(slice(0, split)).astype(bf16)

        @pl.when(y == 1)
        def _():
            back.start()

    def rows_here():
        for copy in late[2:6]:
            copy.wait()
        query = held[2][...]
        grad = jnp.concatenate([mm(query, part[...], NT) for part in self_q], axis=1)
        add_rows(grad + key_value_rows(slice(split, 2 * split)))

    def add_rows(grad):
        value = rows_held[...].astype(f32)
        grad_ref[...] += norm_back(value, inverse_rms(value), gain_ref[...], grad)

    def rows_back():
        @pl.when(y == 0)
        def _():
            arrived(back_in, back_sems.at[1])
            add_rows(back_in[...].astype(f32))

        @pl.when(y == 1)
        def _():
            back.wait_send()

    make(0)
    make(1)
    send_first(0)
    make(2)
    send_first(1)
    send_second(0)
    line_self(0)
    make(3)
    for copy in late:
        copy.start()
    send_first(2)
    send_second(1)
    line_self(1)
    line_cross(0)
    send_first(3)
    rows_before()
    send_second(2)
    line_self(2)
    line_cross(1)
    memory_rows(0)
    send_second(3)
    line_cross(2)
    rows_here()
    memory_rows(1)
    last_self()
    line_cross(3)
    memory_rows(2)
    memory_rows(3)
    from_line(1, 0, lambda value: put(1, value, True))
    arrived(second_in[0].at[3], second_recv.at[0, 3])
    put(0, wide(second_in[0], 3), True)
    def by_rows(which, j):
        weight = own_weights[which][j].astype(bf16).astype(f32)
        return jnp.sum(weight * outs[2 * which][j], axis=1, keepdims=True)

    lane = lax.broadcasted_iota(jnp.int32, outs[4].shape, 1)
    first_gain = by_rows(0, 0) + by_rows(0, 1) + by_rows(0, 2)
    values = jnp.where(lane == 1, first_gain, outs[4][...])
    outs[4][...] = jnp.where(lane == 2, by_rows(1, 0), values)
    rows_back()
    memory_copy(2).wait()
    memory_copy(3).wait()

    for which in (0, 1):
        for i in range(4):
            for first, second in every:
                to_mate(which, i, first, second).wait_send()
            for second in (0, 1):
                to_first(which, i, second).wait_send()
            if which == 1 or i == 3:
                to_second(which, i).wait_send()
            if i < 3:
                for second in (0, 1)[: 2 - which]:
                    along_line(which, i, second)[1].wait_send()


def scatter_products(
    self_arrays, cross_arrays, small, weights, cross_weights, tokens, resid, gain, self_proj, cross_proj
):
    counts = (len(self_arrays), len(cross_arrays))
    arrays = (*self_arrays, *cross_arrays)
    shard = small.shape[1]
    shapes = [(shard, 4 * D + small.shape[2]), (shard, 4 * D)]
    dma = pltpu.SemaphoreType.DMA

    def buffers(slots):
        return [pltpu.VMEM((slots, *shape), bf16) for shape in shapes]

    return pl.pallas_call(
        functools.partial(scatter_body, counts),
        in_specs=[pl.BlockSpec(memory_space=pl.ANY)] * (len(arrays) + 5)
        + [pl.BlockSpec(memory_space=pltpu.VMEM)] * 3,
        out_specs=[pl.BlockSpec(memory_space=pltpu.VMEM)] * 6 + [pl.BlockSpec(memory_space=pl.ANY)],
        out_shape=[
            jax.ShapeDtypeStruct(shape, f32)
            for shape in (
                (3, shard, D),
                (shard, D),
                (3, shard, D),
                (shard, D),
                (shard, small.shape[2]),
                resid.shape,
                cross_arrays[2].shape,
            )
        ],
        scratch_shapes=[pltpu.VMEM(array.shape, array.dtype) for array in (*arrays, small)]
        + buffers(32)
        + buffers(16)
        + buffers(8)
        + buffers(4)
        + [pltpu.VMEM((16 - 8 * i, *shape), bf16) for i, shape in enumerate(shapes)]
        + [
            dma((len(arrays) + 1,)),
            dma((2, 16)),
            dma((2, 8)),
            dma((2, 4)),
            dma((2, 6)),
            dma((2, 16)),
            dma((2, 8)),
            dma((2, 4)),
            dma((2, 16)),
            pltpu.VMEM(tokens.shape, bf16),
            dma((2,)),
            dma((8,)),
            pltpu.VMEM((2, 256, D), f32),
            dma((2,)),
        ],
        compiler_params=pltpu.CompilerParams(
            collective_id=1, has_side_effects=True, vmem_limit_bytes=60 << 20
        ),
        name="scatter_products",
    )(*arrays, small, weights, cross_weights, tokens, resid, gain, self_proj, cross_proj)


def gelu_and_slope(value):
    upper = 0.5 * (1.0 + lax.erf(value * math.sqrt(0.5)))
    density = jnp.exp(-0.5 * value * value) * (1.0 / math.sqrt(2.0 * math.pi))
    return value * upper, upper + value * density


def feed_forward_body(rows, *refs):
    x1_ref, mixed_ref, out_ref, gain_ref, grad_ref, in_ref, back_ref = refs[:7]
    layer_ref, dx_ref, low_ref, mixed_back_ref, weight_ref = refs[7:12]
    x2, h3, h3_t, total, back, act = refs[12:]
    step, part = pl.program_id(0), pl.program_id(1)
    first = jnp.logical_and(step == 0, part == 0)
    last = jnp.logical_and(step == pl.num_programs(0) - 1, part == 1)

    @pl.when(first)
    def _():
        value = x1_ref[...] + mm(mixed_ref[...], out_ref[...])
        x2[...] = value
        normed = (value * inverse_rms(value) * gain_ref[...]).astype(bf16)
        h3[...] = normed
        h3_t[...] = normed.T
        total[...] = value
        back[...] = jnp.zeros_like(back)

    @pl.when(part == 0)
    def _():
        hidden, slope = gelu_and_slope(mm(h3[...], in_ref[...]))
        hidden = hidden.astype(bf16)
        act[...] = hidden
        total[...] += mm(hidden, back_ref[...])
        grad_pre = (slope * mm(grad_ref[...], back_ref[...], NT)).astype(bf16)
        back[...] += mm(grad_pre, in_ref[...], NT)
        weight_ref[...] = mm(h3_t[...], grad_pre).astype(bf16)

    @pl.when(part == 1)
    def _():
        weight_ref[...] = mm(act[...].T, grad_ref[...]).astype(bf16)

    @pl.when(last)
    def _():
        layer_ref[...] = total[...].astype(bf16)
        value = x2[...]
        grad = grad_ref[...].astype(f32)
        grad = grad + norm_back(value, inverse_rms(value), gain_ref[...], back[...])
        dx_ref[...] = grad
        low = grad.astype(bf16)
        low_ref[...] = low
        mixed_back_ref[...] = mm(low, out_ref[...], NT).astype(bf16)


def feed_forward(resid, mixed, all_cross, gain, grad_out, all_ffn):
    rows = resid.shape[0]
    units = FF // D

    def whole(height):
        return pl.BlockSpec((height, D), lambda j, s: (0, 0))

    rows_f32 = jax.ShapeDtypeStruct((rows, D), f32)
    rows_bf16 = jax.ShapeDtypeStruct((rows, D), bf16)
    return pl.pallas_call(
        functools.partial(feed_forward_body, rows),
        grid=(units, 2),
        in_specs=[
            whole(rows),
            whole(rows),
            pl.BlockSpec((D, D), lambda j, s: (0, 3)),
            whole(1),
            whole(rows),
            pl.BlockSpec((D, D), lambda j, s: (0, j)),
            pl.BlockSpec((D, D), lambda j, s: (0, units + j)),
        ],
        out_specs=[
            whole(rows),
            whole(rows),
            whole(rows),
            whole(rows),
            pl.BlockSpec((D, D), lambda j, s: (0, s * units + j)),
        ],
        out_shape=[
            rows_bf16,
            rows_f32,
            rows_bf16,
            rows_bf16,
            jax.ShapeDtypeStruct((D, 2 * FF), bf16),
        ],
        scratch_shapes=[
            pltpu.VMEM((rows, D), f32),
            pltpu.VMEM((rows, D), bf16),
            pltpu.VMEM((D, rows), bf16),
            pltpu.VMEM((rows, D), f32),
            pltpu.VMEM((rows, D), f32),
            pltpu.VMEM((rows, D), bf16),
        ],
        compiler_params=pltpu.CompilerParams(vmem_limit_bytes=48 << 20),
        name="feed_forward",
    )(resid, mixed, all_cross, gain[None], grad_out, all_ffn, all_ffn)


def bias_matrices():
    place = np.arange(256)
    distance = np.where(place <= 128, 128 - place, 384 - place)
    edges = np.array(bucket_edges)
    buckets = np.where(distance < 16, distance, 16 + (distance[:, None] >= edges).sum(axis=1))
    spread = np.zeros((2, 2, BUCKETS, 2, 2, 256), np.float32)
    columns = np.zeros((2, 2, BUCKETS, 128), np.float32)
    sums = np.zeros((2, 2, 128, 2, 2, BUCKETS), np.float32)
    for which in (0, 1):
        for flag in (0, 1):
            spread[which, flag, buckets, which, flag, place] += 1.0
            spread[which, flag, BUCKETS - 1, which, flag, :] -= 1.0
            base = (HDIM if which == 0 else 0) + 3 + 2 * flag
            columns[which, flag, BUCKETS - 1, base : base + 2] = 1.0
            sums[which, flag, HDIM if which == 0 else 0, which, flag, BUCKETS - 1] = 1.0
    spread = spread.reshape(128, 1024)
    forward = np.concatenate((spread, columns.reshape(128, 128)), axis=1)
    backward = np.concatenate((spread.T, sums.reshape(512, 128)), axis=0)
    return forward, backward


def bias_parts(table_low):
    place = np.arange(2 * BUCKETS * HEADS)
    code, head = place // HEADS, place % HEADS
    chosen = (head // 2 == np.arange(PAIRS)[:, None]).astype(np.float32)
    spread = bias_matrices()[0][(head % 2) * 2 * BUCKETS + code]
    both = mm(jnp.asarray(chosen, bf16), table_low * jnp.asarray(spread, bf16)) * LOG2E
    far = both[:, 1024:]
    high = far.astype(bf16)
    rest = (far - high.astype(f32)).astype(bf16)
    odd = lax.broadcasted_iota(jnp.int32, (1, 128), 1) % 2 == 1
    return jnp.where(odd, high, rest).reshape(PAIRS, 1, 128), both[:, :1024].reshape(PAIRS, 4, 256)


def table_gradient(near_sums, row_sums):
    both = jnp.concatenate((near_sums.reshape(PAIRS, -1), row_sums.reshape(PAIRS, -1)), axis=1)
    matrix = jnp.asarray(bias_matrices()[1], f32)
    by_pair = jnp.dot(both, matrix, precision=lax.Precision.HIGHEST, preferred_element_type=f32)
    return by_pair.reshape(HEADS, 2 * BUCKETS).T.reshape(-1)


def seq_shift(array, count):
    length = array.shape[0]
    return lax.dynamic_slice_in_dim(jnp.concatenate((array, array), axis=0), count, length, axis=0)


def others_rows(rows, own_last):
    parts = lax.axis_size("seq")
    if parts == 2:
        return lax.ppermute(rows, "seq", [(0, 1)] if own_last else [(0, 1), (1, 0)])
    whole = lax.all_gather(rows, "seq", axis=0, tiled=True)
    step = rows.shape[0]
    start = lax.rem(lax.axis_index("seq") + 1, parts) * step
    return seq_shift(whole, start)[: (parts - 1) * step]


def to_owners(grads, own_last):
    parts = lax.axis_size("seq")
    if parts == 2:
        return lax.ppermute(grads, "seq", [(1, 0)] if own_last else [(0, 1), (1, 0)])
    step = grads.shape[0] // (parts - 1)
    whole = jnp.concatenate((grads, jnp.zeros((step, grads.shape[1]), grads.dtype)), axis=0)
    start = lax.rem(parts - 1 - lax.axis_index("seq"), parts) * step
    return lax.psum_scatter(seq_shift(whole, start), "seq", scatter_dimension=0, tiled=True)


def on_device(
    decoder_in,
    encoder_out,
    dec_lengths,
    pair_flags,
    enc_segments,
    self_proj,
    self_out,
    cross_proj,
    cross_out,
    ffn_in,
    ffn_out,
    norm_gains,
    rel_table,
    out_grad,
):
    shard = self_out.shape[0]
    units = FF // D
    own_kernels = (lax.axis_size("dp"), lax.axis_size("seq")) == (16, 2)
    if own_kernels:
        all_self, all_cross, pair_ffn = gather_blocks(
            self_proj, self_out, cross_proj, cross_out, ffn_in, ffn_out, norm_gains, rel_table
        )
        all_self = all_self.reshape(-1, all_self.shape[2])
        all_cross = all_cross.reshape(-1, all_cross.shape[2])
        pair_ffn = pair_ffn.reshape(2 * shard, 2 * FF)
        all_ffn = lax.all_gather(pair_ffn, "dp", axis=0, tiled=True)
    else:
        small = jnp.concatenate((norm_gains, rel_table[None]), axis=0).T
        small = jnp.pad(small, ((0, 0), (0, 124)))
        block_self = jnp.concatenate((*self_proj, self_out, small), axis=1).astype(bf16)
        block_cross = jnp.concatenate((*cross_proj, cross_out), axis=1).astype(bf16)
        ffn_in_here = jnp.swapaxes(ffn_in.reshape(shard, D, units), 1, 2).reshape(shard, FF)
        block_ffn = jnp.concatenate((ffn_in_here, ffn_out.reshape(shard, FF)), axis=1).astype(bf16)
        all_self = lax.all_gather(block_self, BOTH, axis=0, tiled=True)
        all_cross = lax.all_gather(block_cross, BOTH, axis=0, tiled=True)
        all_ffn = lax.all_gather(block_ffn, BOTH, axis=0, tiled=True)
    encoder_out = lax.optimization_barrier((encoder_out, all_cross))[0]
    self_q, self_k, self_v, out_self = (all_self[:, i * D : (i + 1) * D] for i in range(4))
    cross_q, cross_k, cross_v = (all_cross[:, i * D : (i + 1) * D] for i in range(3))
    small_all = all_self[:, 4 * D :]
    gains = small_all[:, :3].T.astype(f32)
    far_lanes, near_lines = bias_parts(small_all[:, 3:4])

    tokens = decoder_in[0]
    memory = encoder_out[0]
    grad_out = out_grad[0]
    rows, enc_rows = tokens.shape[0], memory.shape[0]
    seq_count = lax.axis_size("seq")
    seq_index = lax.axis_index("seq")
    keys, enc_keys = rows * seq_count, enc_rows * seq_count

    numbers = (dec_lengths, pair_flags)
    before = others_rows(tokens, True)
    others = others_rows(memory, False)

    scale = 0.125 * LOG2E
    tokens = tokens.astype(f32)
    inverse_one = inverse_rms(tokens)
    normed_one = (tokens * inverse_one * gains[0]).astype(bf16)
    before = before.astype(f32)
    normed_before = (before * inverse_rms(before) * gains[0]).astype(bf16)
    query_one = (mm(normed_one, self_q) * scale).astype(bf16)
    kv_one = mm(normed_one, all_self[:, D : 3 * D]).astype(bf16)
    kv_before = mm(normed_before, all_self[:, D : 3 * D]).astype(bf16)
    parts_one = ((kv_before, 0, PAIRS), (kv_one, 0, PAIRS))
    mixed_one, weights_one, total_one = attend(
        numbers, rows, query_one, parts_one, far=far_lanes, near=near_lines
    )
    resid_one = tokens + mm(mixed_one, out_self)
    inverse_two = inverse_rms(resid_one)
    normed_two = (resid_one * inverse_two * gains[1]).astype(bf16)
    query_two = (mm(normed_two, cross_q) * scale).astype(bf16)
    kv_memory = mm(memory, all_cross[:, D : 3 * D]).astype(bf16)
    kv_others = mm(others, all_cross[:, D : 3 * D]).astype(bf16)
    parts_two = ((kv_memory, 0, PAIRS), (kv_others, 0, PAIRS))
    mixed_two, weights_two, total_two = attend(numbers, rows, query_two, parts_two, segments=enc_segments)
    layer_out, grad_resid, grad_low_two, grad_mixed, grad_ffn = feed_forward(
        resid_one, mixed_two, all_cross, gains[2], grad_out, all_ffn
    )

    grad_query, grad_key, grad_value = attend_back(
        numbers, query_two, parts_two, weights_two, mixed_two, total_two, grad_mixed, False
    )
    turned = (((0,), (1,)), ((), ()))
    kv_other = mm(grad_key[:, enc_rows:], cross_k, turned)
    kv_other = (kv_other + mm(grad_value[:, enc_rows:], cross_v, turned)).astype(bf16)
    grad_two = (grad_query, grad_key, grad_value)
    grad_normed = mm(grad_query, cross_q, NT)
    grad_resid = grad_resid + norm_back(resid_one, inverse_two, gains[1], grad_normed)
    grad_low = grad_resid.astype(bf16)
    grad_mixed = mm(grad_low, out_self, NT).astype(bf16)
    grad_mixed, kv_other = lax.optimization_barrier((grad_mixed, kv_other))
    grad_query, grad_key, grad_value, near_sums, row_sums = attend_back(
        numbers, query_one, parts_one, weights_one, mixed_one, total_one, grad_mixed, True
    )
    grad_others = to_owners(kv_other, False)
    table_grad = table_gradient(near_sums, row_sums)
    small = jnp.broadcast_to(table_grad[:, None], (D, 128)).astype(bf16)

    def owned(array):
        return lax.psum_scatter(array, BOTH, scatter_dimension=0, tiled=True).astype(f32)

    def projections(block):
        return jnp.stack([block[:, i * D : (i + 1) * D] for i in range(3)], axis=0)

    if own_kernels:
        own_self, own_self_out, own_cross, own_cross_out, own_small, grad_input, grad_memory = scatter_products(
            (normed_before, normed_one, grad_query, grad_key, grad_value, mixed_one, grad_low),
            (normed_two, grad_two[0], memory, others, grad_two[1], grad_two[2], mixed_two, grad_low_two),
            small.reshape(-1, shard, small.shape[1]),
            all_self,
            all_cross,
            decoder_in[0],
            grad_resid,
            gains[:1],
            self_proj,
            cross_proj,
        )
    else:
        normed_all = jnp.concatenate((normed_before, normed_one), axis=0)
        memory_all = jnp.concatenate((memory, others), axis=0)
        self_grads = (
            mm(normed_one, grad_query, TN),
            mm(normed_all, grad_key, turned),
            mm(normed_all, grad_value, turned),
            mm(mixed_one, grad_low, TN),
        )
        cross_grads = (
            mm(normed_two, grad_two[0], TN),
            mm(memory_all, grad_two[1], turned),
            mm(memory_all, grad_two[2], turned),
            mm(mixed_two, grad_low_two, TN),
        )
        self_grads = jnp.concatenate(self_grads, axis=1).astype(bf16)
        block = owned(jnp.concatenate((self_grads, small), axis=1))
        own_self, own_self_out = projections(block), block[:, 3 * D : 4 * D]
        own_small = block[:, 4 * D :]
        block = owned(jnp.concatenate(cross_grads, axis=1).astype(bf16))
        own_cross, own_cross_out = projections(block), block[:, 3 * D :]
        split = keys - rows
        grad_before = mm(grad_key[:, :split], self_k, turned) + mm(grad_value[:, :split], self_v, turned)
        grad_before = to_owners(grad_before.astype(bf16), True)
        grad_normed = mm(grad_key[:, split:], self_k, turned) + mm(grad_value[:, split:], self_v, turned)
        grad_normed = grad_normed + mm(grad_query, self_q, NT) + grad_before.astype(f32)
        grad_input = grad_resid + norm_back(tokens, inverse_one, gains[0], grad_normed)
        grad_memory = mm(grad_two[1][:, :enc_rows], cross_k, turned)
        grad_memory = grad_memory + mm(grad_two[2][:, :enc_rows], cross_v, turned)

    grad_others, own_small = lax.optimization_barrier((grad_others, own_small))
    grad_encoder = grad_memory + grad_others.astype(f32)
    if own_kernels:
        both_ffn = lax.psum_scatter(grad_ffn, "dp", scatter_dimension=0, tiled=True)
        both_ffn, own_small = lax.optimization_barrier((both_ffn, own_small))
        theirs = lax.dynamic_slice_in_dim(both_ffn, (1 - seq_index) * shard, shard, axis=0)
        own_ffn = lax.dynamic_slice_in_dim(both_ffn, seq_index * shard, shard, axis=0)
        came = lax.ppermute(theirs, "seq", [(0, 1), (1, 0)])
        own_ffn = own_ffn.astype(f32) + came.astype(f32)
    else:
        own_ffn = owned(grad_ffn)
    own_ffn_in = jnp.swapaxes(own_ffn[:, :FF].reshape(shard, units, D), 1, 2).reshape(shard, FF)
    own_ffn_out = own_ffn[:, FF:].reshape(ffn_out.shape)

    def products(weight, grad):
        return jnp.sum(weight.astype(bf16).astype(f32) * grad, axis=-1)

    if own_kernels:
        gain_one, gain_two = own_small[:, 1], own_small[:, 2]
    else:
        gain_one = jnp.sum(products(self_proj, own_self), axis=0)
        gain_two = products(cross_proj[0], own_cross[0])
    gain_grads = jnp.stack((gain_one, gain_two, products(ffn_in, own_ffn_in)), axis=0)
    gain_grads = gain_grads / norm_gains.astype(bf16).astype(f32)

    return (
        layer_out[None],
        grad_input[None],
        grad_encoder[None],
        own_self,
        own_self_out,
        own_cross,
        own_cross_out,
        own_ffn_in,
        own_ffn_out,
        gain_grads,
        own_small[:, 0],
    )


def solution(mesh):
    hidden = P("dp", "seq", None)
    rows_split = P(BOTH, None)
    stacked = P(None, BOTH, None)
    stream = P("dp", None)
    return jax.shard_map(
        on_device,
        mesh=mesh,
        in_specs=(
            hidden,
            hidden,
            stream,
            stream,
            stream,
            stacked,
            rows_split,
            stacked,
            rows_split,
            rows_split,
            rows_split,
            P(None, BOTH),
            P(BOTH),
            hidden,
        ),
        out_specs=(
            hidden,
            hidden,
            hidden,
            stacked,
            rows_split,
            stacked,
            rows_split,
            rows_split,
            rows_split,
            P(None, BOTH),
            P(BOTH),
        ),
        check_vma=False,
    )
```
